32 devices in a mesh: fsdp: 32 (over z, y, x, core).
Axes of the slice: x: 2, y: 2, z: 4, core: 2. Of those that a mesh axis runs over, the one named last changes fastest.
Arguments:
- patches: bfloat16 [2, 16384, 768], P(None, 'fsdp'), may hold values from -6 to 6
- tile_kind: int32 [64], P('fsdp'), may hold values from 0 to 2
- out_grad: bfloat16 [2, 16384, 768], P(None, 'fsdp'), may hold values from -6 to 6
- norm1_gain: bfloat16 [2, 768], P(None, 'fsdp'), may hold values from 0.25 to 1.75
- norm1_bias: bfloat16 [2, 768], P(None, 'fsdp'), may hold values from -1.75 to 1.75
- w_qkv: bfloat16 [2, 768, 2304], P(None, 'fsdp'), may hold values from -0.21875 to 0.21875
- w_proj: bfloat16 [2, 768, 768], P(None, 'fsdp'), may hold values from -1.25 to 1.25
- b_proj: bfloat16 [2, 768], P(None, 'fsdp'), may hold values from -3 to 3
- norm2_gain: bfloat16 [2, 768], P(None, 'fsdp'), may hold values from 0.25 to 1.75
- norm2_bias: bfloat16 [2, 768], P(None, 'fsdp'), may hold values from -1.75 to 1.75
- w_fc1: bfloat16 [2, 768, 3072], P(None, 'fsdp'), may hold values from -0.21875 to 0.21875
- b_fc1: bfloat16 [2, 3072], P(None, 'fsdp'), may hold values from -3 to 3
- w_fc2: bfloat16 [2, 3072, 768], P(None, 'fsdp'), may hold values from -0.109375 to 0.109375
- b_fc2: bfloat16 [2, 768], P(None, 'fsdp'), may hold values from -3 to 3
Outputs:
- encoded: bfloat16 [2, 16384, 768], P(None, 'fsdp')
- patches_grad: float32 [2, 16384, 768], P(None, 'fsdp')
- norm1_gain_grad: float32 [2, 768], P(None, 'fsdp')
- norm1_bias_grad: float32 [2, 768], P(None, 'fsdp')
- w_qkv_grad: float32 [2, 768, 2304], P(None, 'fsdp')
- w_proj_grad: float32 [2, 768, 768], P(None, 'fsdp')
- b_proj_grad: float32 [2, 768], P(None, 'fsdp')
- norm2_gain_grad: float32 [2, 768], P(None, 'fsdp')
- norm2_bias_grad: float32 [2, 768], P(None, 'fsdp')
- w_fc1_grad: float32 [2, 768, 3072], P(None, 'fsdp')
- b_fc1_grad: float32 [2, 3072], P(None, 'fsdp')
- w_fc2_grad: float32 [2, 3072, 768], P(None, 'fsdp')
- b_fc2_grad: float32 [2, 768], P(None, 'fsdp')
The draws below stay inside these ranges and needn't reach their ends.
All inputs are finite; a program needn't handle non-finite values.
Results may differ from the reference program's by a relative error of at most 0.011.
Values may be sent and summed in bfloat16 or wider, within the bound.
A program may use at most 256 MiB of HBM per device.

```python
from functools import partial
import jax
import jax.numpy as jnp
from jax import lax

D = 768
HEADS = 12
FF = 3072
SIDE_S = 12
SIDE_M = 15
SIDE_L = 20
TOK_DEV = 512
SLOTS = 2
TOKENS = 16384
SAMPLES = 64
N_FSDP = 32


def touch_ends(array, own_key, least, largest):
    place = [jax.random.randint(jax.random.fold_in(own_key, axis), (), 0, length) for axis, length in enumerate(array.shape)]
    main_axis = array.shape.index(max(array.shape))
    neighbour = place[:main_axis] + [(place[main_axis] + 1) % array.shape[main_axis]] + place[main_axis + 1:]
    return array.at[tuple(place)].set(least).at[tuple(neighbour)].set(largest)


def strengthened(values, key, source, target, shards_of, factor):
    def block_of(dim):
        return (jnp.arange(values.shape[dim]) // (values.shape[dim] // shards_of)).reshape((-1,) + (1,) * (values.ndim - 1 - dim))

    first = jax.random.permutation(key, shards_of)[block_of(target)]
    other_side = (block_of(target) + shards_of // 2) % shards_of
    return jnp.where((block_of(source) == first) | (block_of(source) == other_side), factor * values, values)


def block_scale(rng, dims, cuts, smallest, top_value):
    level, own = 1.0, jax.random.fold_in(rng, 6)
    for axis_at, parts in cuts:
        heights = jnp.exp(jax.random.uniform(jax.random.fold_in(own, axis_at), (parts,), jnp.float32, smallest / len(cuts), top_value / len(cuts)))
        level = level * jnp.repeat(heights, dims[axis_at] // parts).reshape([-1 if axis == axis_at else 1 for axis in range(len(dims))])
    return level


def bell_draw(key, extent, scale, most, cuts=(), held_as=jnp.bfloat16):
    values = jax.random.normal(key, extent, jnp.float32) * scale
    if len(cuts) > 0:
        values = block_scale(key, extent, cuts, -0.22, 0.18) * values
    return jnp.clip(values, min=-most, max=most).astype(held_as)


def gaussian_with(stream_key, dims, deviation, limit, split, heavy, kind=jnp.bfloat16):
    values = deviation * jax.random.normal(stream_key, dims, jnp.float32)
    if split:
        values = values * block_scale(stream_key, dims, split, -0.22, 0.18)
    return jnp.clip(strengthened(values, jax.random.fold_in(stream_key, 3), *heavy), -limit, limit).astype(kind)


def setup_inputs(seed: int = 0) -> dict:
    streams_of = jax.random.split(jax.random.key(seed), 15)
    patches = bell_draw(streams_of[0], (2, TOKENS, D), 1.0, 6.0, ((1, 32),))
    tile_kind = touch_ends(jax.random.randint(streams_of[1], (SAMPLES,), 0, 3), jax.random.fold_in(streams_of[1], 1), 0, 2).astype(jnp.int32)
    out_grad = gaussian_with(streams_of[2], (2, TOKENS, D), 1.0, 6.0, ((1, 32),), (1, 2, 32, 2.75))
    norm1_gain = jnp.clip(1.0 + 0.15 * jax.random.normal(streams_of[3], (2, D), jnp.float32), 0.25, 1.75).astype(jnp.bfloat16)
    norm1_bias = bell_draw(streams_of[4], (2, D), 0.3, 1.75, ((1, 32),))
    w_qkv = bell_draw(streams_of[5], (2, D, 3 * D), D ** -0.5, 0.21875, ((1, 32),))
    w_proj = bell_draw(streams_of[6], (2, D, D), (D // 32) ** -0.5, 1.25, ((1, 32),))
    b_proj = bell_draw(streams_of[7], (2, D), 0.5, 3.0, ((1, 32),))
    norm2_gain = jnp.clip(1.0 + 0.15 * jax.random.normal(streams_of[8], (2, D), jnp.float32), 0.25, 1.75).astype(jnp.bfloat16)
    norm2_bias = bell_draw(streams_of[9], (2, D), 0.3, 1.75, ((1, 32),))
    w_fc1 = bell_draw(streams_of[10], (2, D, FF), D ** -0.5, 0.21875, ((1, 32),))
    b_fc1 = bell_draw(streams_of[11], (2, FF), 0.5, 3.0, ((1, 32),))
    w_fc2 = bell_draw(streams_of[12], (2, FF, D), FF ** -0.5, 0.109375, ((1, 32),))
    b_fc2 = bell_draw(streams_of[13], (2, D), 0.5, 3.0, ((1, 32),))
    return {"patches": patches, "tile_kind": tile_kind, "out_grad": out_grad, "norm1_gain": norm1_gain, "norm1_bias": norm1_bias, "w_qkv": w_qkv, "w_proj": w_proj, "b_proj": b_proj, "norm2_gain": norm2_gain, "norm2_bias": norm2_bias, "w_fc1": w_fc1, "b_fc1": b_fc1, "w_fc2": w_fc2, "b_fc2": b_fc2}


@jax.custom_vjp
def low(v):
    return lax.optimization_barrier(v.astype(jnp.bfloat16)).astype(jnp.float32)

@jax.custom_vjp
def low_back(v):
    return v

def low_keep(v):
    return (low(v), None)

def low_pass(kept, grad):
    return (grad,)

def back_keep(v):
    return (v, None)

def back_low(kept, grad):
    return (low(grad),)
low.defvjp(low_keep, low_pass)
low_back.defvjp(back_keep, back_low)

def layer_norm(values, gain, shift):
    center = values - lax.optimization_barrier(jnp.mean(values, axis=-1, keepdims=True))
    spread = lax.optimization_barrier(jnp.mean(center * center, axis=-1, keepdims=True))
    return center * lax.rsqrt(spread + 1e-06) * gain + shift

def matmul(left, right):
    return jnp.dot(left, right, precision=lax.Precision.HIGHEST)

def packing(kind_ids):
    grid_sides = jnp.where(kind_ids == 0, SIDE_S, jnp.where(kind_ids == 1, SIDE_M, SIDE_L)).astype(jnp.int32)
    lengths = (grid_sides * grid_sides).astype(jnp.int32)
    end_rows = jnp.cumsum(lengths).astype(jnp.int32)
    starts = (end_rows - lengths).astype(jnp.int32)
    places = jnp.arange(TOK_DEV, dtype=jnp.int32)
    fitting = end_rows <= TOK_DEV
    inside = (fitting[None, :] & (places[:, None] >= starts[None, :]) & (places[:, None] < end_rows[None, :])).astype(jnp.int32)
    filled = lax.optimization_barrier(jnp.sum(inside, axis=1)).astype(jnp.int32)
    slot_ids = jnp.arange(SLOTS, dtype=jnp.int32)
    segment = (lax.optimization_barrier(jnp.sum(inside * slot_ids[None, :], axis=1)) + (1 - filled) * (SLOTS + places)).astype(jnp.int32)
    offset = (places - lax.optimization_barrier(jnp.sum(inside * starts[None, :], axis=1))).astype(jnp.int32)
    grid_side = (lax.optimization_barrier(jnp.sum(inside * grid_sides[None, :], axis=1)) + (1 - filled)).astype(jnp.int32)
    grid_rows = (offset // grid_side).astype(jnp.int32)
    grid_cols = (offset % grid_side).astype(jnp.int32)
    return (segment, grid_rows, grid_cols, filled)

def encode(weights, inputs):
    gain_a, shift_a, w_attn, w_out, bias_out, gain_b, shift_b, w_up, bias_up, w_down, bias_down = weights
    tokens_in, segment, grid_rows, grid_cols = inputs
    row_count = tokens_in.shape[0]
    head_size = D // HEADS
    normed = low(layer_norm(tokens_in, gain_a, shift_a))
    qkv_rows = low(low_back(matmul(normed, w_attn)))
    queries = qkv_rows[:, :D].reshape(row_count, HEADS, head_size)
    keys_all = qkv_rows[:, D:2 * D].reshape(row_count, HEADS, head_size)
    values_all = qkv_rows[:, 2 * D:].reshape(row_count, HEADS, head_size)
    slopes = jnp.exp2(-8.0 * (jnp.arange(HEADS, dtype=jnp.float32) + 1.0) / HEADS)
    row_gap = (grid_rows[:, None] - grid_rows[None, :]).astype(jnp.float32)
    col_gap = (grid_cols[:, None] - grid_cols[None, :]).astype(jnp.float32)
    distance = jnp.sqrt(row_gap * row_gap + col_gap * col_gap)
    same_sample = segment[:, None] == segment[None, :]
    logits = jnp.einsum('qhd,khd->hqk', queries, keys_all, precision=lax.Precision.HIGHEST) * head_size ** (-0.5) - slopes[:, None, None] * distance[None]
    masked = jnp.where(same_sample[None], low_back(logits), -1e+30)
    probability = low(jax.nn.softmax(masked, axis=-1))
    mixed = jnp.einsum('hqk,khd->qhd', probability, values_all, precision=lax.Precision.HIGHEST).reshape(row_count, D)
    mixed = low(low_back(mixed))
    first = tokens_in + low_back(matmul(mixed, w_out) + bias_out)
    normed_b = low(layer_norm(first, gain_b, shift_b))
    hidden = low_back(matmul(normed_b, w_up) + bias_up)
    active = low(jax.nn.gelu(hidden, approximate=False))
    return first + low_back(matmul(active, w_down) + bias_down)

def forward(params, patches_f, layout):
    segment, grid_rows, grid_cols = layout
    encoded = []
    for modality in range(2):
        weights = tuple((parameter[modality] for parameter in params))
        device_block = jax.checkpoint(partial(encode, weights))
        encoded.append(lax.map(device_block, (patches_f[modality], segment, grid_rows, grid_cols)))
    return jnp.stack(encoded)

def reference(patches, tile_kind, out_grad, norm1_gain, norm1_bias, w_qkv, w_proj, b_proj, norm2_gain, norm2_bias, w_fc1, b_fc1, w_fc2, b_fc2):
    kind_grid = tile_kind.reshape(N_FSDP, SLOTS)
    segment, grid_rows, grid_cols, filled = jax.vmap(packing)(kind_grid)
    params = tuple((parameter.astype(jnp.float32) for parameter in (norm1_gain, norm1_bias, w_qkv, w_proj, b_proj, norm2_gain, norm2_bias, w_fc1, b_fc1, w_fc2, b_fc2)))
    patches_f = patches.astype(jnp.float32).reshape(2, N_FSDP, TOK_DEV, D)

    def whole_net(weights, inputs_f):
        return forward(weights, inputs_f, (segment, grid_rows, grid_cols))
    encoded, pullback = jax.vjp(whole_net, params, patches_f)
    cotangent = out_grad.astype(jnp.float32).reshape(2, N_FSDP, TOK_DEV, D) * filled.astype(jnp.float32)[None, :, :, None]
    gradients, patches_grad = pullback(cotangent)
    return (encoded.reshape(2, TOKENS, D).astype(jnp.bfloat16), patches_grad.reshape(2, TOKENS, D).astype(jnp.float32), gradients[0].astype(jnp.float32), gradients[1].astype(jnp.float32), gradients[2].astype(jnp.float32), gradients[3].astype(jnp.float32), gradients[4].astype(jnp.float32), gradients[5].astype(jnp.float32), gradients[6].astype(jnp.float32), gradients[7].astype(jnp.float32), gradients[8].astype(jnp.float32), gradients[9].astype(jnp.float32), gradients[10].astype(jnp.float32))
```

```python
import functools

import jax
import jax.numpy as jnp
from jax import lax
from jax.experimental import pallas as pl
from jax.experimental.pallas import tpu as pltpu
from jax.sharding import PartitionSpec as P

HEADS = 12
SIDE_S = 12
SIDE_M = 15
SIDE_L = 20
RING = 32
MESH = pl.DeviceIdType.MESH
BF = jnp.bfloat16
F32 = jnp.float32
FAR = 1e33


def packing(kind_ids, row_count):
    slot_count = kind_ids.shape[0]
    sides = jnp.where(kind_ids == 0, SIDE_S, jnp.where(kind_ids == 1, SIDE_M, SIDE_L)).astype(
        jnp.int32
    )
    lengths = sides * sides
    slots = jnp.arange(slot_count, dtype=jnp.int32)
    ends = jnp.sum(jnp.where(slots[None, :] <= slots[:, None], lengths[None, :], 0), axis=1)
    starts = ends - lengths
    places = jnp.arange(row_count, dtype=jnp.int32)
    inside = (
        (ends <= row_count)[None, :]
        & (places[:, None] >= starts[None, :])
        & (places[:, None] < ends[None, :])
    ).astype(jnp.int32)
    filled = jnp.sum(inside, axis=1)
    segment = jnp.sum(inside * slots[None, :], axis=1) + (1 - filled) * (slot_count + places)
    offset = places - jnp.sum(inside * starts[None, :], axis=1)
    side = jnp.sum(inside * sides[None, :], axis=1) + (1 - filled)
    return segment, offset // side, offset % side, filled


class Place:
    def __init__(self, spread):
        me = lax.axis_index("fsdp")
        rest = lax.rem(me, spread)
        p = me // spread
        self.p = p
        self.c = lax.rem(p, 2)
        self.x = lax.rem(p // 2, 2)
        self.y = lax.rem(p // 4, 2)
        self.m = lax.rem(p // 8, 2)
        self.z = lax.rem(p // 16, 2)
        dev = lambda q: (q * spread + rest,)
        sib = p + 1 - 2 * self.c
        pair = p + 8 * (1 - 2 * self.m)
        self.sib = dev(sib)
        self.xn = dev(p + 2 * (1 - 2 * self.x))
        self.yn = dev(p + 4 * (1 - 2 * self.y))
        self.zn = dev(p + 16 * (1 - 2 * self.z))
        self.pair = dev(pair)
        self.cross = dev(pair + 1 - 2 * self.c)

    def chip(self, fz, fc, fy, fx):
        flip = lambda v, f: 1 - v if f else v
        return (
            (flip(self.z, fz) * 2 + flip(self.c, fc)) * 2 + flip(self.y, fy)
        ) * 2 + flip(self.x, fx)

    def greet(self):
        barrier = pltpu.get_barrier_semaphore()
        everyone = (self.sib, self.xn, self.yn, self.zn, self.pair, self.cross)
        for other in everyone:
            pl.semaphore_signal(barrier, inc=1, device_id=other, device_id_type=MESH)
        pl.semaphore_wait(barrier, len(everyone))


OWN, ZB, X0, X1, Y0, Y1, D0, D1 = range(8)
FLIPS = ((0, 0, 0), (1, 0, 0), (0, 0, 1), (1, 0, 1), (0, 1, 0), (1, 1, 0), (0, 1, 1), (1, 1, 1))


def rcopy(src, dst, ssem, rsem, dev):
    return pltpu.make_async_remote_copy(
        src_ref=src, dst_ref=dst, send_sem=ssem, recv_sem=rsem, device_id=dev, device_id_type=MESH
    )


class Gather:
    def __init__(self, place, full, rows, ssem, rsem):
        self.pl, self.full, self.rows, self.ssem, self.rsem = place, full, rows, ssem, rsem

    def block(self, kind, other=0):
        fz, fy, fx = FLIPS[kind]
        start = self.pl.chip(fz, other, fy, fx) * self.rows
        return self.full.at[pl.ds(pl.multiple_of(start, self.rows), self.rows)]

    def send(self, kind, way):
        place = self.pl
        if way == "s":
            dev, slot = place.sib, 8 + kind
        else:
            dev = {"x": place.xn, "y": place.yn, "z": place.zn}[way]
            fz, fy, fx = FLIPS[kind]
            flips = {"x": (fz, fy, 1 - fx), "y": (fz, 1 - fy, fx), "z": (1 - fz, fy, fx)}[way]
            slot = FLIPS.index(flips)
        view = self.block(kind)
        return rcopy(view, view, self.ssem.at[slot], self.rsem.at[slot], dev)

    AFTER = {
        OWN: "zxys",
        ZB: "xys",
        X0: "ys",
        X1: "s",
        Y0: "s",
        Y1: "xs",
        D0: "s",
        D1: "s",
    }

    def start(self, kind):
        for way in self.AFTER[kind]:
            self.send(kind, way).start()

    def arrived(self, kind, other=0):
        view = self.block(kind, other)
        slot = kind + 8 * other
        rcopy(view, view, self.ssem.at[slot], self.rsem.at[slot], self.pl.sib).wait_recv()

    def finish(self):
        for kind in range(8):
            for way in self.AFTER[kind]:
                self.send(kind, way).wait_send()


def hand_in(place, shard, spot, c_rows, ssem, rsem, go):
    mine, theirs = shard.at[place.m], shard.at[1 - place.m]
    here = lambda: pltpu.make_async_copy(mine, spot(place.c), rsem.at[place.c])
    to_sib = lambda: rcopy(mine, spot(place.c), ssem.at[0], rsem.at[place.c], place.sib)
    to_pair = lambda: rcopy(theirs, spot(place.c), ssem.at[1], rsem.at[place.c], place.pair)
    to_cross = lambda: rcopy(theirs, spot(place.c), ssem.at[1], rsem.at[place.c], place.cross)
    if go == "start":

        @pl.when(place.c == place.m)
        def _():
            here().start()
            to_pair().start()

        @pl.when(place.c != place.m)
        def _():
            to_sib().start()
            to_cross().start()

    elif go == "recv":
        for piece in range(2):
            dst = spot(piece)
            rcopy(dst, dst, ssem.at[1], rsem.at[piece], place.sib).wait_recv()
    else:

        @pl.when(place.c != place.m)
        def _():
            to_sib().wait_send()

        to_pair().wait_send()


def ag_kernel(spread, *refs):
    (pat, dog, lay, wq, wp, w1, w2, sm, pat_o, dog_o, lay_o, fq, fp, f1, f2, fs) = refs[:16]
    (gq, gp, g1, hs, hr, ss, rs, as_, ar) = refs[16:]
    place = Place(spread)
    place.greet()
    hand = (
        (sm, fs, None, 16),
        (wq, fq, gq, 24),
        (wp, fp, gp, 24),
        (w1, f1, g1, 24),
        (w2, f2, None, w2.shape[1]),
    )
    gathers = [
        Gather(place, full, 2 * rows, ss.at[k], rs.at[k])
        for k, (_, full, _, rows) in enumerate(hand)
    ]

    def spot_of(k):
        _, full, stage, rows = hand[k]
        if stage is not None:
            return lambda piece: stage.at[piece]
        own = place.chip(0, 0, 0, 0) * 2

        def spot(piece):
            place_of = place.p if piece is place.c else own + piece
            return full.at[pl.ds(pl.multiple_of(place_of * rows, 16), rows)]

        return spot

    acts = [
        rcopy(pat.at[1 - place.m], pat_o, as_.at[0], ar.at[0], place.pair),
        rcopy(lay, lay_o, as_.at[2], ar.at[2], place.pair),
        rcopy(dog.at[1 - place.m], dog_o, as_.at[1], ar.at[1], place.pair),
    ]
    for k in range(5):
        hand_in(place, hand[k][0], spot_of(k), hand[k][3], hs.at[k], hr.at[k], "start")
    for act in acts:
        act.start()
    for k in range(5):
        hand_in(place, hand[k][0], spot_of(k), hand[k][3], hs.at[k], hr.at[k], "recv")
        _, full, stage, rows = hand[k]
        if stage is not None:
            both = jnp.concatenate([stage[0].astype(F32), stage[1].astype(F32)], axis=0)
            start = pl.multiple_of(place.chip(0, 0, 0, 0) * (2 * rows), 2 * rows)
            full[pl.ds(start, 2 * rows), :] = both.astype(BF)
        gathers[k].start(OWN)
    for k in range(5):
        for kind in (ZB, X0, Y0, X1, Y1, D0, D1):
            gathers[k].arrived(kind)
            gathers[k].start(kind)
    for k in range(5):
        for kind in range(8):
            gathers[k].arrived(kind, 1)
    for k in range(5):
        hand_in(place, hand[k][0], spot_of(k), hand[k][3], hs.at[k], hr.at[k], "send")
        gathers[k].finish()
    for act in acts:
        act.wait()


def all_gather(spread, pat, dog, lay, wq, wp, w1, w2, sm):
    any_, vm = pl.BlockSpec(memory_space=pl.ANY), pl.BlockSpec(memory_space=pltpu.VMEM)
    d = pat.shape[2]
    f32, bf = jnp.float32, BF
    out = [
        jax.ShapeDtypeStruct(pat.shape[1:], bf),
        jax.ShapeDtypeStruct(pat.shape[1:], bf),
        jax.ShapeDtypeStruct(lay.shape, f32),
        jax.ShapeDtypeStruct((d, wq.shape[2]), bf),
        jax.ShapeDtypeStruct((d, wp.shape[2]), bf),
        jax.ShapeDtypeStruct((d, w1.shape[2]), bf),
        jax.ShapeDtypeStruct((w2.shape[1] * RING, d), bf),
        jax.ShapeDtypeStruct((RING * 16, 128), bf),
    ]
    dma = pltpu.SemaphoreType.DMA
    return pl.pallas_call(
        functools.partial(ag_kernel, spread),
        out_shape=out,
        in_specs=[any_] * 8,
        out_specs=[any_, any_, any_] + [vm] * 5,
        scratch_shapes=[
            pltpu.VMEM((2, 24, wq.shape[2]), bf),
            pltpu.VMEM((2, 24, wp.shape[2]), bf),
            pltpu.VMEM((2, 24, w1.shape[2]), bf),
            dma((5, 2)),
            dma((5, 2)),
            dma((5, 16)),
            dma((5, 16)),
            dma((3,)),
            dma((3,)),
        ],
        compiler_params=pltpu.CompilerParams(
            collective_id=0, has_side_effects=True, vmem_limit_bytes=48 * 2**20
        ),
        name="gather",
    )(pat, dog, lay, wq, wp, w1, w2, sm)


class Scatter:
    def __init__(self, place, full, rows, got_sib, got, ssem, rsem):
        self.pl, self.full, self.rows = place, full, rows
        self.got_sib, self.got, self.ssem, self.rsem = got_sib, got, ssem, rsem

    def start_of(self, kind):
        fz, fy, fx = FLIPS[kind]
        return pl.multiple_of(self.pl.chip(fz, 0, fy, fx) * self.rows, self.rows)

    def plane(self, z, other):
        c = 1 - self.pl.c if other else self.pl.c
        return pl.ds(pl.multiple_of((z * 2 + c) * (4 * self.rows), self.rows), 4 * self.rows)

    def sib(self, z):
        return rcopy(
            self.full.at[self.plane(z, 1)],
            self.got_sib.at[z],
            self.ssem.at[z],
            self.rsem.at[z],
            self.pl.sib,
        )

    MOVES = {D0: ("y", 0), D1: ("x", 1), X0: ("x", 2), X1: ("x", 3), Y0: ("y", 4), Y1: ("y", 5), ZB: ("z", 6)}

    def move(self, kind):
        way, slot = self.MOVES[kind]
        dev = {"x": self.pl.xn, "y": self.pl.yn, "z": self.pl.zn}[way]
        return rcopy(
            self.full.at[pl.ds(self.start_of(kind), self.rows)],
            self.got.at[slot],
            self.ssem.at[2 + slot],
            self.rsem.at[2 + slot],
            dev,
        )

    def add(self, kind, slots):
        rows = pl.ds(self.start_of(kind), self.rows)
        total = self.full[rows, :].astype(F32)
        for slot in slots:
            total = total + self.got[slot].astype(F32)
        self.full[rows, :] = total.astype(BF)

    def begin(self):
        self.sib(0).start()
        self.sib(1).start()

    def second(self):
        for z in range(2):
            self.sib(z).wait()
        step = 16

        for z in range(2):
            base = (z * 2 + self.pl.c) * (4 * self.rows)

            @pl.loop(0, 4 * self.rows // step)
            def _(i, z=z, base=base):
                rows = pl.ds(pl.multiple_of(base + i * step, step), step)
                theirs = self.got_sib[z, pl.ds(pl.multiple_of(i * step, step), step), :]
                self.full[rows, :] = (self.full[rows, :].astype(F32) + theirs.astype(F32)).astype(BF)

        for kind in (D0, D1, X1, Y0):
            self.move(kind).start()

    def third(self):
        self.move(D0).wait()
        self.add(X0, (0,))
        self.move(X0).start()
        self.move(D1).wait()
        self.add(Y1, (1,))
        self.move(Y1).start()

    def fourth(self):
        self.move(X1).wait()
        self.move(Y1).wait()
        self.add(ZB, (3, 5))
        self.move(ZB).start()

    def total(self):
        self.move(X0).wait()
        self.move(Y0).wait()
        self.move(ZB).wait()
        rows = pl.ds(self.start_of(OWN), self.rows)
        total = self.full[rows, :].astype(F32)
        for slot in (2, 4, 6):
            total = total + self.got[slot].astype(F32)
        return total


def hand_back(place, stage, out, ssem, rsem, go):
    if go == "start":

        @pl.when(place.c == place.m)
        def _():
            pltpu.make_async_copy(stage.at[place.c], out.at[place.m], rsem.at[place.m]).start()
            rcopy(
                stage.at[1 - place.c], out.at[place.m], ssem.at[0], rsem.at[place.m], place.sib
            ).start()

        @pl.when(place.c != place.m)
        def _():
            rcopy(
                stage.at[place.c], out.at[place.m], ssem.at[0], rsem.at[place.m], place.pair
            ).start()
            rcopy(
                stage.at[1 - place.c], out.at[place.m], ssem.at[1], rsem.at[place.m], place.cross
            ).start()

    elif go == "recv":
        for k in range(2):
            rcopy(out.at[k], out.at[k], ssem.at[0], rsem.at[k], place.sib).wait_recv()
    else:
        rcopy(stage.at[0], out.at[0], ssem.at[0], rsem.at[0], place.sib).wait_send()

        @pl.when(place.c != place.m)
        def _():
            rcopy(stage.at[0], out.at[0], ssem.at[1], rsem.at[0], place.sib).wait_send()


def rs_kernel(spread, *refs):
    (gq, gp, g1, g2, gs, enc, pgr) = refs[:7]
    (oq, op, o1, o2, os_, enc_o, pgr_o) = refs[7:14]
    scratch = refs[14:]
    got_sib, got, stages = scratch[0:4], scratch[4:8], scratch[8:12]
    (sgot, ss, rs, hs, hr, es, er, ts, tr) = scratch[12:]
    place = Place(spread)
    place.greet()
    acts = [
        rcopy(enc, enc_o, es.at[0], er.at[0], place.pair),
        rcopy(pgr, pgr_o, es.at[1], er.at[1], place.pair),
    ]
    for act in acts:
        act.start()
    order = (3, 2, 1, 0)
    fulls = (gq, gp, g1, g2)
    outs = (oq, op, o1, o2)
    rows = (48, 48, 48, g2.shape[0] // 16)
    sc = [
        Scatter(place, fulls[k], rows[k], got_sib[k], got[k], ss.at[k], rs.at[k]) for k in range(4)
    ]
    for k in order:
        sc[k].begin()
    os_[place.m] = gs[...]
    for i, dev in enumerate((place.sib, place.xn, place.yn, place.zn)):
        copy = rcopy(os_.at[place.m], sgot.at[i], ts.at[i], tr.at[i], dev)
        copy.start()
        copy.wait()
        os_[place.m] = os_[place.m] + sgot[i]
    copy = rcopy(os_.at[place.m], os_.at[place.m], ts.at[4], tr.at[4], place.pair)
    copy.start()
    for k in order:
        sc[k].second()
    for k in order:
        sc[k].third()
    for k in order:
        sc[k].fourth()
    for k in order:
        total = sc[k].total()
        half = rows[k] // 2
        stages[k][0] = total[:half].astype(BF)
        stages[k][1] = total[half:].astype(BF)
        hand_back(place, stages[k], outs[k], hs.at[k], hr.at[k], "start")
    for k in order:
        hand_back(place, stages[k], outs[k], hs.at[k], hr.at[k], "recv")
        hand_back(place, stages[k], outs[k], hs.at[k], hr.at[k], "send")
    copy.wait_send()
    theirs = os_.at[1 - place.m]
    rcopy(theirs, theirs, ts.at[4], tr.at[4], place.pair).wait_recv()
    for act in acts:
        act.wait()


def reduce_scatter(spread, gq, gp, g1, g2, gs, enc, pgr):
    any_, vm = pl.BlockSpec(memory_space=pl.ANY), pl.BlockSpec(memory_space=pltpu.VMEM)
    d = gq.shape[0]
    fulls = (gq, gp, g1, g2)
    rows = [g.shape[0] // 16 for g in fulls]
    out = [jax.ShapeDtypeStruct((2, r // 2, g.shape[1]), BF) for r, g in zip(rows, fulls)]
    out += [
        jax.ShapeDtypeStruct((2,) + gs.shape, F32),
        jax.ShapeDtypeStruct(enc.shape, BF),
        jax.ShapeDtypeStruct(pgr.shape, BF),
    ]
    dma = pltpu.SemaphoreType.DMA
    return pl.pallas_call(
        functools.partial(rs_kernel, spread),
        out_shape=out,
        in_specs=[vm] * 5 + [any_] * 2,
        out_specs=[any_] * 4 + [vm] + [any_] * 2,
        scratch_shapes=[pltpu.VMEM((2, 4 * r, g.shape[1]), BF) for r, g in zip(rows, fulls)]
        + [pltpu.VMEM((7, r, g.shape[1]), BF) for r, g in zip(rows, fulls)]
        + [pltpu.VMEM((2, r // 2, g.shape[1]), BF) for r, g in zip(rows, fulls)]
        + [
            pltpu.VMEM((4,) + gs.shape, F32),
            dma((4, 9)),
            dma((4, 9)),
            dma((4, 2)),
            dma((4, 2)),
            dma((2,)),
            dma((2,)),
            dma((5,)),
            dma((5,)),
        ],
        compiler_params=pltpu.CompilerParams(
            collective_id=1, has_side_effects=True, vmem_limit_bytes=56 * 2**20
        ),
        name="scatter",
    )(gq, gp, g1, g2, gs, enc, pgr)


def small_pack(parts, b1):
    rows = jnp.stack([jnp.pad(v, ((0, 0), (0, 128 - v.shape[1]))) for v in (*parts, b1)], axis=1)
    return jnp.pad(rows, ((0, 0), (0, 16 - rows.shape[1]), (0, 0)))


def norm_stats(v):
    mean = jnp.mean(v, axis=-1, keepdims=True)
    center = v - mean
    r = lax.rsqrt(jnp.mean(center * center, axis=-1, keepdims=True) + 1e-06)
    return center * r, r


def norm_back(dn, nhat, r, gain):
    dh = dn * gain
    row = r * (
        dh - jnp.mean(dh, axis=-1, keepdims=True) - nhat * jnp.mean(dh * nhat, axis=-1, keepdims=True)
    )
    return row, jnp.sum(dn * nhat, axis=0), jnp.sum(dn, axis=0)


def mm(a, b, ca, cb):
    return lax.dot_general(a, b, (((ca,), (cb,)), ((), ())), preferred_element_type=F32)


def compute(xs, dos, lays, wq, wp, w1, w2, vecs, b1):
    d = xs.shape[1]
    rows = lays.shape[2]
    hd = d // HEADS
    g1n, b1n, bp, g2n, b2n, bf2 = (vecs[i] for i in range(6))
    seg, gr, gc, live = (lays[:, i] for i in range(4))
    dist = jnp.sqrt(
        (gr[:, :, None] - gr[:, None, :]) ** 2 + (gc[:, :, None] - gc[:, None, :]) ** 2
    )
    dist = jnp.where(seg[:, :, None] == seg[:, None, :], dist, FAR)
    slopes = jnp.exp2(-8.0 * (jnp.arange(HEADS, dtype=F32) + 1.0) / HEADS)
    x = xs.astype(F32)
    n1, r1 = norm_stats(x)
    a = (n1 * g1n + b1n).astype(BF)
    qkv = mm(a, wq, 1, 0).astype(BF)
    heads = qkv.reshape(2, rows, 3, HEADS, hd)
    q, k, v = heads[:, :, 0], heads[:, :, 1], heads[:, :, 2]
    s = (
        jnp.einsum("gqhd,gkhd->ghqk", q, k, preferred_element_type=F32) * hd**-0.5
        - slopes[None, :, None, None] * dist[:, None]
    )
    prob = jax.nn.softmax(s, axis=-1)
    pb = prob.astype(BF)
    o = jnp.einsum("ghqk,gkhd->gqhd", pb, v, preferred_element_type=F32).astype(BF)
    o = o.reshape(2 * rows, d)
    y1 = x + (mm(o, wp, 1, 0) + bp)
    n2, r2 = norm_stats(y1)
    c = (n2 * g2n + b2n).astype(BF)
    u = mm(c, w1, 1, 0) + b1
    phi = 0.5 * (1.0 + lax.erf(u * 2**-0.5))
    g = (u * phi).astype(BF)
    slope = phi + u * (jnp.exp(-0.5 * u * u) * 0.3989422804014327)
    y = y1 + (mm(g, w2, 1, 0) + bf2)
    dy = dos.astype(F32) * live.reshape(-1, 1)
    dz = dy.astype(BF)
    gw2 = mm(g, dz, 0, 0).astype(BF)
    dg = mm(dz, w2, 1, 1)
    du = (dg * slope).astype(BF)
    gw1 = mm(c, du, 0, 0).astype(BF)
    dc = mm(du, w1, 1, 1)
    row, gg2, gb2 = norm_back(dc, n2, r2, g2n)
    dy1 = dy + row
    dy1r = dy1.astype(BF)
    gwp = mm(o, dy1r, 0, 0).astype(BF)
    do = mm(dy1r, wp, 1, 1).astype(BF).reshape(2, rows, HEADS, hd)
    dv = jnp.einsum("ghqk,gqhd->gkhd", pb, do, preferred_element_type=F32)
    dp = jnp.einsum("gqhd,gkhd->ghqk", do, v, preferred_element_type=F32)
    ds = (prob * (dp - jnp.sum(prob * dp, axis=-1, keepdims=True))).astype(BF)
    dq = jnp.einsum("ghqk,gkhd->gqhd", ds, k, preferred_element_type=F32) * hd**-0.5
    dk = jnp.einsum("ghqk,gqhd->gkhd", ds, q, preferred_element_type=F32) * hd**-0.5
    dqkv = jnp.stack([dq, dk, dv], axis=2).reshape(2 * rows, 3 * d).astype(BF)
    gwq = mm(a, dqkv, 0, 0).astype(BF)
    da = mm(dqkv, wq, 1, 1)
    row, gg1, gb1 = norm_back(da, n1, r1, g1n)
    sums = [
        gg1,
        gb1,
        jnp.sum(dy1r.astype(F32), axis=0),
        gg2,
        gb2,
        jnp.sum(dz.astype(F32), axis=0),
    ]
    bias1 = jnp.sum(du.astype(F32), axis=0).reshape(-1, d)
    small = jnp.concatenate([jnp.stack(sums), bias1], axis=0)
    small = jnp.pad(small, ((0, 16 - small.shape[0]), (0, 0)))
    return y.astype(BF), (dy1 + row).astype(BF), gwq, gwp, gw1, gw2, small


def local(
    count, patches, tile_kind, out_grad, n1g, n1b, wq, wp, bp, n2g, n2b, w1, b1, w2, b2
):
    spread = count // RING
    idx = lax.axis_index("fsdp")
    p = idx // spread
    m = (p // 8) % 2
    rows, d = patches.shape[1:]
    parts = (n1g, n1b, bp, n2g, n2b, b2)
    if spread > 1:
        groups = [[q * spread + j for j in range(spread)] for q in range(RING)]
        ag = functools.partial(
            lax.all_gather, axis_name="fsdp", axis=1, tiled=True, axis_index_groups=groups
        )
        wq, wp, w1, w2, b1 = ag(wq), ag(wp), ag(w1), ag(w2), ag(b1)
        parts = tuple(ag(v) for v in parts)
    lay = jnp.stack([v.astype(F32) for v in packing(tile_kind, rows)])
    lay = jnp.pad(lay, ((0, 4), (0, 0)))
    sm = small_pack(parts, b1)
    pat2, dog2, lay2, fq, fp, f1, f2, fs = all_gather(
        spread, patches, out_grad, lay, wq, wp, w1, w2, sm
    )
    own = b2.shape[1] * spread
    fs = fs.astype(F32).reshape(RING, 16, 128)
    vecs = fs[:, :6, : d // RING].transpose(1, 0, 2).reshape(6, d)
    hb = fs[:, 6, : w2.shape[1]].reshape(-1)
    mine = lambda v: lax.dynamic_index_in_dim(v, m, 0, keepdims=False)
    y, pg, gq, gp, g1, g2, gs = compute(
        jnp.concatenate([mine(patches), pat2]),
        jnp.concatenate([mine(out_grad), dog2]),
        jnp.stack([lay, lay2]),
        fq, fp, f1, f2, vecs, hb,
    )
    oq, op, o1, o2, os_, enc2, pg2 = reduce_scatter(
        spread, gq, gp, g1, g2, gs, y[rows:], pg[rows:]
    )
    order = lambda a, b: jnp.where(m == 0, jnp.stack([a, b]), jnp.stack([b, a]))
    encoded = order(y[:rows], enc2)
    pgrad = order(pg[:rows], pg2).astype(F32)
    seg = d // RING
    vec = lax.dynamic_slice_in_dim(os_[:, :6], p * seg, seg, axis=2)
    hid = os_[:, 6 : 6 + w2.shape[1] * RING // d].reshape(2, -1)
    hid = lax.dynamic_slice_in_dim(hid, p * w2.shape[1], w2.shape[1], axis=1)
    grads = [oq.astype(F32), op.astype(F32), o1.astype(F32), o2.astype(F32)]
    if spread > 1:
        rs = functools.partial(
            lax.psum_scatter, axis_name="fsdp", tiled=True, axis_index_groups=groups
        )
        grads = [rs(v, scatter_dimension=1) for v in grads]
        vec, hid = rs(vec, scatter_dimension=2), rs(hid, scatter_dimension=1)
    return (
        encoded,
        pgrad,
        vec[:, 0],
        vec[:, 1],
        grads[0],
        grads[1],
        vec[:, 2],
        vec[:, 3],
        vec[:, 4],
        grads[2],
        hid,
        grads[3],
        vec[:, 5],
    )


def solution(mesh):
    three, two = P(None, "fsdp", None), P(None, "fsdp")
    in_specs = (three, P("fsdp"), three, two, two, three, three, two, two, two, three, two, three, two)
    out_specs = (three, three, two, two, three, three, two, two, two, three, two, three, two)
    return jax.shard_map(
        functools.partial(local, mesh.shape["fsdp"]),
        mesh=mesh,
        in_specs=in_specs,
        out_specs=out_specs,
        check_vma=False,
    )
```

```python
import functools

import jax
import jax.numpy as jnp
from jax import lax
from jax.experimental import pallas as pl
from jax.experimental.pallas import tpu as pltpu
from jax.sharding import PartitionSpec as P

HEADS = 12
SIDE_S = 12
SIDE_M = 15
SIDE_L = 20
RING = 32
MESH = pl.DeviceIdType.MESH
BF = jnp.bfloat16
F32 = jnp.float32
FAR = 1e33


def packing(kind_ids, row_count):
    slot_count = kind_ids.shape[0]
    sides = jnp.where(kind_ids == 0, SIDE_S, jnp.where(kind_ids == 1, SIDE_M, SIDE_L)).astype(
        jnp.int32
    )
    lengths = sides * sides
    slots = jnp.arange(slot_count, dtype=jnp.int32)
    ends = jnp.sum(jnp.where(slots[None, :] <= slots[:, None], lengths[None, :], 0), axis=1)
    starts = ends - lengths
    places = jnp.arange(row_count, dtype=jnp.int32)
    inside = (
        (ends <= row_count)[None, :]
        & (places[:, None] >= starts[None, :])
        & (places[:, None] < ends[None, :])
    ).astype(jnp.int32)
    filled = jnp.sum(inside, axis=1)
    segment = jnp.sum(inside * slots[None, :], axis=1) + (1 - filled) * (slot_count + places)
    offset = places - jnp.sum(inside * starts[None, :], axis=1)
    side = jnp.sum(inside * sides[None, :], axis=1) + (1 - filled)
    return segment, offset // side, offset % side, filled


class Place:
    def __init__(self, spread):
        me = lax.axis_index("fsdp")
        rest = lax.rem(me, spread)
        p = me // spread
        self.p = p
        self.c = lax.rem(p, 2)
        self.x = lax.rem(p // 2, 2)
        self.y = lax.rem(p // 4, 2)
        self.m = lax.rem(p // 8, 2)
        self.z = lax.rem(p // 16, 2)
        dev = lambda q: (q * spread + rest,)
        sib = p + 1 - 2 * self.c
        pair = p + 8 * (1 - 2 * self.m)
        self.sib = dev(sib)
        self.xn = dev(p + 2 * (1 - 2 * self.x))
        self.yn = dev(p + 4 * (1 - 2 * self.y))
        self.zn = dev(p + 16 * (1 - 2 * self.z))
        self.pair = dev(pair)
        self.cross = dev(pair + 1 - 2 * self.c)

    def chip(self, fz, fc, fy, fx):
        flip = lambda v, f: 1 - v if f else v
        return (
            (flip(self.z, fz) * 2 + flip(self.c, fc)) * 2 + flip(self.y, fy)
        ) * 2 + flip(self.x, fx)

    def greet(self):
        barrier = pltpu.get_barrier_semaphore()
        everyone = (self.sib, self.xn, self.yn, self.zn, self.pair, self.cross)
        for other in everyone:
            pl.semaphore_signal(barrier, inc=1, device_id=other, device_id_type=MESH)
        pl.semaphore_wait(barrier, len(everyone))


OWN, ZB, X0, X1, Y0, Y1, D0, D1 = range(8)
FLIPS = ((0, 0, 0), (1, 0, 0), (0, 0, 1), (1, 0, 1), (0, 1, 0), (1, 1, 0), (0, 1, 1), (1, 1, 1))


def rcopy(src, dst, ssem, rsem, dev):
    return pltpu.make_async_remote_copy(
        src_ref=src, dst_ref=dst, send_sem=ssem, recv_sem=rsem, device_id=dev, device_id_type=MESH
    )


class Gather:
    def __init__(self, place, full, rows, ssem, rsem):
        self.pl, self.full, self.rows, self.ssem, self.rsem = place, full, rows, ssem, rsem

    def block(self, kind, other=0):
        fz, fy, fx = FLIPS[kind]
        start = self.pl.chip(fz, other, fy, fx) * self.rows
        return self.full.at[pl.ds(pl.multiple_of(start, self.rows), self.rows)]

    def send(self, kind, way):
        place = self.pl
        if way == "s":
            dev, slot = place.sib, 8 + kind
        else:
            dev = {"x": place.xn, "y": place.yn, "z": place.zn}[way]
            fz, fy, fx = FLIPS[kind]
            flips = {"x": (fz, fy, 1 - fx), "y": (fz, 1 - fy, fx), "z": (1 - fz, fy, fx)}[way]
            slot = FLIPS.index(flips)
        view = self.block(kind)
        return rcopy(view, view, self.ssem.at[slot], self.rsem.at[slot], dev)

    AFTER = {
        OWN: "zxys",
        ZB: "xys",
        X0: "ys",
        X1: "s",
        Y0: "s",
        Y1: "xs",
        D0: "s",
        D1: "s",
    }

    def start(self, kind):
        for way in self.AFTER[kind]:
            self.send(kind, way).start()

    def arrived(self, kind, other=0):
        view = self.block(kind, other)
        slot = kind + 8 * other
        rcopy(view, view, self.ssem.at[slot], self.rsem.at[slot], self.pl.sib).wait_recv()

    def finish(self):
        for kind in range(8):
            for way in self.AFTER[kind]:
                self.send(kind, way).wait_send()


def hand_in(place, shard, spot, c_rows, ssem, rsem, go):
    mine, theirs = shard.at[place.m], shard.at[1 - place.m]
    here = lambda: pltpu.make_async_copy(mine, spot(place.c), rsem.at[place.c])
    to_sib = lambda: rcopy(mine, spot(place.c), ssem.at[0], rsem.at[place.c], place.sib)
    to_pair = lambda: rcopy(theirs, spot(place.c), ssem.at[1], rsem.at[place.c], place.pair)
    to_cross = lambda: rcopy(theirs, spot(place.c), ssem.at[1], rsem.at[place.c], place.cross)
    if go == "start":

        @pl.when(place.c == place.m)
        def _():
            here().start()
            to_pair().start()

        @pl.when(place.c != place.m)
        def _():
            to_sib().start()
            to_cross().start()

    elif go == "recv":
        for piece in range(2):
            dst = spot(piece)
            rcopy(dst, dst, ssem.at[1], rsem.at[piece], place.sib).wait_recv()
    else:

        @pl.when(place.c != place.m)
        def _():
            to_sib().wait_send()

        to_pair().wait_send()


def dot(a, b, ca, cb):
    return lax.dot_general(a, b, (((ca,), (cb,)), ((), ())), preferred_element_type=F32)


def chunks(count, step, body):
    @pl.loop(0, count // step)
    def _(i):
        body(pl.ds(pl.multiple_of(i * step, step), step))


def norm(v):
    center = v - jnp.mean(v, axis=-1, keepdims=True)
    r = lax.rsqrt(jnp.mean(center * center, axis=-1, keepdims=True) + 1e-06)
    return center * r, r


def fill_distance(dist, lay):
    across = lay[...]
    down = across.T
    gap_r = down[:, 1:2] - across[1:2]
    gap_c = down[:, 2:3] - across[2:3]
    far = jnp.sqrt(gap_r * gap_r + gap_c * gap_c)
    dist[...] = jnp.where(down[:, 0:1] == across[0:1], far, FAR)


def lanes(half):
    return lax.broadcasted_iota(jnp.int32, (1, 128), 1) // 64 == half


def slope_of(head):
    return jnp.exp2(jnp.full((1, 1), -8.0 / HEADS, F32) * (head + 1).astype(F32))


def attend_pair(qkv, rows, dist, j, prob, slot, o, d):
    col = pl.multiple_of(j * 128, 128)
    q = qkv[rows, pl.ds(col, 128)] * jnp.asarray(0.125, BF)
    k = qkv[rows, pl.ds(d + col, 128)]
    v = qkv[rows, pl.ds(2 * d + col, 128)]
    zero = jnp.zeros((), BF)
    total = None
    for half in range(2):
        keep = lanes(half)
        s = dot(k, jnp.where(keep, q, zero), 1, 1) - slope_of(2 * j + half) * dist
        e = jnp.exp(s - jnp.max(s, axis=0, keepdims=True))
        p = (e * (1.0 / jnp.sum(e, axis=0, keepdims=True))).astype(BF)
        prob[slot + half] = p
        part = dot(jnp.where(keep, v, zero), p, 0, 0)
        total = part if total is None else total + part
    o[rows, pl.ds(col, 128)] = total.T.astype(BF)


def forward_kernel(spread, *refs):
    (pat, dog, lay, wq, wp, w1, w2, sm) = refs[:8]
    (x_o, dog_o, lay_o, wq_o, wp_o, w1_o, w2_o, vec_o, b1_o) = refs[8:17]
    (qkv_o, p_o, o_o, y1_o, c_o, g_o, gs_o, enc_o) = refs[17:25]
    (fq, fp, f1, f2, fs, gq, gp, g1) = refs[25:33]
    (lays, dist, xb, ac, qkv, prob, ob, y1, g, gs) = refs[33:43]
    (hs, hr, ss, rs, as_, ar, ls, ps) = refs[43:]
    place = Place(spread)
    d = xb.shape[2]
    n = xb.shape[1]
    place.greet()
    hand = ((sm, fs, None, 16), (wq, fq, gq, 24), (wp, fp, gp, 24), (w1, f1, g1, 24))
    hand += ((w2, f2, None, w2.shape[1]),)
    gathers = [
        Gather(place, full, 2 * rows, ss.at[k], rs.at[k])
        for k, (_, full, _, rows) in enumerate(hand)
    ]

    def spot_of(k):
        _, full, stage, rows = hand[k]
        if stage is not None:
            return lambda piece: stage.at[piece]
        own = place.chip(0, 0, 0, 0) * 2

        def spot(piece):
            place_of = place.p if piece is place.c else own + piece
            return full.at[pl.ds(pl.multiple_of(place_of * rows, 16), rows)]

        return spot

    def hand_over(k, go):
        hand_in(place, hand[k][0], spot_of(k), hand[k][3], hs.at[k], hr.at[k], go)

    def own_ready(k):
        hand_over(k, "recv")
        _, full, stage, rows = hand[k]
        if stage is not None:
            both = jnp.concatenate([stage[0].astype(F32), stage[1].astype(F32)], axis=0)
            start = pl.multiple_of(place.chip(0, 0, 0, 0) * (2 * rows), 2 * rows)
            full[pl.ds(start, 2 * rows), :] = both.astype(BF)
        gathers[k].start(OWN)

    def pump(k, *kinds):
        for kind in kinds:
            gathers[k].arrived(kind)
            gathers[k].start(kind)

    def whole(k):
        for kind in range(8):
            gathers[k].arrived(kind, 1)

    saves = []

    def save(src, dst):
        copy = pltpu.make_async_copy(src, dst, ls.at[len(saves)])
        copy.start()
        saves.append(copy)

    acts = [
        rcopy(pat.at[1 - place.m], xb.at[1], as_.at[0], ar.at[0], place.pair),
        rcopy(lay, lays.at[1], as_.at[2], ar.at[2], place.pair),
        rcopy(dog.at[1 - place.m], dog_o, as_.at[1], ar.at[1], place.pair),
    ]
    own_x = pltpu.make_async_copy(pat.at[place.m], xb.at[0], ps.at[0])
    own_lay = pltpu.make_async_copy(lay, lays.at[0], ps.at[1])
    for k in range(3):
        hand_over(k, "start")
    own_lay.start()
    own_x.start()
    own_lay.wait()
    fill_distance(dist.at[0], lays.at[0])
    for k in range(3):
        own_ready(k)
    hand_over(3, "start")
    acts[1].start()
    acts[0].start()
    hand_over(4, "start")
    pump(0, ZB, X0, Y0, X1, Y1, D0, D1)
    own_ready(3)
    pump(1, ZB, X0, Y0, X1, Y1, D0, D1)
    own_ready(4)
    acts[2].start()
    whole(0)
    seg = d // RING
    hid = w2.shape[1]
    for q in range(RING):
        tile = fs[16 * q : 16 * q + 16].astype(F32)
        vec_o[0:8, seg * q : seg * q + seg] = tile[0:8, 0:seg]
        b1_o[0:1, hid * q : hid * q + hid] = tile[6:7, 0:hid]
    own_x.wait()

    def first_norm(grp):
        def body(rows):
            nhat, _ = norm(xb[grp, rows, :].astype(F32))
            here = pl.ds(pl.multiple_of(grp * n + rows.start, 128), 128)
            ac[here, :] = (nhat * vec_o[0:1] + vec_o[1:2]).astype(BF)

        chunks(n, 128, body)

    first_norm(0)
    whole(1)
    save(fq, wq_o)
    qkv[0:n] = dot(ac[0:n], fq[...], 1, 0).astype(BF)
    acts[1].wait_recv()
    fill_distance(dist.at[1], lays.at[1])
    acts[0].wait_recv()
    first_norm(1)
    qkv[n : 2 * n] = dot(ac[n : 2 * n], fq[...], 1, 0).astype(BF)
    save(qkv, qkv_o)
    save(xb.at[1], x_o)
    save(lays.at[1], lay_o)
    pairs = HEADS // 2
    early = {
        0: [(2, ZB, X0, Y0)],
        1: [(2, X1, Y1)],
        2: [(2, D0, D1)],
        3: [(3, ZB, X0, Y0)],
        5: [(3, X1, Y1)],
        7: [(3, D0, D1)],
        9: [(4, X0, Y0)],
        10: [(4, ZB)],
    }

    @pl.loop(0, 2 * pairs)
    def _(i):
        grp, j = i // pairs, lax.rem(i, pairs)
        rows = pl.ds(pl.multiple_of(grp * n, n), n)
        attend_pair(qkv, rows, dist[grp], j, prob, 2 * i, ob, d)
        pltpu.make_async_copy(
            prob.at[pl.ds(2 * i, 2)], p_o.at[pl.ds(2 * i, 2)], ps.at[2 + i]
        ).start()
        for at, steps in early.items():

            @pl.when(i == at)
            def _(steps=steps):
                for step in steps:
                    pump(*step)

    save(ob, o_o)
    whole(2)
    save(fp, wp_o)

    def second_norm(rows):
        first = (
            xb[rows.start // n, pl.ds(pl.multiple_of(lax.rem(rows.start, n), 256), 256), :].astype(F32)
            + dot(ob[rows, :], fp[...], 1, 0)
            + vec_o[2:3]
        )
        y1[rows, :] = first
        nhat, _ = norm(first)
        ac[rows, :] = (nhat * vec_o[3:4] + vec_o[4:5]).astype(BF)

    chunks(2 * n, 256, second_norm)
    save(y1, y1_o)
    save(ac, c_o)
    pump(4, X1, Y1)
    whole(3)
    save(f1, w1_o)

    def hidden(cols):
        u = dot(ac[...], f1[:, cols], 1, 0) + b1_o[0:1, cols]
        phi = 0.5 + 0.5 * lax.erf(u * 0.7071067811865476)
        g[:, cols] = (u * phi).astype(BF)
        gs[:, cols] = (phi + u * (0.3989422804014327 * jnp.exp(-0.5 * u * u))).astype(BF)

    chunks(g.shape[1], 256, hidden)
    save(g, g_o)
    save(gs, gs_o)
    pump(4, D0, D1)
    whole(4)
    save(f2, w2_o)

    def result(rows):
        ac_rows = y1[rows, :] + dot(g[rows, :], f2[...], 1, 0) + vec_o[5:6]
        qkv[rows, 0:d] = ac_rows.astype(BF)

    saves[1].wait()
    chunks(2 * n, 512, result)
    save(qkv.at[:, pl.ds(0, d)], enc_o)
    for k in range(5):
        hand_over(k, "send")
        gathers[k].finish()
    acts[0].wait_send()
    acts[1].wait_send()
    acts[2].wait()
    for i in range(2 * pairs):
        pltpu.make_async_copy(
            prob.at[pl.ds(2 * i, 2)], p_o.at[pl.ds(2 * i, 2)], ps.at[2 + i]
        ).wait()
    for k, copy in enumerate(saves):
        if k != 1:
            copy.wait()


def forward(spread, pat, dog, lay, wq, wp, w1, w2, sm):
    any_, vm = pl.BlockSpec(memory_space=pl.ANY), pl.BlockSpec(memory_space=pltpu.VMEM)
    n, d = pat.shape[1:]
    ff = w2.shape[1] * RING
    sd = jax.ShapeDtypeStruct
    out = [
        sd((n, d), BF),
        sd((n, d), BF),
        sd(lay.shape, F32),
        sd((d, wq.shape[2]), BF),
        sd((d, d), BF),
        sd((d, ff), BF),
        sd((ff, d), BF),
        sd((8, d), F32),
        sd((8, ff), F32),
        sd((2 * n, wq.shape[2]), BF),
        sd((2 * HEADS, n, n), BF),
        sd((2 * n, d), BF),
        sd((2 * n, d), F32),
        sd((2 * n, d), BF),
        sd((2 * n, ff), BF),
        sd((2 * n, ff), BF),
        sd((2 * n, d), BF),
    ]
    dma = pltpu.SemaphoreType.DMA
    vmem = pltpu.VMEM
    return pl.pallas_call(
        functools.partial(forward_kernel, spread),
        out_shape=out,
        in_specs=[any_] * 8,
        out_specs=[any_] * 7 + [vm] * 2 + [any_] * 8,
        scratch_shapes=[
            vmem((d, wq.shape[2]), BF),
            vmem((d, d), BF),
            vmem((d, ff), BF),
            vmem((ff, d), BF),
            vmem((RING * 16, 128), BF),
            vmem((2, 24, wq.shape[2]), BF),
            vmem((2, 24, d), BF),
            vmem((2, 24, ff), BF),
            vmem((2,) + lay.shape, F32),
            vmem((2, n, n), F32),
            vmem((2, n, d), BF),
            vmem((2 * n, d), BF),
            vmem((2 * n, wq.shape[2]), BF),
            vmem((2 * HEADS, n, n), BF),
            vmem((2 * n, d), BF),
            vmem((2 * n, d), F32),
            vmem((2 * n, ff), BF),
            vmem((2 * n, ff), BF),
            dma((5, 2)),
            dma((5, 2)),
            dma((5, 16)),
            dma((5, 16)),
            dma((3,)),
            dma((3,)),
            dma((16,)),
            dma((2 + HEADS,)),
        ],
        compiler_params=pltpu.CompilerParams(
            collective_id=0, has_side_effects=True, vmem_limit_bytes=62 * 2**20
        ),
        name="forward",
    )(pat, dog, lay, wq, wp, w1, w2, sm)


class Scatter:
    def __init__(self, place, full, rows, got_sib, got, ssem, rsem):
        self.pl, self.full, self.rows = place, full, rows
        self.got_sib, self.got, self.ssem, self.rsem = got_sib, got, ssem, rsem

    def start_of(self, kind):
        fz, fy, fx = FLIPS[kind]
        return pl.multiple_of(self.pl.chip(fz, 0, fy, fx) * self.rows, self.rows)

    def plane(self, z, other):
        c = 1 - self.pl.c if other else self.pl.c
        return pl.ds(pl.multiple_of((z * 2 + c) * (4 * self.rows), self.rows), 4 * self.rows)

    def sib(self, z):
        return rcopy(
            self.full.at[self.plane(z, 1)],
            self.got_sib.at[z],
            self.ssem.at[z],
            self.rsem.at[z],
            self.pl.sib,
        )

    MOVES = {D0: ("y", 0), D1: ("x", 1), X0: ("x", 2), X1: ("x", 3), Y0: ("y", 4), Y1: ("y", 5), ZB: ("z", 6)}

    def move(self, kind):
        way, slot = self.MOVES[kind]
        dev = {"x": self.pl.xn, "y": self.pl.yn, "z": self.pl.zn}[way]
        return rcopy(
            self.full.at[pl.ds(self.start_of(kind), self.rows)],
            self.got.at[slot],
            self.ssem.at[2 + slot],
            self.rsem.at[2 + slot],
            dev,
        )

    def add(self, kind, slots):
        rows = pl.ds(self.start_of(kind), self.rows)
        total = self.full[rows, :].astype(F32)
        for slot in slots:
            total = total + self.got[slot].astype(F32)
        self.full[rows, :] = total.astype(BF)

    def begin(self):
        self.sib(0).start()
        self.sib(1).start()

    def second(self):
        for z in range(2):
            self.sib(z).wait()
        step = 16

        for z in range(2):
            base = (z * 2 + self.pl.c) * (4 * self.rows)

            @pl.loop(0, 4 * self.rows // step)
            def _(i, z=z, base=base):
                rows = pl.ds(pl.multiple_of(base + i * step, step), step)
                theirs = self.got_sib[z, pl.ds(pl.multiple_of(i * step, step), step), :]
                self.full[rows, :] = (self.full[rows, :].astype(F32) + theirs.astype(F32)).astype(BF)

        for kind in (D0, D1, X1, Y0):
            self.move(kind).start()

    def third(self):
        self.move(D0).wait()
        self.add(X0, (0,))
        self.move(X0).start()
        self.move(D1).wait()
        self.add(Y1, (1,))
        self.move(Y1).start()

    def fourth(self):
        self.move(X1).wait()
        self.move(Y1).wait()
        self.add(ZB, (3, 5))
        self.move(ZB).start()

    def total(self):
        self.move(X0).wait()
        self.move(Y0).wait()
        self.move(ZB).wait()
        rows = pl.ds(self.start_of(OWN), self.rows)
        total = self.full[rows, :].astype(F32)
        for slot in (2, 4, 6):
            total = total + self.got[slot].astype(F32)
        return total


def hand_back(place, stage, out, ssem, rsem, go):
    if go == "start":

        @pl.when(place.c == place.m)
        def _():
            pltpu.make_async_copy(stage.at[place.c], out.at[place.m], rsem.at[place.m]).start()
            rcopy(
                stage.at[1 - place.c], out.at[place.m], ssem.at[0], rsem.at[place.m], place.sib
            ).start()

        @pl.when(place.c != place.m)
        def _():
            rcopy(
                stage.at[place.c], out.at[place.m], ssem.at[0], rsem.at[place.m], place.pair
            ).start()
            rcopy(
                stage.at[1 - place.c], out.at[place.m], ssem.at[1], rsem.at[place.m], place.cross
            ).start()

    elif go == "recv":
        for k in range(2):
            rcopy(out.at[k], out.at[k], ssem.at[0], rsem.at[k], place.sib).wait_recv()
    else:
        rcopy(stage.at[0], out.at[0], ssem.at[0], rsem.at[0], place.sib).wait_send()

        @pl.when(place.c != place.m)
        def _():
            rcopy(stage.at[0], out.at[0], ssem.at[1], rsem.at[0], place.sib).wait_send()


def rs_kernel(spread, *refs):
    (gq, gp, g1, g2, gs, enc, pgr) = refs[:7]
    (oq, op, o1, o2, os_, enc_o, pgr_o) = refs[7:14]
    scratch = refs[14:]
    got_sib, got, stages = scratch[0:4], scratch[4:8], scratch[8:12]
    (sgot, ss, rs, hs, hr, es, er, ts, tr) = scratch[12:]
    place = Place(spread)
    place.greet()
    acts = [
        rcopy(enc, enc_o, es.at[0], er.at[0], place.pair),
        rcopy(pgr, pgr_o, es.at[1], er.at[1], place.pair),
    ]
    for act in acts:
        act.start()
    order = (3, 2, 1, 0)
    fulls = (gq, gp, g1, g2)
    outs = (oq, op, o1, o2)
    rows = (48, 48, 48, g2.shape[0] // 16)
    sc = [
        Scatter(place, fulls[k], rows[k], got_sib[k], got[k], ss.at[k], rs.at[k]) for k in range(4)
    ]
    for k in order:
        sc[k].begin()
    os_[place.m] = gs[...]
    for i, dev in enumerate((place.sib, place.xn, place.yn, place.zn)):
        copy = rcopy(os_.at[place.m], sgot.at[i], ts.at[i], tr.at[i], dev)
        copy.start()
        copy.wait()
        os_[place.m] = os_[place.m] + sgot[i]
    copy = rcopy(os_.at[place.m], os_.at[place.m], ts.at[4], tr.at[4], place.pair)
    copy.start()
    for k in order:
        sc[k].second()
    for k in order:
        sc[k].third()
    for k in order:
        sc[k].fourth()
    for k in order:
        total = sc[k].total()
        half = rows[k] // 2
        stages[k][0] = total[:half].astype(BF)
        stages[k][1] = total[half:].astype(BF)
        hand_back(place, stages[k], outs[k], hs.at[k], hr.at[k], "start")
    for k in order:
        hand_back(place, stages[k], outs[k], hs.at[k], hr.at[k], "recv")
        hand_back(place, stages[k], outs[k], hs.at[k], hr.at[k], "send")
    copy.wait_send()
    theirs = os_.at[1 - place.m]
    rcopy(theirs, theirs, ts.at[4], tr.at[4], place.pair).wait_recv()
    for act in acts:
        act.wait()


def reduce_scatter(spread, gq, gp, g1, g2, gs, enc, pgr):
    any_, vm = pl.BlockSpec(memory_space=pl.ANY), pl.BlockSpec(memory_space=pltpu.VMEM)
    d = gq.shape[0]
    fulls = (gq, gp, g1, g2)
    rows = [g.shape[0] // 16 for g in fulls]
    out = [jax.ShapeDtypeStruct((2, r // 2, g.shape[1]), BF) for r, g in zip(rows, fulls)]
    out += [
        jax.ShapeDtypeStruct((2,) + gs.shape, F32),
        jax.ShapeDtypeStruct(enc.shape, BF),
        jax.ShapeDtypeStruct(pgr.shape, BF),
    ]
    dma = pltpu.SemaphoreType.DMA
    return pl.pallas_call(
        functools.partial(rs_kernel, spread),
        out_shape=out,
        in_specs=[vm] * 5 + [any_] * 2,
        out_specs=[any_] * 4 + [vm] + [any_] * 2,
        scratch_shapes=[pltpu.VMEM((2, 4 * r, g.shape[1]), BF) for r, g in zip(rows, fulls)]
        + [pltpu.VMEM((7, r, g.shape[1]), BF) for r, g in zip(rows, fulls)]
        + [pltpu.VMEM((2, r // 2, g.shape[1]), BF) for r, g in zip(rows, fulls)]
        + [
            pltpu.VMEM((4,) + gs.shape, F32),
            dma((4, 9)),
            dma((4, 9)),
            dma((4, 2)),
            dma((4, 2)),
            dma((2,)),
            dma((2,)),
            dma((5,)),
            dma((5,)),
        ],
        compiler_params=pltpu.CompilerParams(
            collective_id=1, has_side_effects=True, vmem_limit_bytes=56 * 2**20
        ),
        name="scatter",
    )(gq, gp, g1, g2, gs, enc, pgr)


def small_pack(parts, b1):
    rows = jnp.stack([jnp.pad(v, ((0, 0), (0, 128 - v.shape[1]))) for v in (*parts, b1)], axis=1)
    return jnp.pad(rows, ((0, 0), (0, 16 - rows.shape[1]), (0, 0)))


def norm_back(dn, nhat, r, gain):
    dh = dn * gain
    row = r * (
        dh - jnp.mean(dh, axis=-1, keepdims=True) - nhat * jnp.mean(dh * nhat, axis=-1, keepdims=True)
    )
    return row, jnp.sum(dn * nhat, axis=0), jnp.sum(dn, axis=0)


def compute(xs, dos, lays, wq, wp, w1, w2, vecs, qkv, prob, o, y1, c, g, slope):
    d = xs.shape[1]
    mm = dot
    rows = lays.shape[2]
    hd = d // HEADS
    g1n, b1n, bp, g2n, b2n, bf2 = (vecs[i] for i in range(6))
    live = lays[:, 3]
    x = xs.astype(F32)
    n1, r1 = norm(x)
    a = (n1 * g1n + b1n).astype(BF)
    heads = qkv.reshape(2, rows, 3, HEADS, hd)
    q, k, v = heads[:, :, 0], heads[:, :, 1], heads[:, :, 2]
    pb = prob.reshape(2, HEADS, rows, rows)
    n2, r2 = norm(y1)
    dy = dos.astype(F32) * live.reshape(-1, 1)
    dz = dy.astype(BF)
    gw2 = mm(g, dz, 0, 0).astype(BF)
    dg = mm(dz, w2, 1, 1)
    du = (dg * slope.astype(F32)).astype(BF)
    gw1 = mm(c, du, 0, 0).astype(BF)
    dc = mm(du, w1, 1, 1)
    row, gg2, gb2 = norm_back(dc, n2, r2, g2n)
    dy1 = dy + row
    dy1r = dy1.astype(BF)
    gwp = mm(o, dy1r, 0, 0).astype(BF)
    do = mm(dy1r, wp, 1, 1).astype(BF).reshape(2, rows, HEADS, hd)
    dv = jnp.einsum("ghkq,gqhd->gkhd", pb, do, preferred_element_type=F32)
    dp = jnp.einsum("gqhd,gkhd->ghkq", do, v, preferred_element_type=F32)
    pf = pb.astype(F32)
    ds = (pf * (dp - jnp.sum(pf * dp, axis=2, keepdims=True))).astype(BF)
    dq = jnp.einsum("ghkq,gkhd->gqhd", ds, k, preferred_element_type=F32) * hd**-0.5
    dk = jnp.einsum("ghkq,gqhd->gkhd", ds, q, preferred_element_type=F32) * hd**-0.5
    dqkv = jnp.stack([dq, dk, dv], axis=2).reshape(2 * rows, 3 * d).astype(BF)
    gwq = mm(a, dqkv, 0, 0).astype(BF)
    da = mm(dqkv, wq, 1, 1)
    row, gg1, gb1 = norm_back(da, n1, r1, g1n)
    sums = [
        gg1,
        gb1,
        jnp.sum(dy1r.astype(F32), axis=0),
        gg2,
        gb2,
        jnp.sum(dz.astype(F32), axis=0),
    ]
    bias1 = jnp.sum(du.astype(F32), axis=0).reshape(-1, d)
    small = jnp.concatenate([jnp.stack(sums), bias1], axis=0)
    small = jnp.pad(small, ((0, 16 - small.shape[0]), (0, 0)))
    return (dy1 + row).astype(BF), gwq, gwp, gw1, gw2, small


def local(
    count, patches, tile_kind, out_grad, n1g, n1b, wq, wp, bp, n2g, n2b, w1, b1, w2, b2
):
    spread = count // RING
    idx = lax.axis_index("fsdp")
    p = idx // spread
    m = (p // 8) % 2
    rows, d = patches.shape[1:]
    parts = (n1g, n1b, bp, n2g, n2b, b2)
    if spread > 1:
        groups = [[q * spread + j for j in range(spread)] for q in range(RING)]
        ag = functools.partial(
            lax.all_gather, axis_name="fsdp", axis=1, tiled=True, axis_index_groups=groups
        )
        wq, wp, w1, w2, b1 = ag(wq), ag(wp), ag(w1), ag(w2), ag(b1)
        parts = tuple(ag(v) for v in parts)
    lay = jnp.stack([v.astype(F32) for v in packing(tile_kind, rows)])
    lay = jnp.pad(lay, ((0, 4), (0, 0)))
    sm = small_pack(parts, b1)
    pat2, dog2, lay2, fq, fp, f1, f2, vecs, _, qkv, prob, o, y1, c, g, slope, y = forward(
        spread, patches, out_grad, lay, wq, wp, w1, w2, sm
    )
    mine = lambda v: lax.dynamic_index_in_dim(v, m, 0, keepdims=False)
    pg, gq, gp, g1, g2, gs = compute(
        jnp.concatenate([mine(patches), pat2]),
        jnp.concatenate([mine(out_grad), dog2]),
        jnp.stack([lay, lay2]),
        fq, fp, f1, f2, vecs, qkv, prob, o, y1, c, g, slope,
    )
    oq, op, o1, o2, os_, enc2, pg2 = reduce_scatter(
        spread, gq, gp, g1, g2, gs, y[rows:], pg[rows:]
    )
    order = lambda a, b: jnp.where(m == 0, jnp.stack([a, b]), jnp.stack([b, a]))
    encoded = order(y[:rows], enc2)
    pgrad = order(pg[:rows], pg2).astype(F32)
    seg = d // RING
    vec = lax.dynamic_slice_in_dim(os_[:, :6], p * seg, seg, axis=2)
    hid = os_[:, 6 : 6 + w2.shape[1] * RING // d].reshape(2, -1)
    hid = lax.dynamic_slice_in_dim(hid, p * w2.shape[1], w2.shape[1], axis=1)
    grads = [oq.astype(F32), op.astype(F32), o1.astype(F32), o2.astype(F32)]
    if spread > 1:
        rs = functools.partial(
            lax.psum_scatter, axis_name="fsdp", tiled=True, axis_index_groups=groups
        )
        grads = [rs(v, scatter_dimension=1) for v in grads]
        vec, hid = rs(vec, scatter_dimension=2), rs(hid, scatter_dimension=1)
    return (
        encoded,
        pgrad,
        vec[:, 0],
        vec[:, 1],
        grads[0],
        grads[1],
        vec[:, 2],
        vec[:, 3],
        vec[:, 4],
        grads[2],
        hid,
        grads[3],
        vec[:, 5],
    )


def solution(mesh):
    three, two = P(None, "fsdp", None), P(None, "fsdp")
    in_specs = (three, P("fsdp"), three, two, two, three, three, two, two, two, three, two, three, two)
    out_specs = (three, three, two, two, three, three, two, two, two, three, two, three, two)
    return jax.shard_map(
        functools.partial(local, mesh.shape["fsdp"]),
        mesh=mesh,
        in_specs=in_specs,
        out_specs=out_specs,
        check_vma=False,
    )
```

```python
import functools

import jax
import jax.numpy as jnp
from jax import lax
from jax.experimental import pallas as pl
from jax.experimental.pallas import tpu as pltpu
from jax.sharding import PartitionSpec as P

HEADS = 12
SIDE_S = 12
SIDE_M = 15
SIDE_L = 20
RING = 32
MESH = pl.DeviceIdType.MESH
BF = jnp.bfloat16
F32 = jnp.float32
FAR = 1e33


def packing(kind_ids, row_count):
    slot_count = kind_ids.shape[0]
    sides = jnp.where(kind_ids == 0, SIDE_S, jnp.where(kind_ids == 1, SIDE_M, SIDE_L)).astype(
        jnp.int32
    )
    lengths = sides * sides
    slots = jnp.arange(slot_count, dtype=jnp.int32)
    ends = jnp.sum(jnp.where(slots[None, :] <= slots[:, None], lengths[None, :], 0), axis=1)
    starts = ends - lengths
    places = jnp.arange(row_count, dtype=jnp.int32)
    inside = (
        (ends <= row_count)[None, :]
        & (places[:, None] >= starts[None, :])
        & (places[:, None] < ends[None, :])
    ).astype(jnp.int32)
    filled = jnp.sum(inside, axis=1)
    segment = jnp.sum(inside * slots[None, :], axis=1) + (1 - filled) * (slot_count + places)
    offset = places - jnp.sum(inside * starts[None, :], axis=1)
    side = jnp.sum(inside * sides[None, :], axis=1) + (1 - filled)
    return segment, offset // side, offset % side, filled


class Place:
    def __init__(self, spread):
        me = lax.axis_index("fsdp")
        rest = lax.rem(me, spread)
        p = me // spread
        self.p = p
        self.c = lax.rem(p, 2)
        self.x = lax.rem(p // 2, 2)
        self.y = lax.rem(p // 4, 2)
        self.m = lax.rem(p // 8, 2)
        self.z = lax.rem(p // 16, 2)
        dev = lambda q: (q * spread + rest,)
        sib = p + 1 - 2 * self.c
        pair = p + 8 * (1 - 2 * self.m)
        self.sib = dev(sib)
        self.xn = dev(p + 2 * (1 - 2 * self.x))
        self.yn = dev(p + 4 * (1 - 2 * self.y))
        self.zn = dev(p + 16 * (1 - 2 * self.z))
        self.pair = dev(pair)
        self.cross = dev(pair + 1 - 2 * self.c)

    def chip(self, fz, fc, fy, fx):
        flip = lambda v, f: 1 - v if f else v
        return (
            (flip(self.z, fz) * 2 + flip(self.c, fc)) * 2 + flip(self.y, fy)
        ) * 2 + flip(self.x, fx)

    def greet(self):
        barrier = pltpu.get_barrier_semaphore()
        everyone = (self.sib, self.xn, self.yn, self.zn, self.pair, self.cross)
        for other in everyone:
            pl.semaphore_signal(barrier, inc=1, device_id=other, device_id_type=MESH)
        pl.semaphore_wait(barrier, len(everyone))


OWN, ZB, X0, X1, Y0, Y1, D0, D1 = range(8)
FLIPS = ((0, 0, 0), (1, 0, 0), (0, 0, 1), (1, 0, 1), (0, 1, 0), (1, 1, 0), (0, 1, 1), (1, 1, 1))


def rcopy(src, dst, ssem, rsem, dev):
    return pltpu.make_async_remote_copy(
        src_ref=src, dst_ref=dst, send_sem=ssem, recv_sem=rsem, device_id=dev, device_id_type=MESH
    )


class Gather:
    def __init__(self, place, full, rows, ssem, rsem):
        self.pl, self.full, self.rows, self.ssem, self.rsem = place, full, rows, ssem, rsem

    def block(self, kind, other=0):
        fz, fy, fx = FLIPS[kind]
        start = self.pl.chip(fz, other, fy, fx) * self.rows
        return self.full.at[pl.ds(pl.multiple_of(start, self.rows), self.rows)]

    def send(self, kind, way):
        place = self.pl
        if way == "s":
            dev, slot = place.sib, 8 + kind
        else:
            dev = {"x": place.xn, "y": place.yn, "z": place.zn}[way]
            fz, fy, fx = FLIPS[kind]
            flips = {"x": (fz, fy, 1 - fx), "y": (fz, 1 - fy, fx), "z": (1 - fz, fy, fx)}[way]
            slot = FLIPS.index(flips)
        view = self.block(kind)
        return rcopy(view, view, self.ssem.at[slot], self.rsem.at[slot], dev)

    AFTER = {
        OWN: "zxys",
        ZB: "xys",
        X0: "ys",
        X1: "s",
        Y0: "s",
        Y1: "xs",
        D0: "s",
        D1: "s",
    }

    def start(self, kind):
        for way in self.AFTER[kind]:
            self.send(kind, way).start()

    def arrived(self, kind, other=0):
        view = self.block(kind, other)
        slot = kind + 8 * other
        rcopy(view, view, self.ssem.at[slot], self.rsem.at[slot], self.pl.sib).wait_recv()

    def finish(self):
        for kind in range(8):
            for way in self.AFTER[kind]:
                self.send(kind, way).wait_send()


def hand_in(place, shard, spot, c_rows, ssem, rsem, go):
    mine, theirs = shard.at[place.m], shard.at[1 - place.m]
    here = lambda: pltpu.make_async_copy(mine, spot(place.c), rsem.at[place.c])
    to_sib = lambda: rcopy(mine, spot(place.c), ssem.at[0], rsem.at[place.c], place.sib)
    to_pair = lambda: rcopy(theirs, spot(place.c), ssem.at[1], rsem.at[place.c], place.pair)
    to_cross = lambda: rcopy(theirs, spot(place.c), ssem.at[1], rsem.at[place.c], place.cross)
    if go == "start":

        @pl.when(place.c == place.m)
        def _():
            here().start()
            to_pair().start()

        @pl.when(place.c != place.m)
        def _():
            to_sib().start()
            to_cross().start()

    elif go == "recv":
        for piece in range(2):
            dst = spot(piece)
            rcopy(dst, dst, ssem.at[1], rsem.at[piece], place.sib).wait_recv()
    else:

        @pl.when(place.c != place.m)
        def _():
            to_sib().wait_send()

        to_pair().wait_send()


def dot(a, b, ca, cb):
    return lax.dot_general(a, b, (((ca,), (cb,)), ((), ())), preferred_element_type=F32)


def chunks(count, step, body):
    @pl.loop(0, count // step)
    def _(i):
        body(pl.ds(pl.multiple_of(i * step, step), step))


def norm(v):
    center = v - jnp.mean(v, axis=-1, keepdims=True)
    r = lax.rsqrt(jnp.mean(center * center, axis=-1, keepdims=True) + 1e-06)
    return center * r, r


def fill_distance(dist, lay):
    across = lay[...]
    down = across.T
    gap_r = down[:, 1:2] - across[1:2]
    gap_c = down[:, 2:3] - across[2:3]
    far = jnp.sqrt(gap_r * gap_r + gap_c * gap_c)
    dist[...] = jnp.where(down[:, 0:1] == across[0:1], far, FAR)


def lanes(half):
    return lax.broadcasted_iota(jnp.int32, (1, 128), 1) // 64 == half


def slope_of(head):
    return jnp.exp2(jnp.full((1, 1), -8.0 / HEADS, F32) * (head + 1).astype(F32))


def attend_pair(qkv, rows, dist, j, prob, slot, o, d):
    col = pl.multiple_of(j * 128, 128)
    q = qkv[rows, pl.ds(col, 128)] * jnp.asarray(0.125, BF)
    k = qkv[rows, pl.ds(d + col, 128)]
    v = qkv[rows, pl.ds(2 * d + col, 128)]
    zero = jnp.zeros((), BF)
    total = None
    for half in range(2):
        keep = lanes(half)
        s = dot(k, jnp.where(keep, q, zero), 1, 1) - slope_of(2 * j + half) * dist
        e = jnp.exp(s - jnp.max(s, axis=0, keepdims=True))
        p = (e * (1.0 / jnp.sum(e, axis=0, keepdims=True))).astype(BF)
        prob[slot + half] = p
        part = dot(jnp.where(keep, v, zero), p, 0, 0)
        total = part if total is None else total + part
    o[rows, pl.ds(col, 128)] = total.T.astype(BF)


def forward_kernel(spread, *refs):
    (pat, dog, lay, wq, wp, w1, w2, sm) = refs[:8]
    (x_o, dog_o, lay_o, wq_o, wp_o, w1_o, w2_o, vec_o, b1_o) = refs[8:17]
    (qkv_o, p_o, o_o, y1_o, c_o, g_o, gs_o, enc_o) = refs[17:25]
    (fq, fp, f1, f2, fs, gq, gp, g1) = refs[25:33]
    (lays, dist, xb, ac, qkv, prob, ob, y1, g, gs) = refs[33:43]
    (hs, hr, ss, rs, as_, ar, ls, ps) = refs[43:]
    place = Place(spread)
    d = xb.shape[2]
    n = xb.shape[1]
    place.greet()
    hand = ((sm, fs, None, 16), (wq, fq, gq, 24), (wp, fp, gp, 24), (w1, f1, g1, 24))
    hand += ((w2, f2, None, w2.shape[1]),)
    gathers = [
        Gather(place, full, 2 * rows, ss.at[k], rs.at[k])
        for k, (_, full, _, rows) in enumerate(hand)
    ]

    def spot_of(k):
        _, full, stage, rows = hand[k]
        if stage is not None:
            return lambda piece: stage.at[piece]
        own = place.chip(0, 0, 0, 0) * 2

        def spot(piece):
            place_of = place.p if piece is place.c else own + piece
            return full.at[pl.ds(pl.multiple_of(place_of * rows, 16), rows)]

        return spot

    def hand_over(k, go):
        hand_in(place, hand[k][0], spot_of(k), hand[k][3], hs.at[k], hr.at[k], go)

    def own_ready(k):
        hand_over(k, "recv")
        _, full, stage, rows = hand[k]
        if stage is not None:
            both = jnp.concatenate([stage[0].astype(F32), stage[1].astype(F32)], axis=0)
            start = pl.multiple_of(place.chip(0, 0, 0, 0) * (2 * rows), 2 * rows)
            full[pl.ds(start, 2 * rows), :] = both.astype(BF)
        gathers[k].start(OWN)

    def pump(k, *kinds):
        for kind in kinds:
            gathers[k].arrived(kind)
            gathers[k].start(kind)

    def whole(k):
        for kind in range(8):
            gathers[k].arrived(kind, 1)

    saves = []

    def save(src, dst):
        copy = pltpu.make_async_copy(src, dst, ls.at[len(saves)])
        copy.start()
        saves.append(copy)

    acts = [
        rcopy(pat.at[1 - place.m], xb.at[1], as_.at[0], ar.at[0], place.pair),
        rcopy(lay, lays.at[1], as_.at[2], ar.at[2], place.pair),
        rcopy(dog.at[1 - place.m], dog_o, as_.at[1], ar.at[1], place.pair),
    ]
    own_x = pltpu.make_async_copy(pat.at[place.m], xb.at[0], ps.at[0])
    own_lay = pltpu.make_async_copy(lay, lays.at[0], ps.at[1])
    for k in range(3):
        hand_over(k, "start")
    own_lay.start()
    own_x.start()
    own_lay.wait()
    fill_distance(dist.at[0], lays.at[0])
    for k in range(3):
        own_ready(k)
    hand_over(3, "start")
    acts[1].start()
    acts[0].start()
    hand_over(4, "start")
    pump(0, ZB, X0, Y0, X1, Y1, D0, D1)
    own_ready(3)
    pump(1, ZB, X0, Y0, X1, Y1, D0, D1)
    own_ready(4)
    acts[2].start()
    whole(0)
    seg = d // RING
    hid = w2.shape[1]
    for q in range(RING):
        tile = fs[16 * q : 16 * q + 16].astype(F32)
        vec_o[0:8, seg * q : seg * q + seg] = tile[0:8, 0:seg]
        b1_o[0:1, hid * q : hid * q + hid] = tile[6:7, 0:hid]
    own_x.wait()

    def first_norm(grp):
        def body(rows):
            nhat, _ = norm(xb[grp, rows, :].astype(F32))
            here = pl.ds(pl.multiple_of(grp * n + rows.start, 128), 128)
            ac[here, :] = (nhat * vec_o[0:1] + vec_o[1:2]).astype(BF)

        chunks(n, 128, body)

    first_norm(0)
    whole(1)
    save(fq, wq_o)
    qkv[0:n] = dot(ac[0:n], fq[...], 1, 0).astype(BF)
    acts[1].wait_recv()
    fill_distance(dist.at[1], lays.at[1])
    acts[0].wait_recv()
    first_norm(1)
    qkv[n : 2 * n] = dot(ac[n : 2 * n], fq[...], 1, 0).astype(BF)
    save(qkv, qkv_o)
    save(xb.at[1], x_o)
    save(lays.at[1], lay_o)
    pairs = HEADS // 2
    early = {
        0: [(2, ZB, X0, Y0)],
        1: [(2, X1, Y1)],
        2: [(2, D0, D1)],
        3: [(3, ZB, X0, Y0)],
        5: [(3, X1, Y1)],
        7: [(3, D0, D1)],
        9: [(4, X0, Y0)],
        10: [(4, ZB)],
    }

    @pl.loop(0, 2 * pairs)
    def _(i):
        grp, j = i // pairs, lax.rem(i, pairs)
        rows = pl.ds(pl.multiple_of(grp * n, n), n)
        attend_pair(qkv, rows, dist[grp], j, prob, 2 * i, ob, d)
        pltpu.make_async_copy(
            prob.at[pl.ds(2 * i, 2)], p_o.at[pl.ds(2 * i, 2)], ps.at[2 + i]
        ).start()
        for at, steps in early.items():

            @pl.when(i == at)
            def _(steps=steps):
                for step in steps:
                    pump(*step)

    save(ob, o_o)
    whole(2)
    save(fp, wp_o)

    def second_norm(rows):
        first = (
            xb[rows.start // n, pl.ds(pl.multiple_of(lax.rem(rows.start, n), 256), 256), :].astype(F32)
            + dot(ob[rows, :], fp[...], 1, 0)
            + vec_o[2:3]
        )
        y1[rows, :] = first
        nhat, _ = norm(first)
        ac[rows, :] = (nhat * vec_o[3:4] + vec_o[4:5]).astype(BF)

    chunks(2 * n, 256, second_norm)
    save(y1, y1_o)
    save(ac, c_o)
    pump(4, X1, Y1)
    whole(3)
    save(f1, w1_o)

    def hidden(cols):
        u = dot(ac[...], f1[:, cols], 1, 0) + b1_o[0:1, cols]
        phi = 0.5 + 0.5 * lax.erf(u * 0.7071067811865476)
        g[:, cols] = (u * phi).astype(BF)
        gs[:, cols] = (phi + u * (0.3989422804014327 * jnp.exp(-0.5 * u * u))).astype(BF)

    chunks(g.shape[1], 256, hidden)
    save(g, g_o)
    save(gs, gs_o)
    pump(4, D0, D1)
    whole(4)
    save(f2, w2_o)

    def result(rows):
        ac_rows = y1[rows, :] + dot(g[rows, :], f2[...], 1, 0) + vec_o[5:6]
        qkv[rows, 0:d] = ac_rows.astype(BF)

    saves[1].wait()
    chunks(2 * n, 512, result)
    save(qkv.at[:, pl.ds(0, d)], enc_o)
    for k in range(5):
        hand_over(k, "send")
        gathers[k].finish()
    acts[0].wait_send()
    acts[1].wait_send()
    acts[2].wait()
    for i in range(2 * pairs):
        pltpu.make_async_copy(
            prob.at[pl.ds(2 * i, 2)], p_o.at[pl.ds(2 * i, 2)], ps.at[2 + i]
        ).wait()
    for k, copy in enumerate(saves):
        if k != 1:
            copy.wait()


def forward(spread, pat, dog, lay, wq, wp, w1, w2, sm):
    any_, vm = pl.BlockSpec(memory_space=pl.ANY), pl.BlockSpec(memory_space=pltpu.VMEM)
    n, d = pat.shape[1:]
    ff = w2.shape[1] * RING
    sd = jax.ShapeDtypeStruct
    out = [
        sd((n, d), BF),
        sd((n, d), BF),
        sd(lay.shape, F32),
        sd((d, wq.shape[2]), BF),
        sd((d, d), BF),
        sd((d, ff), BF),
        sd((ff, d), BF),
        sd((8, d), F32),
        sd((8, ff), F32),
        sd((2 * n, wq.shape[2]), BF),
        sd((2 * HEADS, n, n), BF),
        sd((2 * n, d), BF),
        sd((2 * n, d), F32),
        sd((2 * n, d), BF),
        sd((2 * n, ff), BF),
        sd((2 * n, ff), BF),
        sd((2 * n, d), BF),
    ]
    dma = pltpu.SemaphoreType.DMA
    vmem = pltpu.VMEM
    return pl.pallas_call(
        functools.partial(forward_kernel, spread),
        out_shape=out,
        in_specs=[any_] * 8,
        out_specs=[any_] * 7 + [vm] * 2 + [any_] * 8,
        scratch_shapes=[
            vmem((d, wq.shape[2]), BF),
            vmem((d, d), BF),
            vmem((d, ff), BF),
            vmem((ff, d), BF),
            vmem((RING * 16, 128), BF),
            vmem((2, 24, wq.shape[2]), BF),
            vmem((2, 24, d), BF),
            vmem((2, 24, ff), BF),
            vmem((2,) + lay.shape, F32),
            vmem((2, n, n), F32),
            vmem((2, n, d), BF),
            vmem((2 * n, d), BF),
            vmem((2 * n, wq.shape[2]), BF),
            vmem((2 * HEADS, n, n), BF),
            vmem((2 * n, d), BF),
            vmem((2 * n, d), F32),
            vmem((2 * n, ff), BF),
            vmem((2 * n, ff), BF),
            dma((5, 2)),
            dma((5, 2)),
            dma((5, 16)),
            dma((5, 16)),
            dma((3,)),
            dma((3,)),
            dma((16,)),
            dma((2 + HEADS,)),
        ],
        compiler_params=pltpu.CompilerParams(
            collective_id=0, has_side_effects=True, vmem_limit_bytes=62 * 2**20
        ),
        name="forward",
    )(pat, dog, lay, wq, wp, w1, w2, sm)


class Scatter:
    def __init__(self, place, full, rows, got_sib, got, ssem, rsem):
        self.pl, self.full, self.rows = place, full, rows
        self.got_sib, self.got, self.ssem, self.rsem = got_sib, got, ssem, rsem

    def start_of(self, kind):
        fz, fy, fx = FLIPS[kind]
        return pl.multiple_of(self.pl.chip(fz, 0, fy, fx) * self.rows, self.rows)

    def plane(self, z, other):
        c = 1 - self.pl.c if other else self.pl.c
        return pl.ds(pl.multiple_of((z * 2 + c) * (4 * self.rows), self.rows), 4 * self.rows)

    def sib(self, z):
        return rcopy(
            self.full.at[self.plane(z, 1)],
            self.got_sib.at[z],
            self.ssem.at[z],
            self.rsem.at[z],
            self.pl.sib,
        )

    MOVES = {D0: ("y", 0), D1: ("x", 1), X0: ("x", 2), X1: ("x", 3), Y0: ("y", 4), Y1: ("y", 5), ZB: ("z", 6)}

    def move(self, kind):
        way, slot = self.MOVES[kind]
        dev = {"x": self.pl.xn, "y": self.pl.yn, "z": self.pl.zn}[way]
        return rcopy(
            self.full.at[pl.ds(self.start_of(kind), self.rows)],
            self.got.at[slot],
            self.ssem.at[2 + slot],
            self.rsem.at[2 + slot],
            dev,
        )

    def add(self, kind, slots):
        rows = pl.ds(self.start_of(kind), self.rows)
        total = self.full[rows, :].astype(F32)
        for slot in slots:
            total = total + self.got[slot].astype(F32)
        self.full[rows, :] = total.astype(BF)

    def begin(self):
        self.sib(0).start()
        self.sib(1).start()

    def second(self):
        for z in range(2):
            self.sib(z).wait()
        step = 16

        for z in range(2):
            base = (z * 2 + self.pl.c) * (4 * self.rows)

            @pl.loop(0, 4 * self.rows // step)
            def _(i, z=z, base=base):
                rows = pl.ds(pl.multiple_of(base + i * step, step), step)
                theirs = self.got_sib[z, pl.ds(pl.multiple_of(i * step, step), step), :]
                self.full[rows, :] = (self.full[rows, :].astype(F32) + theirs.astype(F32)).astype(BF)

        for kind in (D0, D1, X1, Y0):
            self.move(kind).start()

    def third(self):
        self.move(D0).wait()
        self.add(X0, (0,))
        self.move(X0).start()
        self.move(D1).wait()
        self.add(Y1, (1,))
        self.move(Y1).start()

    def fourth(self):
        self.move(X1).wait()
        self.move(Y1).wait()
        self.add(ZB, (3, 5))
        self.move(ZB).start()

    def total(self):
        self.move(X0).wait()
        self.move(Y0).wait()
        self.move(ZB).wait()
        rows = pl.ds(self.start_of(OWN), self.rows)
        total = self.full[rows, :].astype(F32)
        for slot in (2, 4, 6):
            total = total + self.got[slot].astype(F32)
        return total


def hand_back(place, stage, out, ssem, rsem, go):
    if go == "start":

        @pl.when(place.c == place.m)
        def _():
            pltpu.make_async_copy(stage.at[place.c], out.at[place.m], rsem.at[place.m]).start()
            rcopy(
                stage.at[1 - place.c], out.at[place.m], ssem.at[0], rsem.at[place.m], place.sib
            ).start()

        @pl.when(place.c != place.m)
        def _():
            rcopy(
                stage.at[place.c], out.at[place.m], ssem.at[0], rsem.at[place.m], place.pair
            ).start()
            rcopy(
                stage.at[1 - place.c], out.at[place.m], ssem.at[1], rsem.at[place.m], place.cross
            ).start()

    elif go == "recv":
        for k in range(2):
            rcopy(out.at[k], out.at[k], ssem.at[0], rsem.at[k], place.sib).wait_recv()
    else:
        rcopy(stage.at[0], out.at[0], ssem.at[0], rsem.at[0], place.sib).wait_send()

        @pl.when(place.c != place.m)
        def _():
            rcopy(stage.at[0], out.at[0], ssem.at[1], rsem.at[0], place.sib).wait_send()


def unnorm(dn, nhat, r, gain):
    dh = dn * gain
    return r * (
        dh - jnp.mean(dh, axis=-1, keepdims=True) - nhat * jnp.mean(dh * nhat, axis=-1, keepdims=True)
    )


def attend_back(qkv, rows, probs, do, o, j, d):
    col = pl.multiple_of(j * 128, 128)
    eighth = jnp.asarray(0.125, BF)
    zero = jnp.zeros((), BF)
    q = qkv[rows, pl.ds(col, 128)]
    k = qkv[rows, pl.ds(d + col, 128)]
    v = qkv[rows, pl.ds(2 * d + col, 128)]
    g = do[rows, pl.ds(col, 128)]
    both = g.astype(F32) * o[rows, pl.ds(col, 128)].astype(F32)
    dq = dk = dv = 0.0
    for half in range(2):
        keep = lanes(half)
        p = probs[half]
        gm = jnp.where(keep, g, zero)
        centre = jnp.sum(jnp.where(keep, both, 0.0), axis=1, keepdims=True)
        centre = jnp.broadcast_to(centre, (both.shape[0], 128)).T[0:1]
        ds = (p.astype(F32) * (dot(v, gm, 1, 1) - centre)).astype(BF)
        dk = dk + dot(ds, jnp.where(keep, q * eighth, zero), 1, 0)
        dv = dv + dot(p, gm, 1, 0)
        dq = dq + dot(jnp.where(keep, k * eighth, zero), ds, 0, 0)
    qkv[rows, pl.ds(col, 128)] = dq.T.astype(BF)
    qkv[rows, pl.ds(d + col, 128)] = dk.astype(BF)
    qkv[rows, pl.ds(2 * d + col, 128)] = dv.astype(BF)


def backward_kernel(spread, *refs):
    (pat, dog, lay, x_i, dog_i, lay_i, wq_i, wp_i, w1_i, w2_i, vec) = refs[:11]
    (qkv_i, p_i, o_i, y1_i, c_i, g_i, gs_i, y_i) = refs[11:19]
    (oq, op, o1, o2, os_, enc_o, pg_o) = refs[19:26]
    (w2, w1, wp, qkv, g, du, c, ob, dz, y1, do, g2, gp, lays, sums) = refs[26:41]
    got_sib, got, stages = refs[41:45], refs[45:49], refs[49:53]
    (sgot, ss, rs, hs, hr, es, er, ts, tr, ls, ps) = refs[53:]
    place = Place(spread)
    n, d = c.shape[0] // 2, c.shape[1]
    ff = w1.shape[1]
    wide = qkv.shape[1]
    loads = []

    def load(src, dst):
        copy = pltpu.make_async_copy(src, dst, ls.at[len(loads)])
        copy.start()
        loads.append(copy)
        return copy

    lay_l = (load(lay, lays.at[0]), load(lay_i, lays.at[1]))
    dz_l = (
        load(dog.at[place.m], dz.at[pl.ds(0, n)]),
        load(dog_i, dz.at[pl.ds(n, n)]),
    )
    g_l = load(g_i, g)
    w2_l = load(w2_i, w2)
    du_l = load(gs_i, du)
    c_l = load(c_i, c)
    w1_l = load(w1_i, w1)
    y1_l = load(y1_i, y1)
    o_l = load(o_i, ob)
    wp_l = load(wp_i, wp)
    qkv_l = load(qkv_i, qkv)
    place.greet()
    acts = [
        rcopy(y_i.at[pl.ds(n, n)], enc_o.at[place.m], es.at[0], er.at[0], place.pair),
        rcopy(c.at[pl.ds(n, n)], pg_o.at[place.m], es.at[1], er.at[1], place.pair),
    ]
    enc_l = load(y_i.at[pl.ds(0, n)], enc_o.at[place.m])
    acts[0].start()
    gq = du.at[pl.ds(0, d), pl.ds(0, wide)]
    g1 = g.at[pl.ds(0, d)]
    fulls = (gq, gp, g1, g2)
    outs = (oq, op, o1, o2)
    rows_of = (48, 48, 48, ff // 16)
    sc = [
        Scatter(place, fulls[k], rows_of[k], got_sib[k], got[k], ss.at[k], rs.at[k])
        for k in range(4)
    ]

    def close(k):
        total = sc[k].total()
        half = rows_of[k] // 2
        stages[k][0] = total[:half].astype(BF)
        stages[k][1] = total[half:].astype(BF)
        hand_back(place, stages[k], outs[k], hs.at[k], hr.at[k], "start")

    QK, PR, W1, W2 = range(4)
    sums[...] = jnp.zeros_like(sums)

    def add_sum(row, v):
        sums[row : row + 1] += jnp.sum(v, axis=0, keepdims=True)

    for copy in (*lay_l, *dz_l):
        copy.wait()
    for grp in range(2):
        live = lays[grp].T[:, 3:4]

        for part in range(4):
            rows = pl.ds(grp * n + part * (n // 4), n // 4)
            keep = live[part * (n // 4) : (part + 1) * (n // 4)]
            v = dz[rows, :].astype(F32) * keep
            dz[rows, :] = v.astype(BF)
            add_sum(5, v)
    g_l.wait()

    @pl.loop(0, 4)
    def _(i):
        z, other = lax.rem(i, 2), 1 - i // 2
        start = (z * 2 + jnp.where(other == 1, 1 - place.c, place.c)) * (ff // 4)
        cols = pl.ds(pl.multiple_of(start, 128), ff // 4)
        g2[cols, :] = dot(g[:, cols], dz[...], 0, 0).astype(BF)

        @pl.when(i == 1)
        def _():
            sc[W2].begin()

    w2_l.wait()
    du_l.wait()

    def hidden(cols):
        v = dot(dz[...], w2[cols, :], 1, 1) * du[:, cols].astype(F32)
        r = v.astype(BF)
        du[:, cols] = r
        line = jnp.sum(r.astype(F32), axis=0, keepdims=True)
        sums[pl.ds(6 + cols.start // d, 1), pl.ds(pl.multiple_of(lax.rem(cols.start, d), 128), 256)] = line

    chunks(ff, 256, hidden)
    sc[W2].second()
    pairs = HEADS // 2

    def fetch(i):
        src = lax.rem(i + pairs, 2 * pairs) * 2
        slot = lax.rem(i, 3)
        for half in range(2):
            yield pltpu.make_async_copy(
                p_i.at[src + half],
                w2.at[pl.ds(pl.multiple_of((slot * 2 + half) * n, n), n), pl.ds(0, n)],
                ps.at[slot, half],
            )

    for i in range(3):
        for copy in fetch(i):
            copy.start()
    c_l.wait()

    def up_grad(cols):
        g1[:, cols] = dot(c[...], du[:, cols], 0, 0).astype(BF)

    chunks(ff, 768, up_grad)
    sc[W1].begin()
    sc[W2].third()
    w1_l.wait()
    y1_l.wait()

    def second_norm(rows):
        dc = dot(du[rows, :], w1[...], 1, 1)
        nhat, r = norm(y1[rows, :])
        add_sum(3, dc * nhat)
        add_sum(4, dc)
        first = dz[rows, :].astype(F32) + unnorm(dc, nhat, r, vec[3:4])
        y1[rows, :] = first
        low = first.astype(BF)
        c[rows, :] = low
        add_sum(2, low.astype(F32))

    def span(start, count, step, body):
        chunks(count, step, lambda s: body(pl.ds(pl.multiple_of(start + s.start, step), step)))

    span(0, n, 256, second_norm)
    sc[W1].second()
    span(n, n, 256, second_norm)
    wq_l = load(wq_i, w1.at[:, pl.ds(0, wide)])
    sc[W2].fourth()
    o_l.wait()
    wp_l.wait()
    gp[...] = dot(ob[...], c[...], 0, 0).astype(BF)
    sc[PR].begin()
    do[...] = dot(c[...], wp[...], 1, 1).astype(BF)
    x_l = (load(pat.at[place.m], c.at[pl.ds(0, n)]), load(x_i, c.at[pl.ds(n, n)]))
    sc[W1].third()
    for copy in x_l:
        copy.wait()

    def first_norm(rows):
        nhat, _ = norm(c[rows, :].astype(F32))
        dz[rows, :] = (nhat * vec[0:1] + vec[1:2]).astype(BF)

    chunks(2 * n, 256, first_norm)
    qkv_l.wait()
    work = {
        0: lambda: sc[PR].second(),
        1: lambda: close(W2),
        3: lambda: sc[PR].third(),
        4: lambda: sc[W1].fourth(),
        7: lambda: sc[PR].fourth(),
        8: lambda: close(W1),
        10: lambda: close(PR),
    }

    def attention(start):
        @pl.loop(start, start + pairs)
        def _(i):
            j = lax.rem(i, pairs)
            grp = 1 - i // pairs
            rows = pl.ds(pl.multiple_of(grp * n, n), n)
            for copy in fetch(i):
                copy.wait()
            slot = lax.rem(i, 3)
            probs = [
                w2.at[pl.ds(pl.multiple_of((slot * 2 + half) * n, n), n), pl.ds(0, n)]
                for half in range(2)
            ]
            attend_back(qkv, rows, [p[...] for p in probs], do, ob, j, d)

            @pl.when(i + 3 < 2 * pairs)
            def _():
                for copy in fetch(i + 3):
                    copy.start()

            for at, step in work.items():
                if start <= at < start + pairs:

                    @pl.when(i == at)
                    def _(step=step):
                        step()

    def input_grad(rows):
        da = dot(qkv[rows, :], w1[:, pl.ds(0, wide)], 1, 1)
        nhat, r = norm(c[rows, :].astype(F32))
        add_sum(0, da * nhat)
        add_sum(1, da)
        c[rows, :] = (y1[rows, :] + unnorm(da, nhat, r, vec[0:1])).astype(BF)

    attention(0)
    wq_l.wait()
    span(n, n, 256, input_grad)
    acts[1].start()
    attention(pairs)

    def qkv_grad(cols):
        gq[:, cols] = dot(dz[...], qkv[:, cols], 0, 0).astype(BF)

    chunks(wide, 768, qkv_grad)
    sc[QK].begin()
    span(0, n, 256, input_grad)
    pg_l = load(c.at[pl.ds(0, n)], pg_o.at[place.m])
    os_[place.m] = sums[...]
    hops = (place.sib, place.xn, place.yn, place.zn)

    def hop(i):
        return rcopy(os_.at[place.m], sgot.at[i], ts.at[i], tr.at[i], hops[i])

    def landed(i):
        hop(i).wait()
        os_[place.m] = os_[place.m] + sgot[i]

    hop(0).start()
    sc[QK].second()
    landed(0)
    hop(1).start()
    sc[QK].third()
    landed(1)
    hop(2).start()
    sc[QK].fourth()
    landed(2)
    hop(3).start()
    close(QK)
    landed(3)
    last = rcopy(os_.at[place.m], os_.at[place.m], ts.at[4], tr.at[4], place.pair)
    last.start()
    for k in (W2, W1, PR, QK):
        hand_back(place, stages[k], outs[k], hs.at[k], hr.at[k], "recv")
        hand_back(place, stages[k], outs[k], hs.at[k], hr.at[k], "send")
    last.wait_send()
    theirs = os_.at[1 - place.m]
    rcopy(theirs, theirs, ts.at[4], tr.at[4], place.pair).wait_recv()
    for act in acts:
        act.wait()
    enc_l.wait()
    pg_l.wait()


def backward(spread, pat, dog, lay, *kept):
    any_, vm = pl.BlockSpec(memory_space=pl.ANY), pl.BlockSpec(memory_space=pltpu.VMEM)
    n, d = pat.shape[1:]
    wide, ff = kept[3].shape[1], kept[5].shape[1]
    shapes = ((48, wide), (48, d), (48, ff), (ff // 16, d))
    sd = jax.ShapeDtypeStruct
    out = [sd((2, r // 2, k), BF) for r, k in shapes]
    out += [sd((2, 16, d), F32), sd((2, n, d), BF), sd((2, n, d), BF)]
    dma = pltpu.SemaphoreType.DMA
    vmem = pltpu.VMEM
    return pl.pallas_call(
        functools.partial(backward_kernel, spread),
        out_shape=out,
        in_specs=[any_] * 10 + [vm] + [any_] * 8,
        out_specs=[any_] * 4 + [vm] + [any_] * 2,
        scratch_shapes=[
            vmem((ff, d), BF),
            vmem((d, ff), BF),
            vmem((d, d), BF),
            vmem((2 * n, wide), BF),
            vmem((2 * n, ff), BF),
            vmem((2 * n, ff), BF),
            vmem((2 * n, d), BF),
            vmem((2 * n, d), BF),
            vmem((2 * n, d), BF),
            vmem((2 * n, d), F32),
            vmem((2 * n, d), BF),
            vmem((ff, d), BF),
            vmem((d, d), BF),
            vmem((2,) + lay.shape, F32),
            vmem((16, d), F32),
        ]
        + [vmem((2, 4 * r, k), BF) for r, k in shapes]
        + [vmem((7, r, k), BF) for r, k in shapes]
        + [vmem((2, r // 2, k), BF) for r, k in shapes]
        + [
            vmem((4, 16, d), F32),
            dma((4, 9)),
            dma((4, 9)),
            dma((4, 2)),
            dma((4, 2)),
            dma((2,)),
            dma((2,)),
            dma((5,)),
            dma((5,)),
            dma((18,)),
            dma((3, 2)),
        ],
        compiler_params=pltpu.CompilerParams(
            collective_id=1, has_side_effects=True, vmem_limit_bytes=62 * 2**20
        ),
        name="backward",
    )(pat, dog, lay, *kept)


def small_pack(parts, b1):
    rows = jnp.stack([jnp.pad(v, ((0, 0), (0, 128 - v.shape[1]))) for v in (*parts, b1)], axis=1)
    return jnp.pad(rows, ((0, 0), (0, 16 - rows.shape[1]), (0, 0)))


def local(
    count, patches, tile_kind, out_grad, n1g, n1b, wq, wp, bp, n2g, n2b, w1, b1, w2, b2
):
    spread = count // RING
    idx = lax.axis_index("fsdp")
    p = idx // spread
    rows, d = patches.shape[1:]
    parts = (n1g, n1b, bp, n2g, n2b, b2)
    if spread > 1:
        groups = [[q * spread + j for j in range(spread)] for q in range(RING)]
        ag = functools.partial(
            lax.all_gather, axis_name="fsdp", axis=1, tiled=True, axis_index_groups=groups
        )
        wq, wp, w1, w2, b1 = ag(wq), ag(wp), ag(w1), ag(w2), ag(b1)
        parts = tuple(ag(v) for v in parts)
    lay = jnp.stack([v.astype(F32) for v in packing(tile_kind, rows)])
    lay = jnp.pad(lay, ((0, 4), (0, 0)))
    sm = small_pack(parts, b1)
    pat2, dog2, lay2, fq, fp, f1, f2, vecs, _, *saved = forward(
        spread, patches, out_grad, lay, wq, wp, w1, w2, sm
    )
    oq, op, o1, o2, os_, encoded, pgrad = backward(
        spread, patches, out_grad, lay, pat2, dog2, lay2, fq, fp, f1, f2, vecs, *saved
    )
    pgrad = pgrad.astype(F32)
    seg = d // RING
    vec = lax.dynamic_slice_in_dim(os_[:, :6], p * seg, seg, axis=2)
    hid = os_[:, 6 : 6 + w2.shape[1] * RING // d].reshape(2, -1)
    hid = lax.dynamic_slice_in_dim(hid, p * w2.shape[1], w2.shape[1], axis=1)
    grads = [oq.astype(F32), op.astype(F32), o1.astype(F32), o2.astype(F32)]
    if spread > 1:
        rs = functools.partial(
            lax.psum_scatter, axis_name="fsdp", tiled=True, axis_index_groups=groups
        )
        grads = [rs(v, scatter_dimension=1) for v in grads]
        vec, hid = rs(vec, scatter_dimension=2), rs(hid, scatter_dimension=1)
    return (
        encoded,
        pgrad,
        vec[:, 0],
        vec[:, 1],
        grads[0],
        grads[1],
        vec[:, 2],
        vec[:, 3],
        vec[:, 4],
        grads[2],
        hid,
        grads[3],
        vec[:, 5],
    )


def solution(mesh):
    three, two = P(None, "fsdp", None), P(None, "fsdp")
    in_specs = (three, P("fsdp"), three, two, two, three, three, two, two, two, three, two, three, two)
    out_specs = (three, three, two, two, three, three, two, two, two, three, two, three, two)
    return jax.shard_map(
        functools.partial(local, mesh.shape["fsdp"]),
        mesh=mesh,
        in_specs=in_specs,
        out_specs=out_specs,
        check_vma=False,
    )
```

```python
import functools

import jax
import jax.numpy as jnp
from jax import lax
from jax.experimental import pallas as pl
from jax.experimental.pallas import tpu as pltpu
from jax.sharding import PartitionSpec as P

HEADS = 12
SIDE_S = 12
SIDE_M = 15
SIDE_L = 20
RING = 32
MESH = pl.DeviceIdType.MESH
BF = jnp.bfloat16
F32 = jnp.float32
FAR = 1e33


def packing(kind_ids, row_count):
    slot_count = kind_ids.shape[0]
    sides = jnp.where(kind_ids == 0, SIDE_S, jnp.where(kind_ids == 1, SIDE_M, SIDE_L)).astype(
        jnp.int32
    )
    lengths = sides * sides
    slots = jnp.arange(slot_count, dtype=jnp.int32)
    ends = jnp.sum(jnp.where(slots[None, :] <= slots[:, None], lengths[None, :], 0), axis=1)
    starts = ends - lengths
    places = jnp.arange(row_count, dtype=jnp.int32)
    inside = (
        (ends <= row_count)[None, :]
        & (places[:, None] >= starts[None, :])
        & (places[:, None] < ends[None, :])
    ).astype(jnp.int32)
    filled = jnp.sum(inside, axis=1)
    segment = jnp.sum(inside * slots[None, :], axis=1) + (1 - filled) * (slot_count + places)
    offset = places - jnp.sum(inside * starts[None, :], axis=1)
    side = jnp.sum(inside * sides[None, :], axis=1) + (1 - filled)
    return segment, offset // side, offset % side, filled


class Place:
    def __init__(self, spread):
        me = lax.axis_index("fsdp")
        rest = lax.rem(me, spread)
        p = me // spread
        self.p = p
        self.c = lax.rem(p, 2)
        self.x = lax.rem(p // 2, 2)
        self.y = lax.rem(p // 4, 2)
        self.m = lax.rem(p // 8, 2)
        self.z = lax.rem(p // 16, 2)
        dev = lambda q: (q * spread + rest,)
        sib = p + 1 - 2 * self.c
        pair = p + 8 * (1 - 2 * self.m)
        self.sib = dev(sib)
        self.xn = dev(p + 2 * (1 - 2 * self.x))
        self.yn = dev(p + 4 * (1 - 2 * self.y))
        self.zn = dev(p + 16 * (1 - 2 * self.z))
        self.pair = dev(pair)
        self.cross = dev(pair + 1 - 2 * self.c)

    def chip(self, fz, fc, fy, fx):
        flip = lambda v, f: 1 - v if f else v
        return (
            (flip(self.z, fz) * 2 + flip(self.c, fc)) * 2 + flip(self.y, fy)
        ) * 2 + flip(self.x, fx)

    def greet(self):
        barrier = pltpu.get_barrier_semaphore()
        everyone = (self.sib, self.xn, self.yn, self.zn, self.pair, self.cross)
        for other in everyone:
            pl.semaphore_signal(barrier, inc=1, device_id=other, device_id_type=MESH)
        pl.semaphore_wait(barrier, len(everyone))


OWN, ZB, X0, X1, Y0, Y1, D0, D1 = range(8)
FLIPS = ((0, 0, 0), (1, 0, 0), (0, 0, 1), (1, 0, 1), (0, 1, 0), (1, 1, 0), (0, 1, 1), (1, 1, 1))


def rcopy(src, dst, ssem, rsem, dev):
    return pltpu.make_async_remote_copy(
        src_ref=src, dst_ref=dst, send_sem=ssem, recv_sem=rsem, device_id=dev, device_id_type=MESH
    )


class Gather:
    def __init__(self, place, full, rows, ssem, rsem):
        self.pl, self.full, self.rows, self.ssem, self.rsem = place, full, rows, ssem, rsem

    def block(self, kind, other=0):
        fz, fy, fx = FLIPS[kind]
        start = self.pl.chip(fz, other, fy, fx) * self.rows
        return self.full.at[pl.ds(pl.multiple_of(start, self.rows), self.rows)]

    def send(self, kind, way):
        place = self.pl
        if way == "s":
            dev, slot = place.sib, 8 + kind
        else:
            dev = {"x": place.xn, "y": place.yn, "z": place.zn}[way]
            fz, fy, fx = FLIPS[kind]
            flips = {"x": (fz, fy, 1 - fx), "y": (fz, 1 - fy, fx), "z": (1 - fz, fy, fx)}[way]
            slot = FLIPS.index(flips)
        view = self.block(kind)
        return rcopy(view, view, self.ssem.at[slot], self.rsem.at[slot], dev)

    AFTER = {
        OWN: "zxys",
        ZB: "xys",
        X0: "ys",
        X1: "s",
        Y0: "s",
        Y1: "xs",
        D0: "s",
        D1: "s",
    }

    def start(self, kind):
        for way in self.AFTER[kind]:
            self.send(kind, way).start()

    def arrived(self, kind, other=0):
        view = self.block(kind, other)
        slot = kind + 8 * other
        rcopy(view, view, self.ssem.at[slot], self.rsem.at[slot], self.pl.sib).wait_recv()

    def finish(self):
        for kind in range(8):
            for way in self.AFTER[kind]:
                self.send(kind, way).wait_send()


def hand_in(place, shard, spot, c_rows, ssem, rsem, go):
    mine, theirs = shard.at[place.m], shard.at[1 - place.m]
    here = lambda: pltpu.make_async_copy(mine, spot(place.c), rsem.at[place.c])
    to_sib = lambda: rcopy(mine, spot(place.c), ssem.at[0], rsem.at[place.c], place.sib)
    to_pair = lambda: rcopy(theirs, spot(place.c), ssem.at[1], rsem.at[place.c], place.pair)
    to_cross = lambda: rcopy(theirs, spot(place.c), ssem.at[1], rsem.at[place.c], place.cross)
    if go == "start":

        @pl.when(place.c == place.m)
        def _():
            here().start()
            to_pair().start()

        @pl.when(place.c != place.m)
        def _():
            to_sib().start()
            to_cross().start()

    elif go == "recv":
        for piece in range(2):
            dst = spot(piece)
            rcopy(dst, dst, ssem.at[1], rsem.at[piece], place.sib).wait_recv()
    else:

        @pl.when(place.c != place.m)
        def _():
            to_sib().wait_send()

        to_pair().wait_send()


def dot(a, b, ca, cb):
    return lax.dot_general(a, b, (((ca,), (cb,)), ((), ())), preferred_element_type=F32)


def chunks(count, step, body):
    @pl.loop(0, count // step)
    def _(i):
        body(pl.ds(pl.multiple_of(i * step, step), step))


def norm(v):
    center = v - jnp.mean(v, axis=-1, keepdims=True)
    r = lax.rsqrt(jnp.mean(center * center, axis=-1, keepdims=True) + 1e-06)
    return center * r, r


def fill_distance(dist, lay):
    across = lay[...]
    down = across.T
    gap_r = down[:, 1:2] - across[1:2]
    gap_c = down[:, 2:3] - across[2:3]
    far = jnp.sqrt(gap_r * gap_r + gap_c * gap_c)
    dist[...] = jnp.where(down[:, 0:1] == across[0:1], far, FAR)


def lanes(half):
    return lax.broadcasted_iota(jnp.int32, (1, 128), 1) // 64 == half


def slope_of(head):
    return jnp.exp2(jnp.full((1, 1), -8.0 / HEADS, F32) * (head + 1).astype(F32))


def head_columns(j, d):
    pairs = HEADS // 4
    base = (j // pairs) * (3 * d // 2) + lax.rem(j, pairs) * 128
    return [pl.ds(pl.multiple_of(base + part * (d // 2), 128), 128) for part in range(3)]


def attend_pair(qkv, rows, dist, j, prob, slot, o, d):
    col = pl.multiple_of(j * 128, 128)
    cq, ck, cv = head_columns(j, d)
    q = qkv[rows, cq] * jnp.asarray(0.125, BF)
    k = qkv[rows, ck]
    v = qkv[rows, cv]
    zero = jnp.zeros((), BF)
    total = None
    for half in range(2):
        keep = lanes(half)
        s = dot(k, jnp.where(keep, q, zero), 1, 1) - slope_of(2 * j + half) * dist
        e = jnp.exp(s - jnp.max(s, axis=0, keepdims=True))
        p = (e * (1.0 / jnp.sum(e, axis=0, keepdims=True))).astype(BF)
        prob[slot + half] = p
        part = dot(jnp.where(keep, v, zero), p, 0, 0)
        total = part if total is None else total + part
    o[rows, pl.ds(col, 128)] = total.T.astype(BF)


def forward_kernel(spread, *refs):
    (pat, dog, lay, wq, wp, w1, w2, sm) = refs[:8]
    (x_o, dog_o, lay_o, wq_o, wp_o, w1_o, w2_o, vec_o, b1_o) = refs[8:17]
    (qkv_o, p_o, o_o, y1_o, c_o, g_o, gs_o, enc_o) = refs[17:25]
    (fq, fp, f1, f2, fs, gq, gp, g1) = refs[25:33]
    (lays, dist, xb, ac, qkv, prob, ob, y1, g, gs) = refs[33:43]
    (hs, hr, ss, rs, as_, ar, ls, ps) = refs[43:]
    place = Place(spread)
    d = xb.shape[2]
    n = xb.shape[1]
    ff = g.shape[1]
    place.greet()
    hand = ((sm, fs, None, 16), (wq, fq, gq, 24), (wp, fp, gp, 24), (w1, f1, g1, 24))
    hand += ((w2, f2, None, w2.shape[1]),)
    SM, QA, QB, PR, UA, UB, DA, DB = range(8)
    half = 3 * d // 2
    cut = (
        (0, fs),
        (1, fq.at[:, pl.ds(0, half)]),
        (1, fq.at[:, pl.ds(half, half)]),
        (2, fp),
        (3, f1.at[:, pl.ds(0, ff // 2)]),
        (3, f1.at[:, pl.ds(ff // 2, ff // 2)]),
        (4, f2.at[:, pl.ds(0, d // 2)]),
        (4, f2.at[:, pl.ds(d // 2, d // 2)]),
    )
    pieces = [
        Gather(place, view, 2 * hand[k][3], ss.at[i], rs.at[i]) for i, (k, view) in enumerate(cut)
    ]

    def spot_of(k):
        _, full, stage, rows = hand[k]
        if stage is not None:
            return lambda piece: stage.at[piece]
        own = place.chip(0, 0, 0, 0) * 2

        def spot(piece):
            place_of = place.p if piece is place.c else own + piece
            return full.at[pl.ds(pl.multiple_of(place_of * rows, 16), rows)]

        return spot

    def hand_over(k, go):
        hand_in(place, hand[k][0], spot_of(k), hand[k][3], hs.at[k], hr.at[k], go)

    def own_ready(k):
        hand_over(k, "recv")
        _, full, stage, rows = hand[k]
        if stage is not None:
            start = pl.multiple_of(place.chip(0, 0, 0, 0) * (2 * rows), 2 * rows)

            def pack(src, dst):
                both = [stage[piece, :, src].astype(F32) for piece in range(2)]
                full[pl.ds(start, 2 * rows), dst] = jnp.concatenate(both, axis=0).astype(BF)

            if k == 1:
                for part in range(3):
                    for side in range(2):
                        pack(
                            pl.ds(part * d + side * (d // 2), d // 2),
                            pl.ds((side * 3 + part) * (d // 2), d // 2),
                        )
            else:
                pack(pl.ds(0, full.shape[1]), pl.ds(0, full.shape[1]))
        for i, (at, _) in enumerate(cut):
            if at == k:
                pieces[i].start(OWN)

    def pump(i, *kinds):
        for kind in kinds:
            pieces[i].arrived(kind)
            pieces[i].start(kind)

    def whole(i):
        for kind in range(8):
            pieces[i].arrived(kind, 1)

    saves = []

    def save(src, dst):
        copy = pltpu.make_async_copy(src, dst, ls.at[len(saves)])
        copy.start()
        saves.append(copy)
        return copy

    send_x = rcopy(pat.at[1 - place.m], xb.at[1], as_.at[0], ar.at[0], place.pair)
    send_dog = rcopy(dog.at[1 - place.m], dog_o, as_.at[1], ar.at[1], place.pair)
    send_lay = rcopy(lay, lays.at[1], as_.at[2], ar.at[2], place.pair)
    own_x = pltpu.make_async_copy(pat.at[place.m], xb.at[0], ps.at[0])
    own_lay = pltpu.make_async_copy(lay, lays.at[0], ps.at[1])
    own_lay.start()
    own_x.start()
    FIRST = (ZB, X0, Y0)
    THEN = (X1, Y1)
    LAST = (D0, D1)

    def assemble():
        whole(SM)
        seg = d // RING
        hid = w2.shape[1]
        for q in range(RING):
            tile = fs[16 * q : 16 * q + 16].astype(F32)
            vec_o[0:8, seg * q : seg * q + seg] = tile[0:8, 0:seg]
            b1_o[0:1, hid * q : hid * q + hid] = tile[6:7, 0:hid]

    def first_norm(grp):
        def body(rows):
            nhat, _ = norm(xb[grp, rows, :].astype(F32))
            here = pl.ds(pl.multiple_of(grp * n + rows.start, 128), 128)
            ac[here, :] = (nhat * vec_o[0:1] + vec_o[1:2]).astype(BF)

        chunks(n, 128, body)

    def project(grp, side):
        cols = pl.ds(side * half, half)
        qkv[grp * n : grp * n + n, cols] = dot(ac[grp * n : grp * n + n], fq[:, cols], 1, 0).astype(BF)

    pairs = HEADS // 2

    def attention(start, stop, early):
        @pl.loop(start, stop)
        def _(i):
            grp, j = i // pairs, lax.rem(i, pairs)
            rows = pl.ds(pl.multiple_of(grp * n, n), n)
            attend_pair(qkv, rows, dist[grp], j, prob, 2 * i, ob, d)
            pltpu.make_async_copy(
                prob.at[pl.ds(2 * i, 2)], p_o.at[pl.ds(2 * i, 2)], ps.at[2 + i]
            ).start()
            for at, steps in early.items():

                @pl.when(i == at)
                def _(steps=steps):
                    for step in steps:
                        pump(*step)

    def second_norm(rows):
        first = (
            xb[rows.start // n, pl.ds(pl.multiple_of(lax.rem(rows.start, n), 256), 256), :].astype(F32)
            + dot(ob[rows, :], fp[...], 1, 0)
            + vec_o[2:3]
        )
        y1[rows, :] = first
        nhat, _ = norm(first)
        ac[rows, :] = (nhat * vec_o[3:4] + vec_o[4:5]).astype(BF)

    def hidden(cols):
        u = dot(ac[...], f1[:, cols], 1, 0) + b1_o[0:1, cols]
        phi = 0.5 + 0.5 * lax.erf(u * 0.7071067811865476)
        g[:, cols] = (u * phi).astype(BF)
        gs[:, cols] = (phi + u * (0.3989422804014327 * jnp.exp(-0.5 * u * u))).astype(BF)

    def span(start, count, step, body):
        chunks(count, step, lambda s: body(pl.ds(pl.multiple_of(start + s.start, step), step)))

    def result(rows):
        ac_rows = y1[rows, :] + dot(g[rows, :], f2[...], 1, 0) + vec_o[5:6]
        qkv[rows, 0:d] = ac_rows.astype(BF)

    for k in range(5):
        hand_over(k, "start")
    own_lay.wait()
    fill_distance(dist.at[0], lays.at[0])
    for k in range(4):
        own_ready(k)
    send_lay.start()
    send_x.start()
    pump(SM, *FIRST)
    pump(QA, *FIRST)
    pump(QB, *FIRST)
    own_ready(4)
    pump(SM, *THEN)
    pump(QA, *THEN)
    pump(QB, *THEN)
    pump(SM, *LAST)
    send_dog.start()
    assemble()
    own_x.wait()
    first_norm(0)
    pump(QA, *LAST)
    pump(QB, *LAST)
    pump(PR, *FIRST)
    pump(UA, *FIRST)
    whole(QA)
    project(0, 0)
    whole(QB)
    project(0, 1)
    attention(
        0,
        6,
        {
            0: [(PR, *THEN), (UB, *FIRST)],
            2: [(UA, *THEN), (DA, *FIRST)],
            5: [(PR, *LAST), (UB, *THEN), (DB, *FIRST)],
        },
    )
    save(fq, wq_o)
    send_lay.wait_recv()
    fill_distance(dist.at[1], lays.at[1])
    send_x.wait_recv()
    first_norm(1)
    project(1, 0)
    project(1, 1)
    qkv_saved = save(qkv, qkv_o)
    save(xb.at[1], x_o)
    save(lays.at[1], lay_o)
    attention(
        6,
        12,
        {
            8: [(UA, *LAST), (DA, *THEN)],
            10: [(UB, *LAST), (DB, *THEN)],
        },
    )
    save(ob, o_o)
    whole(PR)
    save(fp, wp_o)
    chunks(2 * n, 256, second_norm)
    save(y1, y1_o)
    save(ac, c_o)
    pump(DA, *LAST)
    whole(UA)
    span(0, ff // 2, 256, hidden)
    pump(DB, *LAST)
    whole(UB)
    save(f1, w1_o)
    span(ff // 2, ff // 2, 256, hidden)
    save(g, g_o)
    save(gs, gs_o)
    whole(DA)
    whole(DB)
    save(f2, w2_o)
    qkv_saved.wait()
    chunks(2 * n, 512, result)
    save(qkv.at[:, pl.ds(0, d)], enc_o)
    for k in range(5):
        hand_over(k, "send")
    for piece in pieces:
        piece.finish()
    send_x.wait_send()
    send_lay.wait_send()
    send_dog.wait()
    for i in range(2 * pairs):
        pltpu.make_async_copy(
            prob.at[pl.ds(2 * i, 2)], p_o.at[pl.ds(2 * i, 2)], ps.at[2 + i]
        ).wait()
    for copy in saves:
        if copy is not qkv_saved:
            copy.wait()


def forward(spread, pat, dog, lay, wq, wp, w1, w2, sm):
    any_, vm = pl.BlockSpec(memory_space=pl.ANY), pl.BlockSpec(memory_space=pltpu.VMEM)
    n, d = pat.shape[1:]
    ff = w2.shape[1] * RING
    sd = jax.ShapeDtypeStruct
    out = [
        sd((n, d), BF),
        sd((n, d), BF),
        sd(lay.shape, F32),
        sd((d, wq.shape[2]), BF),
        sd((d, d), BF),
        sd((d, ff), BF),
        sd((ff, d), BF),
        sd((8, d), F32),
        sd((8, ff), F32),
        sd((2 * n, wq.shape[2]), BF),
        sd((2 * HEADS, n, n), BF),
        sd((2 * n, d), BF),
        sd((2 * n, d), F32),
        sd((2 * n, d), BF),
        sd((2 * n, ff), BF),
        sd((2 * n, ff), BF),
        sd((2 * n, d), BF),
    ]
    dma = pltpu.SemaphoreType.DMA
    vmem = pltpu.VMEM
    return pl.pallas_call(
        functools.partial(forward_kernel, spread),
        out_shape=out,
        in_specs=[any_] * 8,
        out_specs=[any_] * 7 + [vm] * 2 + [any_] * 8,
        scratch_shapes=[
            vmem((d, wq.shape[2]), BF),
            vmem((d, d), BF),
            vmem((d, ff), BF),
            vmem((ff, d), BF),
            vmem((RING * 16, 128), BF),
            vmem((2, 24, wq.shape[2]), BF),
            vmem((2, 24, d), BF),
            vmem((2, 24, ff), BF),
            vmem((2,) + lay.shape, F32),
            vmem((2, n, n), F32),
            vmem((2, n, d), BF),
            vmem((2 * n, d), BF),
            vmem((2 * n, wq.shape[2]), BF),
            vmem((2 * HEADS, n, n), BF),
            vmem((2 * n, d), BF),
            vmem((2 * n, d), F32),
            vmem((2 * n, ff), BF),
            vmem((2 * n, ff), BF),
            dma((5, 2)),
            dma((5, 2)),
            dma((8, 16)),
            dma((8, 16)),
            dma((3,)),
            dma((3,)),
            dma((16,)),
            dma((2 + HEADS,)),
        ],
        compiler_params=pltpu.CompilerParams(
            collective_id=0, has_side_effects=True, vmem_limit_bytes=62 * 2**20
        ),
        name="forward",
    )(pat, dog, lay, wq, wp, w1, w2, sm)


class Scatter:
    def __init__(self, place, full, rows, got_sib, got, ssem, rsem):
        self.pl, self.full, self.rows = place, full, rows
        self.got_sib, self.got, self.ssem, self.rsem = got_sib, got, ssem, rsem

    def start_of(self, kind):
        fz, fy, fx = FLIPS[kind]
        return pl.multiple_of(self.pl.chip(fz, 0, fy, fx) * self.rows, self.rows)

    def plane(self, z, other):
        c = 1 - self.pl.c if other else self.pl.c
        return pl.ds(pl.multiple_of((z * 2 + c) * (4 * self.rows), self.rows), 4 * self.rows)

    def sib(self, z):
        return rcopy(
            self.full.at[self.plane(z, 1)],
            self.got_sib.at[z],
            self.ssem.at[z],
            self.rsem.at[z],
            self.pl.sib,
        )

    MOVES = {D0: ("y", 0), D1: ("x", 1), X0: ("x", 2), X1: ("x", 3), Y0: ("y", 4), Y1: ("y", 5), ZB: ("z", 6)}

    def move(self, kind):
        way, slot = self.MOVES[kind]
        dev = {"x": self.pl.xn, "y": self.pl.yn, "z": self.pl.zn}[way]
        return rcopy(
            self.full.at[pl.ds(self.start_of(kind), self.rows)],
            self.got.at[slot],
            self.ssem.at[2 + slot],
            self.rsem.at[2 + slot],
            dev,
        )

    def add(self, kind, slots):
        rows = pl.ds(self.start_of(kind), self.rows)
        total = self.full[rows, :].astype(F32)
        for slot in slots:
            total = total + self.got[slot].astype(F32)
        self.full[rows, :] = total.astype(BF)

    def begin(self):
        self.sib(0).start()
        self.sib(1).start()

    def second(self):
        for z in range(2):
            self.sib(z).wait()
        step = 16

        for z in range(2):
            base = (z * 2 + self.pl.c) * (4 * self.rows)

            @pl.loop(0, 4 * self.rows // step)
            def _(i, z=z, base=base):
                rows = pl.ds(pl.multiple_of(base + i * step, step), step)
                theirs = self.got_sib[z, pl.ds(pl.multiple_of(i * step, step), step), :]
                self.full[rows, :] = (self.full[rows, :].astype(F32) + theirs.astype(F32)).astype(BF)

        for kind in (D0, D1, X1, Y0):
            self.move(kind).start()

    def third(self):
        self.move(D0).wait()
        self.add(X0, (0,))
        self.move(X0).start()
        self.move(D1).wait()
        self.add(Y1, (1,))
        self.move(Y1).start()

    def fourth(self):
        self.move(X1).wait()
        self.move(Y1).wait()
        self.add(ZB, (3, 5))
        self.move(ZB).start()

    def total(self):
        self.move(X0).wait()
        self.move(Y0).wait()
        self.move(ZB).wait()
        rows = pl.ds(self.start_of(OWN), self.rows)
        total = self.full[rows, :].astype(F32)
        for slot in (2, 4, 6):
            total = total + self.got[slot].astype(F32)
        return total


def hand_back(place, stage, out, ssem, rsem, go):
    if go == "start":

        @pl.when(place.c == place.m)
        def _():
            pltpu.make_async_copy(stage.at[place.c], out.at[place.m], rsem.at[place.m]).start()
            rcopy(
                stage.at[1 - place.c], out.at[place.m], ssem.at[0], rsem.at[place.m], place.sib
            ).start()

        @pl.when(place.c != place.m)
        def _():
            rcopy(
                stage.at[place.c], out.at[place.m], ssem.at[0], rsem.at[place.m], place.pair
            ).start()
            rcopy(
                stage.at[1 - place.c], out.at[place.m], ssem.at[1], rsem.at[place.m], place.cross
            ).start()

    elif go == "recv":
        for k in range(2):
            rcopy(out.at[k], out.at[k], ssem.at[0], rsem.at[k], place.sib).wait_recv()
    else:
        rcopy(stage.at[0], out.at[0], ssem.at[0], rsem.at[0], place.sib).wait_send()

        @pl.when(place.c != place.m)
        def _():
            rcopy(stage.at[0], out.at[0], ssem.at[1], rsem.at[0], place.sib).wait_send()


def unnorm(dn, nhat, r, gain):
    dh = dn * gain
    return r * (
        dh - jnp.mean(dh, axis=-1, keepdims=True) - nhat * jnp.mean(dh * nhat, axis=-1, keepdims=True)
    )


def attend_back(qkv, rows, probs, do, o, j, d):
    col = pl.multiple_of(j * 128, 128)
    eighth = jnp.asarray(0.125, BF)
    zero = jnp.zeros((), BF)
    cq, ck, cv = head_columns(j, d)
    q, k, v = qkv[rows, cq], qkv[rows, ck], qkv[rows, cv]
    g = do[rows, pl.ds(col, 128)]
    both = g.astype(F32) * o[rows, pl.ds(col, 128)].astype(F32)
    dq = dk = dv = 0.0
    for half in range(2):
        keep = lanes(half)
        p = probs[half]
        gm = jnp.where(keep, g, zero)
        centre = jnp.sum(jnp.where(keep, both, 0.0), axis=1, keepdims=True)
        centre = jnp.broadcast_to(centre, (both.shape[0], 128)).T[0:1]
        ds = (p.astype(F32) * (dot(v, gm, 1, 1) - centre)).astype(BF)
        dk = dk + dot(ds, jnp.where(keep, q * eighth, zero), 1, 0)
        dv = dv + dot(p, gm, 1, 0)
        dq = dq + dot(jnp.where(keep, k * eighth, zero), ds, 0, 0)
    qkv[rows, cq] = dq.T.astype(BF)
    qkv[rows, ck] = dk.astype(BF)
    qkv[rows, cv] = dv.astype(BF)


def backward_kernel(spread, *refs):
    (pat, dog, lay, x_i, dog_i, lay_i, wq_i, wp_i, w1_i, w2_i, vec) = refs[:11]
    (qkv_i, p_i, o_i, y1_i, c_i, g_i, gs_i, y_i) = refs[11:19]
    (oq, op, o1, o2, os_, enc_o, pg_o) = refs[19:26]
    (w2, w1, wp, qkv, g, du, c, ob, dz, y1, do, g2, gp, lays, sums) = refs[26:41]
    got_sib, got, stages = refs[41:48], refs[48:55], refs[55:59]
    (sgot, ss, rs, hs, hr, es, er, ts, tr, ls, ps) = refs[59:]
    place = Place(spread)
    n, d = c.shape[0] // 2, c.shape[1]
    ff = w1.shape[1]
    wide = qkv.shape[1]
    loads = []

    def load(src, dst):
        copy = pltpu.make_async_copy(src, dst, ls.at[len(loads)])
        copy.start()
        loads.append(copy)
        return copy

    lay_l = (load(lay, lays.at[0]), load(lay_i, lays.at[1]))
    dz_l = (
        load(dog.at[place.m], dz.at[pl.ds(0, n)]),
        load(dog_i, dz.at[pl.ds(n, n)]),
    )
    g_l = load(g_i, g)
    w2_l = load(w2_i, w2)
    du_l = load(gs_i, du)
    c_l = load(c_i, c)
    w1_l = load(w1_i, w1)
    y1_l = load(y1_i, y1)
    o_l = load(o_i, ob)
    wp_l = load(wp_i, wp)
    qkv_l = load(qkv_i, qkv)
    place.greet()
    acts = [
        rcopy(y_i.at[pl.ds(n, n)], enc_o.at[place.m], es.at[0], er.at[0], place.pair),
        rcopy(c.at[pl.ds(n, n)], pg_o.at[place.m], es.at[1], er.at[1], place.pair),
    ]
    enc_l = load(y_i.at[pl.ds(0, n)], enc_o.at[place.m])
    acts[0].start()
    gq = du.at[pl.ds(0, d), pl.ds(0, wide)]
    g1 = g.at[pl.ds(0, d)]
    DA, DB, UA, UB, PR, QA, QB = range(7)
    cut = (
        (3, 0, d // 2),
        (3, d // 2, d // 2),
        (2, 0, ff // 2),
        (2, ff // 2, ff // 2),
        (1, 0, d),
        (0, 0, wide // 2),
        (0, wide // 2, wide // 2),
    )
    fulls = (gq, gp, g1, g2)
    outs = (oq, op, o1, o2)
    sc = [
        Scatter(
            place,
            fulls[w].at[:, pl.ds(at, size)],
            fulls[w].shape[0] // 16,
            got_sib[k],
            got[k],
            ss.at[k],
            rs.at[k],
        )
        for k, (w, at, size) in enumerate(cut)
    ]

    def back(k, go):
        w, at, size = cut[k]
        cols = pl.ds(at, size)
        hand_back(place, stages[w].at[:, :, cols], outs[w].at[:, :, cols], hs.at[k], hr.at[k], go)

    def close(k):
        w, at, size = cut[k]
        total = sc[k].total().astype(BF)
        half = total.shape[0] // 2
        stages[w][0, :, at : at + size] = total[:half]
        stages[w][1, :, at : at + size] = total[half:]
        back(k, "start")

    def do_steps(steps):
        for what, k in steps:
            if what == "c":
                close(k)
            else:
                getattr(sc[k], {"b": "begin", "s": "second", "t": "third", "f": "fourth"}[what])()

    sums[...] = jnp.zeros_like(sums)

    def add_sum(row, v):
        sums[row : row + 1] += jnp.sum(v, axis=0, keepdims=True)

    def span(start, count, step, body):
        chunks(count, step, lambda s: body(pl.ds(pl.multiple_of(start + s.start, step), step)))

    for copy in (*lay_l, *dz_l):
        copy.wait()
    for grp in range(2):
        live = lays[grp].T[:, 3:4]
        for part in range(4):
            rows = pl.ds(grp * n + part * (n // 4), n // 4)
            keep = live[part * (n // 4) : (part + 1) * (n // 4)]
            v = dz[rows, :].astype(F32) * keep
            dz[rows, :] = v.astype(BF)
            add_sum(5, v)
    g_l.wait()

    def down_grad(at, size):
        def body(rows):
            g2[rows, pl.ds(at, size)] = dot(g[:, rows], dz[:, pl.ds(at, size)], 0, 0).astype(BF)

        chunks(ff, 768, body)

    def hidden(cols):
        v = dot(dz[...], w2[cols, :], 1, 1) * du[:, cols].astype(F32)
        r = v.astype(BF)
        du[:, cols] = r
        line = jnp.sum(r.astype(F32), axis=0, keepdims=True)
        sums[pl.ds(6 + cols.start // d, 1), pl.ds(pl.multiple_of(lax.rem(cols.start, d), 128), 256)] = line

    pairs = HEADS // 2

    def turn(i):
        third = i // 3
        return 1 - lax.rem(third, 2), (third // 2) * 3 + lax.rem(i, 3)

    def fetch(i):
        grp, j = turn(i)
        src = (grp * pairs + j) * 2
        slot = lax.rem(i, 3)
        for half in range(2):
            yield pltpu.make_async_copy(
                p_i.at[src + half],
                w2.at[pl.ds(pl.multiple_of((slot * 2 + half) * n, n), n), pl.ds(0, n)],
                ps.at[slot, half],
            )

    def up_grad(cols):
        g1[:, cols] = dot(c[...], du[:, cols], 0, 0).astype(BF)

    def second_norm(rows):
        dc = dot(du[rows, :], w1[...], 1, 1)
        nhat, r = norm(y1[rows, :])
        add_sum(3, dc * nhat)
        add_sum(4, dc)
        first = dz[rows, :].astype(F32) + unnorm(dc, nhat, r, vec[3:4])
        y1[rows, :] = first
        low = first.astype(BF)
        c[rows, :] = low
        add_sum(2, low.astype(F32))

    def first_norm(rows):
        nhat, _ = norm(c[rows, :].astype(F32))
        dz[rows, :] = (nhat * vec[0:1] + vec[1:2]).astype(BF)

    def attention(start, stop, work):
        @pl.loop(start, stop)
        def _(i):
            grp, j = turn(i)
            rows = pl.ds(pl.multiple_of(grp * n, n), n)
            for copy in fetch(i):
                copy.wait()
            slot = lax.rem(i, 3)
            probs = [
                w2.at[pl.ds(pl.multiple_of((slot * 2 + half) * n, n), n), pl.ds(0, n)]
                for half in range(2)
            ]
            attend_back(qkv, rows, [p[...] for p in probs], do, ob, j, d)

            @pl.when(i + 3 < 2 * pairs)
            def _():
                for copy in fetch(i + 3):
                    copy.start()

            for at, steps in work.items():

                @pl.when(i == at)
                def _(steps=steps):
                    do_steps(steps)

    def input_grad(rows):
        da = dot(qkv[rows, :], w1[:, pl.ds(0, wide)], 1, 1)
        nhat, r = norm(c[rows, :].astype(F32))
        add_sum(0, da * nhat)
        add_sum(1, da)
        c[rows, :] = (y1[rows, :] + unnorm(da, nhat, r, vec[0:1])).astype(BF)

    def qkv_grad(side):
        cols = pl.ds(side * (wide // 2), wide // 2)
        gq[:, cols] = dot(dz[...], qkv[:, cols], 0, 0).astype(BF)

    hops = (place.sib, place.xn, place.yn, place.zn)

    def hop(i):
        return rcopy(os_.at[place.m], sgot.at[i], ts.at[i], tr.at[i], hops[i])

    def landed(i):
        hop(i).wait()
        os_[place.m] = os_[place.m] + sgot[i]

    down_grad(0, d // 2)
    do_steps([("b", DA)])
    down_grad(d // 2, d // 2)
    do_steps([("b", DB), ("s", DA)])
    w2_l.wait()
    du_l.wait()
    chunks(ff, 256, hidden)
    do_steps([("t", DA), ("s", DB)])
    for i in range(3):
        for copy in fetch(i):
            copy.start()
    c_l.wait()
    span(0, ff // 2, 768, up_grad)
    do_steps([("b", UA)])
    span(ff // 2, ff // 2, 768, up_grad)
    do_steps([("b", UB), ("f", DA), ("t", DB), ("s", UA)])
    w1_l.wait()
    y1_l.wait()
    chunks(2 * n, 256, second_norm)
    do_steps([("f", DB), ("t", UA), ("s", UB)])
    wq_l = load(wq_i, w1.at[:, pl.ds(0, wide)])
    o_l.wait()
    wp_l.wait()
    gp[...] = dot(ob[...], c[...], 0, 0).astype(BF)
    do_steps([("b", PR)])
    do[...] = dot(c[...], wp[...], 1, 1).astype(BF)
    x_l = (load(pat.at[place.m], c.at[pl.ds(0, n)]), load(x_i, c.at[pl.ds(n, n)]))
    for copy in x_l:
        copy.wait()
    chunks(2 * n, 256, first_norm)
    qkv_l.wait()
    attention(
        0,
        6,
        {
            2: [("c", DA), ("f", UA), ("t", UB), ("s", PR)],
            5: [("c", DB), ("f", UB), ("t", PR)],
        },
    )
    qkv_grad(0)
    do_steps([("b", QA)])
    attention(6, 9, {7: [("c", UA), ("f", PR), ("s", QA)]})
    wq_l.wait()
    span(n, n, 256, input_grad)
    acts[1].start()
    attention(9, 12, {9: [("c", UB), ("t", QA)], 11: [("c", PR)]})
    qkv_grad(1)
    do_steps([("b", QB)])
    span(0, n, 256, input_grad)
    pg_l = load(c.at[pl.ds(0, n)], pg_o.at[place.m])
    os_[place.m] = sums[...]
    hop(0).start()
    do_steps([("f", QA), ("s", QB)])
    landed(0)
    hop(1).start()
    do_steps([("t", QB)])
    landed(1)
    hop(2).start()
    do_steps([("c", QA), ("f", QB)])
    landed(2)
    hop(3).start()
    do_steps([("c", QB)])
    landed(3)
    last = rcopy(os_.at[place.m], os_.at[place.m], ts.at[4], tr.at[4], place.pair)
    last.start()
    for k in range(7):
        back(k, "recv")
        back(k, "send")
    last.wait_send()
    theirs = os_.at[1 - place.m]
    rcopy(theirs, theirs, ts.at[4], tr.at[4], place.pair).wait_recv()
    for act in acts:
        act.wait()
    enc_l.wait()
    pg_l.wait()


def backward(spread, pat, dog, lay, *kept):
    any_, vm = pl.BlockSpec(memory_space=pl.ANY), pl.BlockSpec(memory_space=pltpu.VMEM)
    n, d = pat.shape[1:]
    wide, ff = kept[3].shape[1], kept[5].shape[1]
    shapes = ((48, wide), (48, d), (48, ff), (ff // 16, d))
    cuts = 2 * ((ff // 16, d // 2),) + 2 * ((48, ff // 2),) + ((48, d),) + 2 * ((48, wide // 2),)
    sd = jax.ShapeDtypeStruct
    out = [sd((2, r // 2, k), BF) for r, k in shapes]
    out += [sd((2, 16, d), F32), sd((2, n, d), BF), sd((2, n, d), BF)]
    dma = pltpu.SemaphoreType.DMA
    vmem = pltpu.VMEM
    return pl.pallas_call(
        functools.partial(backward_kernel, spread),
        out_shape=out,
        in_specs=[any_] * 10 + [vm] + [any_] * 8,
        out_specs=[any_] * 4 + [vm] + [any_] * 2,
        scratch_shapes=[
            vmem((ff, d), BF),
            vmem((d, ff), BF),
            vmem((d, d), BF),
            vmem((2 * n, wide), BF),
            vmem((2 * n, ff), BF),
            vmem((2 * n, ff), BF),
            vmem((2 * n, d), BF),
            vmem((2 * n, d), BF),
            vmem((2 * n, d), BF),
            vmem((2 * n, d), F32),
            vmem((2 * n, d), BF),
            vmem((ff, d), BF),
            vmem((d, d), BF),
            vmem((2,) + lay.shape, F32),
            vmem((16, d), F32),
        ]
        + [vmem((2, 4 * r, k), BF) for r, k in cuts]
        + [vmem((7, r, k), BF) for r, k in cuts]
        + [vmem((2, r // 2, k), BF) for r, k in shapes]
        + [
            vmem((4, 16, d), F32),
            dma((7, 9)),
            dma((7, 9)),
            dma((7, 2)),
            dma((7, 2)),
            dma((2,)),
            dma((2,)),
            dma((5,)),
            dma((5,)),
            dma((18,)),
            dma((3, 2)),
        ],
        compiler_params=pltpu.CompilerParams(
            collective_id=1, has_side_effects=True, vmem_limit_bytes=62 * 2**20
        ),
        name="backward",
    )(pat, dog, lay, *kept)


def small_pack(parts, b1):
    rows = jnp.stack([jnp.pad(v, ((0, 0), (0, 128 - v.shape[1]))) for v in (*parts, b1)], axis=1)
    return jnp.pad(rows, ((0, 0), (0, 16 - rows.shape[1]), (0, 0)))


def local(
    count, patches, tile_kind, out_grad, n1g, n1b, wq, wp, bp, n2g, n2b, w1, b1, w2, b2
):
    spread = count // RING
    idx = lax.axis_index("fsdp")
    p = idx // spread
    rows, d = patches.shape[1:]
    parts = (n1g, n1b, bp, n2g, n2b, b2)
    if spread > 1:
        groups = [[q * spread + j for j in range(spread)] for q in range(RING)]
        ag = functools.partial(
            lax.all_gather, axis_name="fsdp", axis=1, tiled=True, axis_index_groups=groups
        )
        wq, wp, w1, w2, b1 = ag(wq), ag(wp), ag(w1), ag(w2), ag(b1)
        parts = tuple(ag(v) for v in parts)
    lay = jnp.stack([v.astype(F32) for v in packing(tile_kind, rows)])
    lay = jnp.pad(lay, ((0, 4), (0, 0)))
    sm = small_pack(parts, b1)
    pat2, dog2, lay2, fq, fp, f1, f2, vecs, _, *saved = forward(
        spread, patches, out_grad, lay, wq, wp, w1, w2, sm
    )
    oq, op, o1, o2, os_, encoded, pgrad = backward(
        spread, patches, out_grad, lay, pat2, dog2, lay2, fq, fp, f1, f2, vecs, *saved
    )
    pgrad = pgrad.astype(F32)
    oq = oq.reshape(*oq.shape[:2], 2, 3, d // 2).swapaxes(2, 3).reshape(oq.shape)
    seg = d // RING
    vec = lax.dynamic_slice_in_dim(os_[:, :6], p * seg, seg, axis=2)
    hid = os_[:, 6 : 6 + w2.shape[1] * RING // d].reshape(2, -1)
    hid = lax.dynamic_slice_in_dim(hid, p * w2.shape[1], w2.shape[1], axis=1)
    grads = [oq.astype(F32), op.astype(F32), o1.astype(F32), o2.astype(F32)]
    if spread > 1:
        rs = functools.partial(
            lax.psum_scatter, axis_name="fsdp", tiled=True, axis_index_groups=groups
        )
        grads = [rs(v, scatter_dimension=1) for v in grads]
        vec, hid = rs(vec, scatter_dimension=2), rs(hid, scatter_dimension=1)
    return (
        encoded,
        pgrad,
        vec[:, 0],
        vec[:, 1],
        grads[0],
        grads[1],
        vec[:, 2],
        vec[:, 3],
        vec[:, 4],
        grads[2],
        hid,
        grads[3],
        vec[:, 5],
    )


def solution(mesh):
    three, two = P(None, "fsdp", None), P(None, "fsdp")
    in_specs = (three, P("fsdp"), three, two, two, three, three, two, two, two, three, two, three, two)
    out_specs = (three, three, two, two, three, three, two, two, two, three, two, three, two)
    return jax.shard_map(
        functools.partial(local, mesh.shape["fsdp"]),
        mesh=mesh,
        in_specs=in_specs,
        out_specs=out_specs,
        check_vma=False,
    )
```

```python
import functools

import jax
import jax.numpy as jnp
from jax import lax
from jax.experimental import pallas as pl
from jax.experimental.pallas import tpu as pltpu
from jax.sharding import PartitionSpec as P

HEADS = 12
SIDE_S = 12
SIDE_M = 15
SIDE_L = 20
RING = 32
MESH = pl.DeviceIdType.MESH
BF = jnp.bfloat16
F32 = jnp.float32
FAR = 1e33


class Place:
    def __init__(self, spread):
        me = lax.axis_index("fsdp")
        self.rest = lax.rem(me, spread)
        self.spread = spread
        p = me // spread
        self.p = p
        self.c = lax.rem(p, 2)
        self.x = lax.rem(p // 2, 2)
        self.y = lax.rem(p // 4, 2)
        self.m = lax.rem(p // 8, 2)
        self.z = lax.rem(p // 16, 2)
        self.sib = self.at(c=1 - self.c)
        self.xn = self.at(x=1 - self.x)
        self.yn = self.at(y=1 - self.y)
        self.zn = self.at(z=1 - self.z)
        self.pair = self.at(m=1 - self.m)

    def at(self, **other):
        z, m, y, x, c = (other.get(k, getattr(self, k)) for k in "zmyxc")
        return ((((z * 2 + m) * 2 + y) * 2 + x) * 2 + c) * self.spread + self.rest,

    def chip(self, fz, fc, fy, fx):
        flip = lambda v, f: 1 - v if f else v
        return (
            (flip(self.z, fz) * 2 + flip(self.c, fc)) * 2 + flip(self.y, fy)
        ) * 2 + flip(self.x, fx)

    def greet(self):
        barrier = pltpu.get_barrier_semaphore()
        everyone = [self.sib, self.xn, self.yn]
        for fz in range(2):
            for fm in range(2):
                for fc in range(2):
                    if fz or fm:
                        z, m, c = self.z, self.m, self.c
                        everyone.append(
                            self.at(
                                z=1 - z if fz else z, m=1 - m if fm else m, c=1 - c if fc else c
                            )
                        )
        for other in everyone:
            pl.semaphore_signal(barrier, inc=1, device_id=other, device_id_type=MESH)
        pl.semaphore_wait(barrier, len(everyone))


OWN, ZB, X0, X1, Y0, Y1, D0, D1 = range(8)
FLIPS = ((0, 0, 0), (1, 0, 0), (0, 0, 1), (1, 0, 1), (0, 1, 0), (1, 1, 0), (0, 1, 1), (1, 1, 1))


def rcopy(src, dst, ssem, rsem, dev):
    return pltpu.make_async_remote_copy(
        src_ref=src, dst_ref=dst, send_sem=ssem, recv_sem=rsem, device_id=dev, device_id_type=MESH
    )


class Gather:
    def __init__(self, place, full, rows, ssem, rsem):
        self.pl, self.full, self.rows, self.ssem, self.rsem = place, full, rows, ssem, rsem

    def block(self, kind, other=0):
        fz, fy, fx = FLIPS[kind]
        start = self.pl.chip(fz, other, fy, fx) * self.rows
        return self.full.at[pl.ds(pl.multiple_of(start, self.rows), self.rows)]

    def send(self, kind, way):
        place = self.pl
        if way == "s":
            dev, slot = place.sib, 8 + kind
        else:
            dev = {"x": place.xn, "y": place.yn}[way]
            fz, fy, fx = FLIPS[kind]
            flips = {"x": (fz, fy, 1 - fx), "y": (fz, 1 - fy, fx)}[way]
            slot = FLIPS.index(flips)
        view = self.block(kind)
        return rcopy(view, view, self.ssem.at[slot], self.rsem.at[slot], dev)

    AFTER = {
        OWN: "xys",
        ZB: "xys",
        X0: "ys",
        X1: "s",
        Y0: "s",
        Y1: "xs",
        D0: "s",
        D1: "s",
    }

    def start(self, kind):
        for way in self.AFTER[kind]:
            self.send(kind, way).start()

    def arrived(self, kind, other=0):
        view = self.block(kind, other)
        slot = kind + 8 * other
        rcopy(view, view, self.ssem.at[slot], self.rsem.at[slot], self.pl.sib).wait_recv()

    def finish(self):
        for kind in range(8):
            for way in self.AFTER[kind]:
                self.send(kind, way).wait_send()


def hand_in(place, shard, spot, ssem, rsem, go):
    def legs():
        for far in range(2):
            for fm in range(2):
                z = 1 - place.z if far else place.z
                m = 1 - place.m if fm else place.m
                yield far, fm, m, place.at(z=z, m=m, c=place.m)

    def copy(far, fm, m, dev):
        return rcopy(
            shard.at[m], spot(far, None), ssem.at[2 * far + fm], rsem.at[2 * far + place.c], dev
        )

    here = place.c == place.m
    if go == "start":
        for far, fm, m, dev in legs():
            if far or fm:
                copy(far, fm, m, dev).start()
            else:

                @pl.when(here)
                def _():
                    pltpu.make_async_copy(shard.at[m], spot(0, None), rsem.at[place.c]).start()

                @pl.when(jnp.logical_not(here))
                def _():
                    copy(far, fm, m, dev).start()

    elif go in ("near", "far"):
        far = int(go == "far")
        for piece in range(2):
            dst = spot(far, piece)
            rcopy(dst, dst, ssem.at[0], rsem.at[2 * far + piece], place.sib).wait_recv()
    else:
        for far, fm, m, dev in legs():
            if far or fm:
                copy(far, fm, m, dev).wait_send()
            else:

                @pl.when(jnp.logical_not(here))
                def _():
                    copy(far, fm, m, dev).wait_send()


def dot(a, b, ca, cb):
    return lax.dot_general(a, b, (((ca,), (cb,)), ((), ())), preferred_element_type=F32)


def chunks(count, step, body):
    @pl.loop(0, count // step)
    def _(i):
        body(pl.ds(pl.multiple_of(i * step, step), step))


def norm(v):
    center = v - jnp.mean(v, axis=-1, keepdims=True)
    r = lax.rsqrt(jnp.mean(center * center, axis=-1, keepdims=True) + 1e-06)
    return center * r, r


def fill_distance(dist, lay):
    across = lay[...]
    down = across.T
    gap_r = down[:, 1:2] - across[1:2]
    gap_c = down[:, 2:3] - across[2:3]
    far = jnp.sqrt(gap_r * gap_r + gap_c * gap_c)
    dist[...] = jnp.where(down[:, 0:1] == across[0:1], far, FAR)


def lanes(half):
    return lax.broadcasted_iota(jnp.int32, (1, 128), 1) // 64 == half


def slope_of(head):
    return jnp.exp2(jnp.full((1, 1), -8.0 / HEADS, F32) * (head + 1).astype(F32))


def head_columns(j, d):
    pairs = HEADS // 4
    base = (j // pairs) * (3 * d // 2) + lax.rem(j, pairs) * 128
    return [pl.ds(pl.multiple_of(base + part * (d // 2), 128), 128) for part in range(3)]


def attend_pair(qkv, rows, dist, j, prob, slot, o, d):
    col = pl.multiple_of(j * 128, 128)
    cq, ck, cv = head_columns(j, d)
    q = qkv[rows, cq] * jnp.asarray(0.125, BF)
    k = qkv[rows, ck]
    v = qkv[rows, cv]
    zero = jnp.zeros((), BF)
    total = None
    for half in range(2):
        keep = lanes(half)
        s = dot(k, jnp.where(keep, q, zero), 1, 1) - slope_of(2 * j + half) * dist
        e = jnp.exp(s - jnp.max(s, axis=0, keepdims=True))
        p = (e * (1.0 / jnp.sum(e, axis=0, keepdims=True))).astype(BF)
        prob[slot + half] = p
        part = dot(jnp.where(keep, v, zero), p, 0, 0)
        total = part if total is None else total + part
    o[rows, pl.ds(col, 128)] = total.T.astype(BF)


def fill_layout(lay, kinds, n):
    at = lax.broadcasted_iota(jnp.int32, (1, n), 1)
    slots = kinds.shape[0]
    segment, row, live = slots + at, at, jnp.zeros((1, n), jnp.int32)
    col = jnp.zeros((1, n), jnp.int32)
    start = jnp.int32(0)
    for slot in range(slots):
        kind = kinds[slot]
        side = jnp.where(kind == 0, SIDE_S, jnp.where(kind == 1, SIDE_M, SIDE_L))
        inverse = jnp.where(kind == 0, 1 / SIDE_S, jnp.where(kind == 1, 1 / SIDE_M, 1 / SIDE_L))
        end = start + side * side
        inside = (at >= start) & (at < end) & (end <= n)
        offset = at - start
        down = jnp.floor((offset.astype(F32) + 0.5) * inverse.astype(F32)).astype(jnp.int32)
        segment = jnp.where(inside, slot, segment)
        row = jnp.where(inside, down, row)
        col = jnp.where(inside, offset - down * side, col)
        live = jnp.where(inside, 1, live)
        start = end
    zero = jnp.zeros((4, n), F32)
    lay[...] = jnp.concatenate([v.astype(F32) for v in (segment, row, col, live)] + [zero], axis=0)


def forward_kernel(spread, *refs):
    (pat, dog, kinds, wq, wp, w1, w2) = refs[:7]
    vectors = refs[7:14]
    (x_o, dog_o, lay_o, wq_o, wp_o, w1_o, w2_o, vec_o, b1_o) = refs[14:23]
    (qkv_o, p_o, o_o, y1_o, c_o, g_o, gs_o, enc_o) = refs[23:31]
    (fq, fp, f1, f2, fs, gq, gp, g1) = refs[31:39]
    (lays, dist, xb, ac, qkv, prob, ob, y1, g, gs, smf, sm) = refs[39:51]
    (hs, hr, ss, rs, as_, ar, ls, ps) = refs[51:]
    place = Place(spread)
    d = xb.shape[2]
    n = xb.shape[1]
    ff = g.shape[1]
    smf[...] = jnp.zeros_like(smf)
    for at, ref in enumerate(vectors):
        both = ref[...].astype(F32)
        for m in range(2):
            smf[m, at : at + 1, 0 : both.shape[1]] = both[m : m + 1]
    for m in range(2):
        sm[m] = smf[m].astype(BF)
    place.greet()
    hand = ((sm, fs, None, 16), (wq, fq, gq, 24), (wp, fp, gp, 24), (w1, f1, g1, 24))
    hand += ((w2, f2, None, w2.shape[1]),)
    SM, QA, QB, PR, UA, UB, DA, DB = range(8)
    half = 3 * d // 2
    cut = (
        (0, fs),
        (1, fq.at[:, pl.ds(0, half)]),
        (1, fq.at[:, pl.ds(half, half)]),
        (2, fp),
        (3, f1.at[:, pl.ds(0, ff // 2)]),
        (3, f1.at[:, pl.ds(ff // 2, ff // 2)]),
        (4, f2.at[:, pl.ds(0, d // 2)]),
        (4, f2.at[:, pl.ds(d // 2, d // 2)]),
    )
    pieces = [
        Gather(place, view, 2 * hand[k][3], ss.at[i], rs.at[i]) for i, (k, view) in enumerate(cut)
    ]

    def spot_of(k):
        _, full, stage, rows = hand[k]

        def spot(far, piece):
            if stage is not None:
                return stage.at[far, place.c if piece is None else piece]
            at = place.p if piece is None else place.chip(far, 0, 0, 0) * 2 + piece
            return full.at[pl.ds(pl.multiple_of(at * rows, 16), rows)]

        return spot

    def hand_over(k, go):
        hand_in(place, hand[k][0], spot_of(k), hs.at[k], hr.at[k], go)

    def ready(k, far):
        hand_over(k, "far" if far else "near")
        _, full, stage, rows = hand[k]
        if stage is not None:
            start = pl.multiple_of(place.chip(far, 0, 0, 0) * (2 * rows), 2 * rows)

            def pack(src, dst):
                both = [stage[far, piece, :, src].astype(F32) for piece in range(2)]
                full[pl.ds(start, 2 * rows), dst] = jnp.concatenate(both, axis=0).astype(BF)

            if k == 1:
                for part in range(3):
                    for side in range(2):
                        pack(
                            pl.ds(part * d + side * (d // 2), d // 2),
                            pl.ds((side * 3 + part) * (d // 2), d // 2),
                        )
            else:
                pack(pl.ds(0, full.shape[1]), pl.ds(0, full.shape[1]))
        for i, (at, _) in enumerate(cut):
            if at == k:
                pieces[i].start(ZB if far else OWN)

    def pump(i, *kinds):
        for kind in kinds:
            pieces[i].arrived(kind)
            pieces[i].start(kind)

    def whole(i):
        for kind in range(8):
            pieces[i].arrived(kind, 1)

    saves = []

    def save(src, dst):
        copy = pltpu.make_async_copy(src, dst, ls.at[len(saves)])
        copy.start()
        saves.append(copy)
        return copy

    send_x = rcopy(pat.at[1 - place.m], xb.at[1], as_.at[0], ar.at[0], place.pair)
    send_dog = rcopy(dog.at[1 - place.m], dog_o, as_.at[1], ar.at[1], place.pair)
    send_lay = rcopy(lays.at[0], lays.at[1], as_.at[2], ar.at[2], place.pair)
    own_x = pltpu.make_async_copy(pat.at[place.m], xb.at[0], ps.at[0])
    own_x.start()
    FIRST = (X0, Y0)
    THEN = (X1, Y1)
    LAST = (D0, D1)

    def assemble():
        whole(SM)
        seg = d // RING
        hid = w2.shape[1]
        for q in range(RING):
            tile = fs[16 * q : 16 * q + 16].astype(F32)
            vec_o[0:8, seg * q : seg * q + seg] = tile[0:8, 0:seg]
            b1_o[0:1, hid * q : hid * q + hid] = tile[6:7, 0:hid]

    def first_norm(grp):
        def body(rows):
            nhat, _ = norm(xb[grp, rows, :].astype(F32))
            here = pl.ds(pl.multiple_of(grp * n + rows.start, 128), 128)
            ac[here, :] = (nhat * vec_o[0:1] + vec_o[1:2]).astype(BF)

        chunks(n, 128, body)

    def project(grp, side):
        cols = pl.ds(side * half, half)
        qkv[grp * n : grp * n + n, cols] = dot(ac[grp * n : grp * n + n], fq[:, cols], 1, 0).astype(BF)

    pairs = HEADS // 2

    def attention(start, stop, early):
        @pl.loop(start, stop)
        def _(i):
            grp, j = i // pairs, lax.rem(i, pairs)
            rows = pl.ds(pl.multiple_of(grp * n, n), n)
            attend_pair(qkv, rows, dist[grp], j, prob, 2 * i, ob, d)
            pltpu.make_async_copy(
                prob.at[pl.ds(2 * i, 2)], p_o.at[pl.ds(2 * i, 2)], ps.at[2 + i]
            ).start()
            for at, steps in early.items():

                @pl.when(i == at)
                def _(steps=steps):
                    for step in steps:
                        if step[0] == "far":
                            ready(step[1], 1)
                        else:
                            pump(*step)

    def second_norm(rows):
        first = (
            xb[rows.start // n, pl.ds(pl.multiple_of(lax.rem(rows.start, n), 256), 256), :].astype(F32)
            + dot(ob[rows, :], fp[...], 1, 0)
            + vec_o[2:3]
        )
        y1[rows, :] = first
        nhat, _ = norm(first)
        ac[rows, :] = (nhat * vec_o[3:4] + vec_o[4:5]).astype(BF)

    def hidden(cols):
        u = dot(ac[...], f1[:, cols], 1, 0) + b1_o[0:1, cols]
        phi = 0.5 + 0.5 * lax.erf(u * 0.7071067811865476)
        g[:, cols] = (u * phi).astype(BF)
        gs[:, cols] = (phi + u * (0.3989422804014327 * jnp.exp(-0.5 * u * u))).astype(BF)

    def span(start, count, step, body):
        chunks(count, step, lambda s: body(pl.ds(pl.multiple_of(start + s.start, step), step)))

    def result(rows):
        ac_rows = y1[rows, :] + dot(g[rows, :], f2[...], 1, 0) + vec_o[5:6]
        qkv[rows, 0:d] = ac_rows.astype(BF)

    for k in range(5):
        hand_over(k, "start")
    fill_layout(lays.at[0], kinds, n)
    send_lay.start()
    send_x.start()
    fill_distance(dist.at[0], lays.at[0])
    for k in range(3):
        ready(k, 0)
    ready(0, 1)
    ready(1, 1)
    ready(3, 0)
    pump(SM, *FIRST)
    pump(QA, *FIRST)
    pump(QB, *FIRST)
    ready(4, 0)
    pump(SM, *THEN)
    pump(QA, *THEN)
    pump(QB, *THEN)
    ready(2, 1)
    pump(PR, *FIRST)
    pump(SM, *LAST)
    assemble()
    own_x.wait()
    first_norm(0)
    pump(QA, *LAST)
    pump(QB, *LAST)
    send_dog.start()
    whole(QA)
    project(0, 0)
    ready(3, 1)
    pump(UA, *FIRST)
    whole(QB)
    project(0, 1)
    pump(UB, *FIRST)
    pump(PR, *THEN)
    attention(0, 1, {})
    attention(1, 6, {1: [("far", 4)], 2: [(UA, *THEN)], 3: [(UB, *THEN)], 4: [(DA, *FIRST)], 5: [(DB, *FIRST), (PR, *LAST)]})
    save(fq, wq_o)
    send_lay.wait_recv()
    fill_distance(dist.at[1], lays.at[1])
    send_x.wait_recv()
    first_norm(1)
    project(1, 0)
    project(1, 1)
    qkv_saved = save(qkv, qkv_o)
    save(xb.at[1], x_o)
    save(lays, lay_o)
    attention(6, 12, {7: [(DA, *THEN)], 8: [(UA, *LAST)], 9: [(DB, *THEN)], 10: [(UB, *LAST)]})
    save(ob, o_o)
    whole(PR)
    save(fp, wp_o)
    chunks(2 * n, 256, second_norm)
    save(y1, y1_o)
    save(ac, c_o)
    pump(DA, *LAST)
    whole(UA)
    span(0, ff // 2, 256, hidden)
    pump(DB, *LAST)
    whole(UB)
    save(f1, w1_o)
    span(ff // 2, ff // 2, 256, hidden)
    save(g, g_o)
    save(gs, gs_o)
    whole(DA)
    whole(DB)
    save(f2, w2_o)
    qkv_saved.wait()
    chunks(2 * n, 512, result)
    save(qkv.at[:, pl.ds(0, d)], enc_o)
    for k in range(5):
        hand_over(k, "send")
    for piece in pieces:
        piece.finish()
    send_x.wait_send()
    send_lay.wait_send()
    send_dog.wait()
    for i in range(2 * pairs):
        pltpu.make_async_copy(
            prob.at[pl.ds(2 * i, 2)], p_o.at[pl.ds(2 * i, 2)], ps.at[2 + i]
        ).wait()
    for copy in saves:
        if copy is not qkv_saved:
            copy.wait()


def forward(spread, pat, dog, kinds, wq, wp, w1, w2, *vectors):
    any_, vm = pl.BlockSpec(memory_space=pl.ANY), pl.BlockSpec(memory_space=pltpu.VMEM)
    n, d = pat.shape[1:]
    ff = w2.shape[1] * RING
    sd = jax.ShapeDtypeStruct
    out = [
        sd((n, d), BF),
        sd((n, d), BF),
        sd((2, 8, n), F32),
        sd((d, wq.shape[2]), BF),
        sd((d, d), BF),
        sd((d, ff), BF),
        sd((ff, d), BF),
        sd((8, d), F32),
        sd((8, ff), F32),
        sd((2 * n, wq.shape[2]), BF),
        sd((2 * HEADS, n, n), BF),
        sd((2 * n, d), BF),
        sd((2 * n, d), F32),
        sd((2 * n, d), BF),
        sd((2 * n, ff), BF),
        sd((2 * n, ff), BF),
        sd((2 * n, d), BF),
    ]
    dma = pltpu.SemaphoreType.DMA
    vmem = pltpu.VMEM
    return pl.pallas_call(
        functools.partial(forward_kernel, spread),
        out_shape=out,
        in_specs=[any_] * 2 + [pl.BlockSpec(memory_space=pltpu.SMEM)] + [any_] * 4 + [vm] * 7,
        out_specs=[any_] * 7 + [vm] * 2 + [any_] * 8,
        scratch_shapes=[
            vmem((d, wq.shape[2]), BF),
            vmem((d, d), BF),
            vmem((d, ff), BF),
            vmem((ff, d), BF),
            vmem((RING * 16, 128), BF),
            vmem((2, 2, 24, wq.shape[2]), BF),
            vmem((2, 2, 24, d), BF),
            vmem((2, 2, 24, ff), BF),
            vmem((2, 8, n), F32),
            vmem((2, n, n), F32),
            vmem((2, n, d), BF),
            vmem((2 * n, d), BF),
            vmem((2 * n, wq.shape[2]), BF),
            vmem((2 * HEADS, n, n), BF),
            vmem((2 * n, d), BF),
            vmem((2 * n, d), F32),
            vmem((2 * n, ff), BF),
            vmem((2 * n, ff), BF),
            vmem((2, 16, 128), F32),
            vmem((2, 16, 128), BF),
            dma((5, 4)),
            dma((5, 4)),
            dma((8, 16)),
            dma((8, 16)),
            dma((3,)),
            dma((3,)),
            dma((16,)),
            dma((2 + HEADS,)),
        ],
        compiler_params=pltpu.CompilerParams(
            collective_id=0, has_side_effects=True, vmem_limit_bytes=62 * 2**20
        ),
        name="forward",
    )(pat, dog, kinds, wq, wp, w1, w2, *vectors)


class Scatter:
    def __init__(self, place, full, rows, got_sib, got, ssem, rsem):
        self.pl, self.full, self.rows = place, full, rows
        self.got_sib, self.got, self.ssem, self.rsem = got_sib, got, ssem, rsem

    def start_of(self, kind):
        fz, fy, fx = FLIPS[kind]
        return pl.multiple_of(self.pl.chip(fz, 0, fy, fx) * self.rows, self.rows)

    def plane(self, z, other):
        c = 1 - self.pl.c if other else self.pl.c
        return pl.ds(pl.multiple_of((z * 2 + c) * (4 * self.rows), self.rows), 4 * self.rows)

    def sib(self, z):
        return rcopy(
            self.full.at[self.plane(z, 1)],
            self.got_sib.at[z],
            self.ssem.at[z],
            self.rsem.at[z],
            self.pl.sib,
        )

    MOVES = {D0: ("y", 0), D1: ("x", 1), X0: ("x", 2), X1: ("x", 3), Y0: ("y", 4), Y1: ("y", 5)}

    def move(self, kind):
        way, slot = self.MOVES[kind]
        dev = {"x": self.pl.xn, "y": self.pl.yn}[way]
        return rcopy(
            self.full.at[pl.ds(self.start_of(kind), self.rows)],
            self.got.at[slot],
            self.ssem.at[2 + slot],
            self.rsem.at[2 + slot],
            dev,
        )

    def add(self, kind, slots):
        rows = pl.ds(self.start_of(kind), self.rows)
        total = self.full[rows, :].astype(F32)
        for slot in slots:
            total = total + self.got[slot].astype(F32)
        self.full[rows, :] = total.astype(BF)

    def begin(self):
        self.sib(0).start()
        self.sib(1).start()

    def second(self):
        for z in range(2):
            self.sib(z).wait()
        step = 16

        for z in range(2):
            base = (z * 2 + self.pl.c) * (4 * self.rows)

            @pl.loop(0, 4 * self.rows // step)
            def _(i, z=z, base=base):
                rows = pl.ds(pl.multiple_of(base + i * step, step), step)
                theirs = self.got_sib[z, pl.ds(pl.multiple_of(i * step, step), step), :]
                self.full[rows, :] = (self.full[rows, :].astype(F32) + theirs.astype(F32)).astype(BF)

        for kind in (D0, D1, X1, Y0):
            self.move(kind).start()

    def third(self):
        self.move(D0).wait()
        self.add(X0, (0,))
        self.move(X0).start()
        self.move(D1).wait()
        self.add(Y1, (1,))
        self.move(Y1).start()

    def total(self, far):
        kind, slots = (ZB, (X1, Y1)) if far else (OWN, (X0, Y0))
        rows = pl.ds(self.start_of(kind), self.rows)
        total = self.full[rows, :].astype(F32)
        for move in slots:
            self.move(move).wait()
            total = total + self.got[self.MOVES[move][1]].astype(F32)
        return total.astype(BF)


def hand_back(place, stage, outs, ssem, rsem, go):
    def leg(far, k):
        z = 1 - place.z if far else place.z
        return rcopy(
            stage.at[far, k],
            outs[far].at[place.m],
            ssem.at[2 * far + k],
            rsem.at[2 * far + place.m],
            place.at(z=z, m=place.c, c=k),
        )

    def each(far, k, local, remote):
        if far:
            remote()
        else:
            here = jnp.logical_and(place.c == place.m, place.c == k)
            pl.when(here)(local)
            pl.when(jnp.logical_not(here))(remote)

    if go in ("near", "far"):
        far = int(go == "far")
        for k in range(2):

            def local(k=k):
                pltpu.make_async_copy(
                    stage.at[0, k], outs[0].at[place.m], rsem.at[place.m]
                ).start()

            each(far, k, local, lambda k=k: leg(far, k).start())
    elif go == "recv":
        for far in range(2):
            for m in range(2):
                dst = outs[far].at[m]
                rcopy(dst, dst, ssem.at[0], rsem.at[2 * far + m], place.sib).wait_recv()
    else:
        for far in range(2):
            for k in range(2):
                each(far, k, lambda: None, lambda far=far, k=k: leg(far, k).wait_send())


def unnorm(dn, nhat, r, gain):
    dh = dn * gain
    return r * (
        dh - jnp.mean(dh, axis=-1, keepdims=True) - nhat * jnp.mean(dh * nhat, axis=-1, keepdims=True)
    )


def attend_back(qkv, rows, probs, do, o, j, d):
    col = pl.multiple_of(j * 128, 128)
    eighth = jnp.asarray(0.125, BF)
    zero = jnp.zeros((), BF)
    cq, ck, cv = head_columns(j, d)
    q, k, v = qkv[rows, cq], qkv[rows, ck], qkv[rows, cv]
    g = do[rows, pl.ds(col, 128)]
    both = g.astype(F32) * o[rows, pl.ds(col, 128)].astype(F32)
    dq = dk = dv = 0.0
    for half in range(2):
        keep = lanes(half)
        p = probs[half]
        gm = jnp.where(keep, g, zero)
        centre = jnp.sum(jnp.where(keep, both, 0.0), axis=1, keepdims=True)
        centre = jnp.broadcast_to(centre, (both.shape[0], 128)).T[0:1]
        ds = (p.astype(F32) * (dot(v, gm, 1, 1) - centre)).astype(BF)
        dk = dk + dot(ds, jnp.where(keep, q * eighth, zero), 1, 0)
        dv = dv + dot(p, gm, 1, 0)
        dq = dq + dot(jnp.where(keep, k * eighth, zero), ds, 0, 0)
    qkv[rows, cq] = dq.T.astype(BF)
    qkv[rows, ck] = dk.astype(BF)
    qkv[rows, cv] = dv.astype(BF)


def backward_kernel(spread, *refs):
    (pat, dog, x_i, dog_i, lay_i, wq_i, wp_i, w1_i, w2_i, vec) = refs[:10]
    (qkv_i, p_i, o_i, y1_i, c_i, g_i, gs_i, y_i) = refs[10:18]
    outs = (refs[18:22], refs[22:26])
    (os_, enc_o, pg_o) = refs[26:29]
    (w2, w1, wp, qkv, g, du, c, ob, dz, y1, do, g2, gp, lays, sums) = refs[29:44]
    got_sib, got, stages = refs[44:51], refs[51:58], refs[58:62]
    (sgot, ss, rs, hs, hr, es, er, ts, tr, ls, ps) = refs[62:]
    place = Place(spread)
    n, d = c.shape[0] // 2, c.shape[1]
    ff = w1.shape[1]
    wide = qkv.shape[1]
    loads = []

    def load(src, dst):
        copy = pltpu.make_async_copy(src, dst, ls.at[len(loads)])
        copy.start()
        loads.append(copy)
        return copy

    lay_l = (load(lay_i, lays),)
    dz_l = (
        load(dog.at[place.m], dz.at[pl.ds(0, n)]),
        load(dog_i, dz.at[pl.ds(n, n)]),
    )
    g_l = load(g_i, g)
    w2_l = load(w2_i, w2)
    du_l = load(gs_i, du)
    c_l = load(c_i, c)
    w1_l = load(w1_i, w1)
    y1_l = load(y1_i, y1)
    o_l = load(o_i, ob)
    wp_l = load(wp_i, wp)
    qkv_l = load(qkv_i, qkv)
    place.greet()
    acts = [
        rcopy(y_i.at[pl.ds(n, n)], enc_o.at[place.m], es.at[0], er.at[0], place.pair),
        rcopy(c.at[pl.ds(n, n)], pg_o.at[place.m], es.at[1], er.at[1], place.pair),
    ]
    enc_l = load(y_i.at[pl.ds(0, n)], enc_o.at[place.m])
    acts[0].start()
    gq = du.at[pl.ds(0, d), pl.ds(0, wide)]
    g1 = g.at[pl.ds(0, d)]
    DA, DB, UA, UB, PR, QA, QB = range(7)
    cut = (
        (3, 0, d // 2),
        (3, d // 2, d // 2),
        (2, 0, ff // 2),
        (2, ff // 2, ff // 2),
        (1, 0, d),
        (0, 0, wide // 2),
        (0, wide // 2, wide // 2),
    )
    fulls = (gq, gp, g1, g2)
    sc = [
        Scatter(
            place,
            fulls[w].at[:, pl.ds(at, size)],
            fulls[w].shape[0] // 16,
            got_sib[k],
            got[k],
            ss.at[k],
            rs.at[k],
        )
        for k, (w, at, size) in enumerate(cut)
    ]

    def back(k, go):
        w, at, size = cut[k]
        cols = pl.ds(at, size)
        into = [outs[far][w].at[:, :, cols] for far in range(2)]
        hand_back(place, stages[w].at[:, :, :, cols], into, hs.at[k], hr.at[k], go)

    def close(k, far):
        w, at, size = cut[k]
        total = sc[k].total(far)
        half = total.shape[0] // 2
        stages[w][far, 0, :, at : at + size] = total[:half]
        stages[w][far, 1, :, at : at + size] = total[half:]
        back(k, "far" if far else "near")

    def do_steps(steps):
        for what, k in steps:
            if what in "fc":
                close(k, int(what == "f"))
            else:
                getattr(sc[k], {"b": "begin", "s": "second", "t": "third"}[what])()

    sums[...] = jnp.zeros_like(sums)

    def add_sum(row, v):
        sums[row : row + 1] += jnp.sum(v, axis=0, keepdims=True)

    def span(start, count, step, body):
        chunks(count, step, lambda s: body(pl.ds(pl.multiple_of(start + s.start, step), step)))

    for copy in (*lay_l, *dz_l):
        copy.wait()
    for grp in range(2):
        live = lays[grp].T[:, 3:4]
        for part in range(4):
            rows = pl.ds(grp * n + part * (n // 4), n // 4)
            keep = live[part * (n // 4) : (part + 1) * (n // 4)]
            v = dz[rows, :].astype(F32) * keep
            dz[rows, :] = v.astype(BF)
            add_sum(5, v)
    g_l.wait()

    def down_grad(at, size):
        def body(rows):
            g2[rows, pl.ds(at, size)] = dot(g[:, rows], dz[:, pl.ds(at, size)], 0, 0).astype(BF)

        chunks(ff, 768, body)

    def hidden(cols):
        v = dot(dz[...], w2[cols, :], 1, 1) * du[:, cols].astype(F32)
        r = v.astype(BF)
        du[:, cols] = r
        line = jnp.sum(r.astype(F32), axis=0, keepdims=True)
        sums[pl.ds(6 + cols.start // d, 1), pl.ds(pl.multiple_of(lax.rem(cols.start, d), 128), 256)] = line

    pairs = HEADS // 2

    def turn(i):
        third = i // 3
        return 1 - lax.rem(third, 2), (third // 2) * 3 + lax.rem(i, 3)

    def fetch(i):
        grp, j = turn(i)
        src = (grp * pairs + j) * 2
        slot = lax.rem(i, 3)
        for half in range(2):
            yield pltpu.make_async_copy(
                p_i.at[src + half],
                w2.at[pl.ds(pl.multiple_of((slot * 2 + half) * n, n), n), pl.ds(0, n)],
                ps.at[slot, half],
            )

    def up_grad(cols):
        g1[:, cols] = dot(c[...], du[:, cols], 0, 0).astype(BF)

    def second_norm(rows):
        dc = dot(du[rows, :], w1[...], 1, 1)
        nhat, r = norm(y1[rows, :])
        add_sum(3, dc * nhat)
        add_sum(4, dc)
        first = dz[rows, :].astype(F32) + unnorm(dc, nhat, r, vec[3:4])
        y1[rows, :] = first
        low = first.astype(BF)
        c[rows, :] = low
        add_sum(2, low.astype(F32))

    def first_norm(rows):
        nhat, _ = norm(c[rows, :].astype(F32))
        dz[rows, :] = (nhat * vec[0:1] + vec[1:2]).astype(BF)

    def attention(start, stop, work):
        @pl.loop(start, stop)
        def _(i):
            grp, j = turn(i)
            rows = pl.ds(pl.multiple_of(grp * n, n), n)
            for copy in fetch(i):
                copy.wait()
            slot = lax.rem(i, 3)
            probs = [
                w2.at[pl.ds(pl.multiple_of((slot * 2 + half) * n, n), n), pl.ds(0, n)]
                for half in range(2)
            ]
            attend_back(qkv, rows, [p[...] for p in probs], do, ob, j, d)

            @pl.when(i + 3 < 2 * pairs)
            def _():
                for copy in fetch(i + 3):
                    copy.start()

            for at, steps in work.items():

                @pl.when(i == at)
                def _(steps=steps):
                    do_steps(steps)

    def input_grad(rows):
        da = dot(qkv[rows, :], w1[:, pl.ds(0, wide)], 1, 1)
        nhat, r = norm(c[rows, :].astype(F32))
        add_sum(0, da * nhat)
        add_sum(1, da)
        c[rows, :] = (y1[rows, :] + unnorm(da, nhat, r, vec[0:1])).astype(BF)

    def qkv_grad(side):
        cols = pl.ds(side * (wide // 2), wide // 2)
        gq[:, cols] = dot(dz[...], qkv[:, cols], 0, 0).astype(BF)

    hops = (place.sib, place.xn, place.yn, place.zn)

    def hop(i):
        return rcopy(os_.at[place.m], sgot.at[i], ts.at[i], tr.at[i], hops[i])

    def landed(i):
        hop(i).wait()
        os_[place.m] = os_[place.m] + sgot[i]

    down_grad(0, d // 2)
    do_steps([("b", DA)])
    down_grad(d // 2, d // 2)
    do_steps([("b", DB), ("s", DA)])
    w2_l.wait()
    du_l.wait()
    chunks(ff, 256, hidden)
    do_steps([("t", DA), ("s", DB)])
    for i in range(3):
        for copy in fetch(i):
            copy.start()
    c_l.wait()
    span(0, ff // 2, 768, up_grad)
    do_steps([("b", UA)])
    span(ff // 2, ff // 2, 768, up_grad)
    do_steps([("b", UB), ("f", DA), ("t", DB), ("s", UA)])
    w1_l.wait()
    y1_l.wait()
    chunks(2 * n, 256, second_norm)
    do_steps([("f", DB), ("t", UA), ("s", UB)])
    wq_l = load(wq_i, w1.at[:, pl.ds(0, wide)])
    o_l.wait()
    wp_l.wait()
    gp[...] = dot(ob[...], c[...], 0, 0).astype(BF)
    do_steps([("b", PR)])
    do[...] = dot(c[...], wp[...], 1, 1).astype(BF)
    x_l = (load(pat.at[place.m], c.at[pl.ds(0, n)]), load(x_i, c.at[pl.ds(n, n)]))
    for copy in x_l:
        copy.wait()
    chunks(2 * n, 256, first_norm)
    qkv_l.wait()
    attention(
        0,
        6,
        {
            2: [("c", DA), ("f", UA), ("t", UB), ("s", PR)],
            5: [("c", DB), ("f", UB), ("t", PR)],
        },
    )
    qkv_grad(0)
    do_steps([("b", QA)])
    attention(6, 9, {7: [("c", UA), ("f", PR), ("s", QA)]})
    wq_l.wait()
    span(n, n, 256, input_grad)
    acts[1].start()
    attention(9, 12, {9: [("c", UB), ("t", QA)], 11: [("c", PR)]})
    qkv_grad(1)
    do_steps([("b", QB)])
    span(0, n, 256, input_grad)
    pg_l = load(c.at[pl.ds(0, n)], pg_o.at[place.m])
    os_[place.m] = sums[...]
    hop(0).start()
    do_steps([("f", QA), ("s", QB)])
    landed(0)
    hop(1).start()
    do_steps([("t", QB)])
    landed(1)
    hop(2).start()
    do_steps([("c", QA), ("f", QB)])
    landed(2)
    hop(3).start()
    do_steps([("c", QB)])
    landed(3)
    last = rcopy(os_.at[place.m], os_.at[place.m], ts.at[4], tr.at[4], place.pair)
    last.start()
    for k in range(7):
        back(k, "recv")
        back(k, "send")
    last.wait_send()
    theirs = os_.at[1 - place.m]
    rcopy(theirs, theirs, ts.at[4], tr.at[4], place.pair).wait_recv()
    for act in acts:
        act.wait()
    enc_l.wait()
    pg_l.wait()


def backward(spread, pat, dog, *kept):
    any_, vm = pl.BlockSpec(memory_space=pl.ANY), pl.BlockSpec(memory_space=pltpu.VMEM)
    n, d = pat.shape[1:]
    wide, ff = kept[3].shape[1], kept[5].shape[1]
    lay = kept[2]
    shapes = ((48, wide), (48, d), (48, ff), (ff // 16, d))
    cuts = 2 * ((ff // 16, d // 2),) + 2 * ((48, ff // 2),) + ((48, d),) + 2 * ((48, wide // 2),)
    sd = jax.ShapeDtypeStruct
    out = 2 * [sd((2, r // 2, k), BF) for r, k in shapes]
    out += [sd((2, 16, d), F32), sd((2, n, d), BF), sd((2, n, d), BF)]
    dma = pltpu.SemaphoreType.DMA
    vmem = pltpu.VMEM
    return pl.pallas_call(
        functools.partial(backward_kernel, spread),
        out_shape=out,
        in_specs=[any_] * 9 + [vm] + [any_] * 8,
        out_specs=[any_] * 8 + [vm] + [any_] * 2,
        scratch_shapes=[
            vmem((ff, d), BF),
            vmem((d, ff), BF),
            vmem((d, d), BF),
            vmem((2 * n, wide), BF),
            vmem((2 * n, ff), BF),
            vmem((2 * n, ff), BF),
            vmem((2 * n, d), BF),
            vmem((2 * n, d), BF),
            vmem((2 * n, d), BF),
            vmem((2 * n, d), F32),
            vmem((2 * n, d), BF),
            vmem((ff, d), BF),
            vmem((d, d), BF),
            vmem(lay.shape, F32),
            vmem((16, d), F32),
        ]
        + [vmem((2, 4 * r, k), BF) for r, k in cuts]
        + [vmem((6, r, k), BF) for r, k in cuts]
        + [vmem((2, 2, r // 2, k), BF) for r, k in shapes]
        + [
            vmem((4, 16, d), F32),
            dma((7, 9)),
            dma((7, 9)),
            dma((7, 4)),
            dma((7, 4)),
            dma((2,)),
            dma((2,)),
            dma((5,)),
            dma((5,)),
            dma((18,)),
            dma((3, 2)),
        ],
        compiler_params=pltpu.CompilerParams(
            collective_id=1, has_side_effects=True, vmem_limit_bytes=62 * 2**20
        ),
        name="backward",
    )(pat, dog, *kept)


def finish_kernel(*refs):
    (pg, enc), near, far = refs[:2], refs[2:6], refs[6:10]
    (pg_o, enc_o), outs = refs[10:12], refs[12:16]
    pg_o[...] = pg[...].astype(F32)
    enc_o[...] = enc[...]

    @pl.when(pl.program_id(0) == 0)
    def _():
        for k, out in enumerate(outs):
            for m in range(2):
                total = near[k][m].astype(F32) + far[k][m].astype(F32)
                if k == 0:
                    width = total.shape[1] // 6
                    for at in range(6):
                        part, side = at // 2, at % 2
                        src = (side * 3 + part) * width
                        out[m, :, at * width : (at + 1) * width] = total[:, src : src + width]
                else:
                    out[m] = total


def finish(pg, enc, parts):
    n, d = pg.shape[1:]
    steps = 4
    tile = pl.BlockSpec((2, n // steps, d), lambda i: (0, i, 0))
    whole = [pl.BlockSpec(v.shape, lambda i: (0, 0, 0)) for v in parts]
    sd = jax.ShapeDtypeStruct
    return pl.pallas_call(
        finish_kernel,
        grid=(steps,),
        out_shape=[sd(pg.shape, F32), sd(enc.shape, BF)] + [sd(v.shape, F32) for v in parts[:4]],
        in_specs=[tile, tile] + whole,
        out_specs=[tile, tile] + whole[:4],
        compiler_params=pltpu.CompilerParams(vmem_limit_bytes=62 * 2**20),
        name="finish",
    )(pg, enc, *parts)


def local(
    count, patches, tile_kind, out_grad, n1g, n1b, wq, wp, bp, n2g, n2b, w1, b1, w2, b2
):
    spread = count // RING
    idx = lax.axis_index("fsdp")
    p = idx // spread
    rows, d = patches.shape[1:]
    parts = (n1g, n1b, bp, n2g, n2b, b2)
    if spread > 1:
        groups = [[q * spread + j for j in range(spread)] for q in range(RING)]
        ag = functools.partial(
            lax.all_gather, axis_name="fsdp", axis=1, tiled=True, axis_index_groups=groups
        )
        wq, wp, w1, w2, b1 = ag(wq), ag(wp), ag(w1), ag(w2), ag(b1)
        parts = tuple(ag(v) for v in parts)
    pat2, dog2, lay2, fq, fp, f1, f2, vecs, _, *saved = forward(
        spread, patches, out_grad, tile_kind, wq, wp, w1, w2, *parts, b1
    )
    *shares, os_, encoded, pgrad = backward(
        spread, patches, out_grad, pat2, dog2, lay2, fq, fp, f1, f2, vecs, *saved
    )
    pgrad, encoded, *grads = finish(pgrad, encoded, shares)
    seg = d // RING
    vec = lax.dynamic_slice_in_dim(os_[:, :6], p * seg, seg, axis=2)
    hid = os_[:, 6 : 6 + w2.shape[1] * RING // d].reshape(2, -1)
    hid = lax.dynamic_slice_in_dim(hid, p * w2.shape[1], w2.shape[1], axis=1)
    if spread > 1:
        rs = functools.partial(
            lax.psum_scatter, axis_name="fsdp", tiled=True, axis_index_groups=groups
        )
        grads = [rs(v, scatter_dimension=1) for v in grads]
        vec, hid = rs(vec, scatter_dimension=2), rs(hid, scatter_dimension=1)
    return (
        encoded,
        pgrad,
        vec[:, 0],
        vec[:, 1],
        grads[0],
        grads[1],
        vec[:, 2],
        vec[:, 3],
        vec[:, 4],
        grads[2],
        hid,
        grads[3],
        vec[:, 5],
    )


def solution(mesh):
    three, two = P(None, "fsdp", None), P(None, "fsdp")
    in_specs = (three, P("fsdp"), three, two, two, three, three, two, two, two, three, two, three, two)
    out_specs = (three, three, two, two, three, three, two, two, two, three, two, three, two)
    return jax.shard_map(
        functools.partial(local, mesh.shape["fsdp"]),
        mesh=mesh,
        in_specs=in_specs,
        out_specs=out_specs,
        check_vma=False,
    )
```

```python
import functools

import jax
import jax.numpy as jnp
from jax import lax
from jax.experimental import pallas as pl
from jax.experimental.pallas import tpu as pltpu
from jax.sharding import PartitionSpec as P

HEADS = 12
SIDE_S = 12
SIDE_M = 15
SIDE_L = 20
RING = 32
MESH = pl.DeviceIdType.MESH
BF = jnp.bfloat16
F32 = jnp.float32
FAR = 1e33


class Place:
    def __init__(self, spread):
        me = lax.axis_index("fsdp")
        self.rest = lax.rem(me, spread)
        self.spread = spread
        p = me // spread
        self.p = p
        self.c = lax.rem(p, 2)
        self.x = lax.rem(p // 2, 2)
        self.y = lax.rem(p // 4, 2)
        self.m = lax.rem(p // 8, 2)
        self.z = lax.rem(p // 16, 2)
        self.sib = self.at(c=1 - self.c)
        self.xn = self.at(x=1 - self.x)
        self.yn = self.at(y=1 - self.y)
        self.zn = self.at(z=1 - self.z)
        self.pair = self.at(m=1 - self.m)

    def at(self, **other):
        z, m, y, x, c = (other.get(k, getattr(self, k)) for k in "zmyxc")
        return ((((z * 2 + m) * 2 + y) * 2 + x) * 2 + c) * self.spread + self.rest,

    def chip(self, fz, fc, fy, fx):
        flip = lambda v, f: 1 - v if f else v
        return (
            (flip(self.z, fz) * 2 + flip(self.c, fc)) * 2 + flip(self.y, fy)
        ) * 2 + flip(self.x, fx)

    def greet(self):
        barrier = pltpu.get_barrier_semaphore()
        everyone = [self.sib, self.xn, self.yn, self.at(x=1 - self.x, y=1 - self.y)]
        for fz in range(2):
            for fm in range(2):
                for fc in range(2):
                    if fz or fm:
                        z, m, c = self.z, self.m, self.c
                        everyone.append(
                            self.at(
                                z=1 - z if fz else z, m=1 - m if fm else m, c=1 - c if fc else c
                            )
                        )
        for other in everyone:
            pl.semaphore_signal(barrier, inc=1, device_id=other, device_id_type=MESH)
        pl.semaphore_wait(barrier, len(everyone))


OWN, ZB, X0, X1, Y0, Y1, D0, D1 = range(8)
FLIPS = ((0, 0, 0), (1, 0, 0), (0, 0, 1), (1, 0, 1), (0, 1, 0), (1, 1, 0), (0, 1, 1), (1, 1, 1))


def rcopy(src, dst, ssem, rsem, dev):
    return pltpu.make_async_remote_copy(
        src_ref=src, dst_ref=dst, send_sem=ssem, recv_sem=rsem, device_id=dev, device_id_type=MESH
    )


class Gather:
    def __init__(self, place, full, rows, ssem, rsem):
        self.pl, self.full, self.rows, self.ssem, self.rsem = place, full, rows, ssem, rsem

    def block(self, kind, other=0):
        fz, fy, fx = FLIPS[kind]
        start = self.pl.chip(fz, other, fy, fx) * self.rows
        return self.full.at[pl.ds(pl.multiple_of(start, self.rows), self.rows)]

    def send(self, kind, way):
        place = self.pl
        if way == "s":
            dev, slot = place.sib, 8 + kind
        else:
            dev = {"x": place.xn, "y": place.yn}[way]
            fz, fy, fx = FLIPS[kind]
            flips = {"x": (fz, fy, 1 - fx), "y": (fz, 1 - fy, fx)}[way]
            slot = FLIPS.index(flips)
        view = self.block(kind)
        return rcopy(view, view, self.ssem.at[slot], self.rsem.at[slot], dev)

    AFTER = {
        OWN: "xys",
        ZB: "xys",
        X0: "ys",
        X1: "s",
        Y0: "s",
        Y1: "xs",
        D0: "s",
        D1: "s",
    }

    def start(self, kind):
        for way in self.AFTER[kind]:
            self.send(kind, way).start()

    def arrived(self, kind, other=0):
        view = self.block(kind, other)
        slot = kind + 8 * other
        rcopy(view, view, self.ssem.at[slot], self.rsem.at[slot], self.pl.sib).wait_recv()

    def finish(self):
        for kind in range(8):
            for way in self.AFTER[kind]:
                self.send(kind, way).wait_send()


def hand_in(place, shard, spot, ssem, rsem, go):
    def legs():
        for far in range(2):
            for fm in range(2):
                z = 1 - place.z if far else place.z
                m = 1 - place.m if fm else place.m
                yield far, fm, m, place.at(z=z, m=m, c=place.m)

    def copy(far, fm, m, dev):
        return rcopy(
            shard.at[m], spot(far, None), ssem.at[2 * far + fm], rsem.at[2 * far + place.c], dev
        )

    here = place.c == place.m
    if go == "start":
        for far, fm, m, dev in legs():
            if far or fm:
                copy(far, fm, m, dev).start()
            else:

                @pl.when(here)
                def _():
                    pltpu.make_async_copy(shard.at[m], spot(0, None), rsem.at[place.c]).start()

                @pl.when(jnp.logical_not(here))
                def _():
                    copy(far, fm, m, dev).start()

    elif go in ("near", "far"):
        far = int(go == "far")
        for piece in range(2):
            dst = spot(far, piece)
            rcopy(dst, dst, ssem.at[0], rsem.at[2 * far + piece], place.sib).wait_recv()
    else:
        for far, fm, m, dev in legs():
            if far or fm:
                copy(far, fm, m, dev).wait_send()
            else:

                @pl.when(jnp.logical_not(here))
                def _():
                    copy(far, fm, m, dev).wait_send()


def dot(a, b, ca, cb):
    return lax.dot_general(a, b, (((ca,), (cb,)), ((), ())), preferred_element_type=F32)


def chunks(count, step, body):
    @pl.loop(0, count // step)
    def _(i):
        body(pl.ds(pl.multiple_of(i * step, step), step))


def norm(v):
    center = v - jnp.mean(v, axis=-1, keepdims=True)
    r = lax.rsqrt(jnp.mean(center * center, axis=-1, keepdims=True) + 1e-06)
    return center * r, r


def fill_distance(dist, lay):
    across = lay[...]
    down = across.T
    gap_r = down[:, 1:2] - across[1:2]
    gap_c = down[:, 2:3] - across[2:3]
    far = jnp.sqrt(gap_r * gap_r + gap_c * gap_c)
    dist[...] = jnp.where(down[:, 0:1] == across[0:1], far, FAR)


STEP = 3


def lanes(half):
    return lax.broadcasted_iota(jnp.int32, (1, 128), 1) // 64 == half


def slope_of(head):
    return jnp.exp2(jnp.full((1, 1), -8.0 / HEADS, F32) * (head + 1).astype(F32))


def head_columns(j, d):
    pairs = HEADS // 4
    base = (j // pairs) * (3 * d // 2) + lax.rem(j, pairs) * 128
    return [pl.ds(pl.multiple_of(base + part * (d // 2), 128), 128) for part in range(3)]


def attend(qkv, rows, dist, pairs, prob, slot, o, d):
    zero = jnp.zeros((), BF)
    scores = []
    for j in pairs:
        cq, ck, _ = head_columns(j, d)
        q = qkv[rows, cq] * jnp.asarray(0.125, BF)
        k = qkv[rows, ck]
        scores.append([dot(k, jnp.where(lanes(half), q, zero), 1, 1) for half in range(2)])
    for at, j in enumerate(pairs):
        v = qkv[rows, head_columns(j, d)[2]]
        total = None
        for half in range(2):
            s = scores[at][half] - slope_of(2 * j + half) * dist
            e = jnp.exp(s - jnp.max(s, axis=0, keepdims=True))
            p = (e * (1.0 / jnp.sum(e, axis=0, keepdims=True))).astype(BF)
            prob[slot + 2 * at + half] = p
            part = dot(jnp.where(lanes(half), v, zero), p, 0, 0)
            total = part if total is None else total + part
        o[rows, pl.ds(pl.multiple_of(j * 128, 128), 128)] = total.T.astype(BF)


def fill_layout(lay, kinds, n):
    at = lax.broadcasted_iota(jnp.int32, (1, n), 1)
    slots = kinds.shape[0]
    segment, row, live = slots + at, at, jnp.zeros((1, n), jnp.int32)
    col = jnp.zeros((1, n), jnp.int32)
    start = jnp.int32(0)
    for slot in range(slots):
        kind = kinds[slot]
        side = jnp.where(kind == 0, SIDE_S, jnp.where(kind == 1, SIDE_M, SIDE_L))
        inverse = jnp.where(kind == 0, 1 / SIDE_S, jnp.where(kind == 1, 1 / SIDE_M, 1 / SIDE_L))
        end = start + side * side
        inside = (at >= start) & (at < end) & (end <= n)
        offset = at - start
        down = jnp.floor((offset.astype(F32) + 0.5) * inverse.astype(F32)).astype(jnp.int32)
        segment = jnp.where(inside, slot, segment)
        row = jnp.where(inside, down, row)
        col = jnp.where(inside, offset - down * side, col)
        live = jnp.where(inside, 1, live)
        start = end
    zero = jnp.zeros((4, n), F32)
    lay[...] = jnp.concatenate([v.astype(F32) for v in (segment, row, col, live)] + [zero], axis=0)


def forward_kernel(spread, *refs):
    (pat, dog, kinds, wq, wp, w1, w2) = refs[:7]
    vectors = refs[7:14]
    (x_o, dog_o, lay_o, wq_o, wp_o, w1_o, w2_o, vec_o, b1_o) = refs[14:23]
    (qkv_o, p_o, o_o, y1_o, c_o, g_o, gs_o, enc_o) = refs[23:31]
    (fq, fp, f1, f2, fs, gq, gp, g1) = refs[31:39]
    (lays, dist, xb, ac, qkv, prob, ob, y1, g, gs, smf, sm) = refs[39:51]
    (hs, hr, ss, rs, as_, ar, ls, ps) = refs[51:]
    place = Place(spread)
    d = xb.shape[2]
    n = xb.shape[1]
    ff = g.shape[1]
    smf[...] = jnp.zeros_like(smf)
    for at, ref in enumerate(vectors):
        both = ref[...].astype(F32)
        for m in range(2):
            smf[m, at : at + 1, 0 : both.shape[1]] = both[m : m + 1]
    for m in range(2):
        sm[m] = smf[m].astype(BF)
    place.greet()
    hand = ((sm, fs, None, 16), (wq, fq, gq, 24), (wp, fp, gp, 24), (w1, f1, g1, 24))
    hand += ((w2, f2, None, w2.shape[1]),)
    SM, QA, QB, PR, UA, UB, DA, DB = range(8)
    half = 3 * d // 2
    cut = (
        (0, fs),
        (1, fq.at[:, pl.ds(0, half)]),
        (1, fq.at[:, pl.ds(half, half)]),
        (2, fp),
        (3, f1.at[:, pl.ds(0, ff // 2)]),
        (3, f1.at[:, pl.ds(ff // 2, ff // 2)]),
        (4, f2.at[:, pl.ds(0, d // 2)]),
        (4, f2.at[:, pl.ds(d // 2, d // 2)]),
    )
    pieces = [
        Gather(place, view, 2 * hand[k][3], ss.at[i], rs.at[i]) for i, (k, view) in enumerate(cut)
    ]

    def spot_of(k):
        _, full, stage, rows = hand[k]

        def spot(far, piece):
            if stage is not None:
                return stage.at[far, place.c if piece is None else piece]
            at = place.p if piece is None else place.chip(far, 0, 0, 0) * 2 + piece
            return full.at[pl.ds(pl.multiple_of(at * rows, 16), rows)]

        return spot

    def hand_over(k, go):
        hand_in(place, hand[k][0], spot_of(k), hs.at[k], hr.at[k], go)

    def ready(k, far):
        hand_over(k, "far" if far else "near")
        _, full, stage, rows = hand[k]
        if stage is not None:
            start = pl.multiple_of(place.chip(far, 0, 0, 0) * (2 * rows), 2 * rows)

            def pack(src, dst):
                both = [stage[far, piece, :, src].astype(F32) for piece in range(2)]
                full[pl.ds(start, 2 * rows), dst] = jnp.concatenate(both, axis=0).astype(BF)

            if k == 1:
                for part in range(3):
                    for side in range(2):
                        pack(
                            pl.ds(part * d + side * (d // 2), d // 2),
                            pl.ds((side * 3 + part) * (d // 2), d // 2),
                        )
            else:
                pack(pl.ds(0, full.shape[1]), pl.ds(0, full.shape[1]))
        for i, (at, _) in enumerate(cut):
            if at == k:
                pieces[i].start(ZB if far else OWN)

    def pump(i, *kinds):
        for kind in kinds:
            pieces[i].arrived(kind)
            pieces[i].start(kind)

    def whole(i):
        for kind in range(8):
            pieces[i].arrived(kind, 1)

    saves = []

    def save(src, dst):
        copy = pltpu.make_async_copy(src, dst, ls.at[len(saves)])
        copy.start()
        saves.append(copy)
        return copy

    send_x = rcopy(pat.at[1 - place.m], xb.at[1], as_.at[0], ar.at[0], place.pair)
    send_dog = rcopy(dog.at[1 - place.m], dog_o, as_.at[1], ar.at[1], place.pair)
    send_lay = rcopy(lays.at[0], lays.at[1], as_.at[2], ar.at[2], place.pair)
    own_x = pltpu.make_async_copy(pat.at[place.m], xb.at[0], ps.at[0])
    own_x.start()
    FIRST = (X0, Y0)
    THEN = (X1, Y1)
    LAST = (D0, D1)

    def assemble():
        whole(SM)
        seg = d // RING
        hid = w2.shape[1]
        for q in range(RING):
            tile = fs[16 * q : 16 * q + 16].astype(F32)
            vec_o[0:8, seg * q : seg * q + seg] = tile[0:8, 0:seg]
            b1_o[0:1, hid * q : hid * q + hid] = tile[6:7, 0:hid]

    def first_norm(grp):
        def body(rows):
            nhat, _ = norm(xb[grp, rows, :].astype(F32))
            here = pl.ds(pl.multiple_of(grp * n + rows.start, 128), 128)
            ac[here, :] = (nhat * vec_o[0:1] + vec_o[1:2]).astype(BF)

        chunks(n, 128, body)

    def project(grp, side):
        cols = pl.ds(side * half, half)
        qkv[grp * n : grp * n + n, cols] = dot(ac[grp * n : grp * n + n], fq[:, cols], 1, 0).astype(BF)

    pairs = HEADS // 2

    def keep_prob(i):
        slots = pl.ds(i * STEP * 2, STEP * 2)
        return pltpu.make_async_copy(prob.at[slots], p_o.at[slots], ps.at[2 + i])

    def attention(start, stop, early):
        @pl.loop(start, stop)
        def _(i):
            grp, j = i // (pairs // STEP), lax.rem(i, pairs // STEP) * STEP
            rows = pl.ds(pl.multiple_of(grp * n, n), n)
            attend(qkv, rows, dist[grp], [j + k for k in range(STEP)], prob, 2 * STEP * i, ob, d)
            keep_prob(i).start()
            for at, steps in early.items():

                @pl.when(i == at)
                def _(steps=steps):
                    for step in steps:
                        if step[0] == "far":
                            ready(step[1], 1)
                        else:
                            pump(*step)

    def second_norm(rows):
        first = (
            xb[rows.start // n, pl.ds(pl.multiple_of(lax.rem(rows.start, n), 256), 256), :].astype(F32)
            + dot(ob[rows, :], fp[...], 1, 0)
            + vec_o[2:3]
        )
        y1[rows, :] = first
        nhat, _ = norm(first)
        ac[rows, :] = (nhat * vec_o[3:4] + vec_o[4:5]).astype(BF)

    def hidden(cols):
        u = dot(ac[...], f1[:, cols], 1, 0) + b1_o[0:1, cols]
        phi = 0.5 + 0.5 * lax.erf(u * 0.7071067811865476)
        g[:, cols] = (u * phi).astype(BF)
        gs[:, cols] = (phi + u * (0.3989422804014327 * jnp.exp(-0.5 * u * u))).astype(BF)

    def span(start, count, step, body):
        chunks(count, step, lambda s: body(pl.ds(pl.multiple_of(start + s.start, step), step)))

    def result(side):
        cols = pl.ds(side * (d // 2), d // 2)

        def body(rows):
            total = y1[rows, cols] + dot(g[rows, :], f2[:, cols], 1, 0) + vec_o[5:6, cols]
            qkv[rows, cols] = total.astype(BF)

        chunks(2 * n, 512, body)

    for k in range(5):
        hand_over(k, "start")
    fill_layout(lays.at[0], kinds, n)
    send_lay.start()
    send_x.start()
    fill_distance(dist.at[0], lays.at[0])
    for k in range(3):
        ready(k, 0)
    ready(0, 1)
    ready(1, 1)
    ready(3, 0)
    pump(SM, *FIRST)
    pump(QA, *FIRST)
    pump(QB, *FIRST)
    ready(4, 0)
    pump(SM, *THEN)
    pump(QA, *THEN)
    pump(QB, *THEN)
    ready(2, 1)
    pump(PR, *FIRST)
    pump(SM, *LAST)
    assemble()
    own_x.wait()
    first_norm(0)
    pump(QA, *LAST)
    pump(QB, *LAST)
    send_dog.start()
    whole(QA)
    project(0, 0)
    ready(3, 1)
    pump(UA, *FIRST)
    whole(QB)
    project(0, 1)
    pump(UB, *FIRST)
    pump(PR, *THEN)
    attention(0, 2, {0: [("far", 4), (UA, *THEN)], 1: [(UB, *THEN), (DA, *FIRST), (DB, *FIRST), (PR, *LAST)]})
    save(fq, wq_o)
    send_lay.wait_recv()
    fill_distance(dist.at[1], lays.at[1])
    send_x.wait_recv()
    first_norm(1)
    project(1, 0)
    project(1, 1)
    qkv_saved = save(qkv, qkv_o)
    save(xb.at[1], x_o)
    save(lays, lay_o)
    attention(2, 4, {2: [(DA, *THEN), (UA, *LAST)], 3: [(DB, *THEN), (UB, *LAST)]})
    save(ob, o_o)
    whole(PR)
    save(fp, wp_o)
    chunks(2 * n, 256, second_norm)
    save(y1, y1_o)
    save(ac, c_o)
    pump(DA, *LAST)
    whole(UA)
    span(0, ff // 2, 256, hidden)
    pump(DB, *LAST)
    whole(UB)
    save(f1, w1_o)
    span(ff // 2, ff // 2, 256, hidden)
    save(g, g_o)
    save(gs, gs_o)
    qkv_saved.wait()
    whole(DA)
    result(0)
    whole(DB)
    save(f2, w2_o)
    result(1)
    save(qkv.at[:, pl.ds(0, d)], enc_o)
    for k in range(5):
        hand_over(k, "send")
    for piece in pieces:
        piece.finish()
    send_x.wait_send()
    send_lay.wait_send()
    send_dog.wait()
    for i in range(2 * pairs // STEP):
        keep_prob(i).wait()
    for copy in saves:
        if copy is not qkv_saved:
            copy.wait()


def forward(spread, pat, dog, kinds, wq, wp, w1, w2, *vectors):
    any_, vm = pl.BlockSpec(memory_space=pl.ANY), pl.BlockSpec(memory_space=pltpu.VMEM)
    n, d = pat.shape[1:]
    ff = w2.shape[1] * RING
    sd = jax.ShapeDtypeStruct
    out = [
        sd((n, d), BF),
        sd((n, d), BF),
        sd((2, 8, n), F32),
        sd((d, wq.shape[2]), BF),
        sd((d, d), BF),
        sd((d, ff), BF),
        sd((ff, d), BF),
        sd((8, d), F32),
        sd((8, ff), F32),
        sd((2 * n, wq.shape[2]), BF),
        sd((2 * HEADS, n, n), BF),
        sd((2 * n, d), BF),
        sd((2 * n, d), F32),
        sd((2 * n, d), BF),
        sd((2 * n, ff), BF),
        sd((2 * n, ff), BF),
        sd((2 * n, d), BF),
    ]
    dma = pltpu.SemaphoreType.DMA
    vmem = pltpu.VMEM
    return pl.pallas_call(
        functools.partial(forward_kernel, spread),
        out_shape=out,
        in_specs=[any_] * 2 + [pl.BlockSpec(memory_space=pltpu.SMEM)] + [any_] * 4 + [vm] * 7,
        out_specs=[any_] * 7 + [vm] * 2 + [any_] * 8,
        scratch_shapes=[
            vmem((d, wq.shape[2]), BF),
            vmem((d, d), BF),
            vmem((d, ff), BF),
            vmem((ff, d), BF),
            vmem((RING * 16, 128), BF),
            vmem((2, 2, 24, wq.shape[2]), BF),
            vmem((2, 2, 24, d), BF),
            vmem((2, 2, 24, ff), BF),
            vmem((2, 8, n), F32),
            vmem((2, n, n), F32),
            vmem((2, n, d), BF),
            vmem((2 * n, d), BF),
            vmem((2 * n, wq.shape[2]), BF),
            vmem((2 * HEADS, n, n), BF),
            vmem((2 * n, d), BF),
            vmem((2 * n, d), F32),
            vmem((2 * n, ff), BF),
            vmem((2 * n, ff), BF),
            vmem((2, 16, 128), F32),
            vmem((2, 16, 128), BF),
            dma((5, 4)),
            dma((5, 4)),
            dma((8, 16)),
            dma((8, 16)),
            dma((3,)),
            dma((3,)),
            dma((16,)),
            dma((2 + HEADS,)),
        ],
        compiler_params=pltpu.CompilerParams(
            collective_id=0, has_side_effects=True, vmem_limit_bytes=62 * 2**20
        ),
        name="forward",
    )(pat, dog, kinds, wq, wp, w1, w2, *vectors)


class Scatter:
    def __init__(self, place, full, rows, got_sib, got, ssem, rsem):
        self.pl, self.full, self.rows = place, full, rows
        self.got_sib, self.got, self.ssem, self.rsem = got_sib, got, ssem, rsem

    def start_of(self, kind):
        fz, fy, fx = FLIPS[kind]
        return pl.multiple_of(self.pl.chip(fz, 0, fy, fx) * self.rows, self.rows)

    def plane(self, z, other):
        c = 1 - self.pl.c if other else self.pl.c
        return pl.ds(pl.multiple_of((z * 2 + c) * (4 * self.rows), self.rows), 4 * self.rows)

    def sib(self, z):
        return rcopy(
            self.full.at[self.plane(z, 1)],
            self.got_sib.at[z],
            self.ssem.at[z],
            self.rsem.at[z],
            self.pl.sib,
        )

    MOVES = {D0: ("y", 0), D1: ("x", 1), X0: ("x", 2), X1: ("x", 3), Y0: ("y", 4), Y1: ("y", 5)}

    def move(self, kind):
        way, slot = self.MOVES[kind]
        dev = {"x": self.pl.xn, "y": self.pl.yn}[way]
        return rcopy(
            self.full.at[pl.ds(self.start_of(kind), self.rows)],
            self.got.at[slot],
            self.ssem.at[2 + slot],
            self.rsem.at[2 + slot],
            dev,
        )

    def add(self, kind, slot):
        rows = pl.ds(self.start_of(kind), self.rows)
        self.full[rows, :] = self.full[rows, :] + self.got[slot]

    def begin(self):
        self.sib(0).start()
        self.sib(1).start()

    def second(self):
        for z in range(2):
            self.sib(z).wait()
        step = 16

        for z in range(2):
            base = (z * 2 + self.pl.c) * (4 * self.rows)

            @pl.loop(0, 4 * self.rows // step)
            def _(i, z=z, base=base):
                rows = pl.ds(pl.multiple_of(base + i * step, step), step)
                theirs = self.got_sib[z, pl.ds(pl.multiple_of(i * step, step), step), :]
                self.full[rows, :] = self.full[rows, :] + theirs

        for kind in (D0, D1, X1, Y0):
            self.move(kind).start()

    def third(self):
        self.move(D0).wait()
        self.add(X0, 0)
        self.move(X0).start()
        self.move(D1).wait()
        self.add(Y1, 1)
        self.move(Y1).start()

    def total(self, far):
        kind, slots = (ZB, (X1, Y1)) if far else (OWN, (X0, Y0))
        rows = pl.ds(self.start_of(kind), self.rows)
        total = self.full[rows, :].astype(F32)
        for move in slots:
            self.move(move).wait()
            total = total + self.got[self.MOVES[move][1]].astype(F32)
        return total.astype(BF)


def hand_back(place, stage, outs, ssem, rsem, go):
    def leg(far, k):
        z = 1 - place.z if far else place.z
        return rcopy(
            stage.at[far, k],
            outs[far].at[place.m],
            ssem.at[2 * far + k],
            rsem.at[2 * far + place.m],
            place.at(z=z, m=place.c, c=k),
        )

    def each(far, k, local, remote):
        if far:
            remote()
        else:
            here = jnp.logical_and(place.c == place.m, place.c == k)
            pl.when(here)(local)
            pl.when(jnp.logical_not(here))(remote)

    if go in ("near", "far"):
        far = int(go == "far")
        for k in range(2):

            def local(k=k):
                pltpu.make_async_copy(
                    stage.at[0, k], outs[0].at[place.m], rsem.at[place.m]
                ).start()

            each(far, k, local, lambda k=k: leg(far, k).start())
    elif go == "recv":
        for far in range(2):
            for m in range(2):
                dst = outs[far].at[m]
                rcopy(dst, dst, ssem.at[0], rsem.at[2 * far + m], place.sib).wait_recv()
    else:
        for far in range(2):
            for k in range(2):
                each(far, k, lambda: None, lambda far=far, k=k: leg(far, k).wait_send())


def unnorm(dn, nhat, r, gain):
    dh = dn * gain
    return r * (
        dh - jnp.mean(dh, axis=-1, keepdims=True) - nhat * jnp.mean(dh * nhat, axis=-1, keepdims=True)
    )


def attend_back(qkv, rows, probs, do, o, j, d):
    col = pl.multiple_of(j * 128, 128)
    eighth = jnp.asarray(0.125, BF)
    zero = jnp.zeros((), BF)
    cq, ck, cv = head_columns(j, d)
    q, k, v = qkv[rows, cq], qkv[rows, ck], qkv[rows, cv]
    g = do[rows, pl.ds(col, 128)]
    both = g.astype(F32) * o[rows, pl.ds(col, 128)].astype(F32)
    dq = dk = dv = 0.0
    for half in range(2):
        keep = lanes(half)
        p = probs[half]
        gm = jnp.where(keep, g, zero)
        centre = jnp.sum(jnp.where(keep, both, 0.0), axis=1, keepdims=True)
        centre = jnp.broadcast_to(centre, (both.shape[0], 128)).T[0:1]
        ds = (p.astype(F32) * (dot(v, gm, 1, 1) - centre)).astype(BF)
        dk = dk + dot(ds, jnp.where(keep, q * eighth, zero), 1, 0)
        dv = dv + dot(p, gm, 1, 0)
        dq = dq + dot(jnp.where(keep, k * eighth, zero), ds, 0, 0)
    qkv[rows, cq] = dq.T.astype(BF)
    qkv[rows, ck] = dk.astype(BF)
    qkv[rows, cv] = dv.astype(BF)


def backward_kernel(spread, *refs):
    (pat, dog, x_i, dog_i, lay_i, wq_i, wp_i, w1_i, w2_i, vec) = refs[:10]
    (qkv_i, p_i, o_i, y1_i, c_i, g_i, gs_i, y_i) = refs[10:18]
    outs = (refs[18:22], refs[22:26])
    (os_, enc_o, pg_o) = refs[26:29]
    (w2, w1, wp, qkv, g, du, c, ob, dz, y1, do, g2, gp, lays, sums) = refs[29:44]
    got_sib, got, stages = refs[44:51], refs[51:58], refs[58:62]
    (sgot, ss, rs, hs, hr, es, er, ts, tr, ls, ps) = refs[62:]
    place = Place(spread)
    n, d = c.shape[0] // 2, c.shape[1]
    ff = w1.shape[1]
    wide = qkv.shape[1]
    loads = []

    def load(src, dst):
        copy = pltpu.make_async_copy(src, dst, ls.at[len(loads)])
        copy.start()
        loads.append(copy)
        return copy

    lay_l = (load(lay_i, lays),)
    dz_l = (
        load(dog.at[place.m], dz.at[pl.ds(0, n)]),
        load(dog_i, dz.at[pl.ds(n, n)]),
    )
    g_l = load(g_i, g)
    w2_l = load(w2_i, w2)
    du_l = load(gs_i, du)
    c_l = load(c_i, c)
    w1_l = load(w1_i, w1)
    y1_l = load(y1_i, y1)
    o_l = load(o_i, ob)
    wp_l = load(wp_i, wp)
    qkv_l = load(qkv_i, qkv)
    place.greet()
    acts = [
        rcopy(y_i.at[pl.ds(n, n)], enc_o.at[place.m], es.at[0], er.at[0], place.pair),
        rcopy(c.at[pl.ds(n, n)], pg_o.at[place.m], es.at[1], er.at[1], place.pair),
    ]
    enc_l = load(y_i.at[pl.ds(0, n)], enc_o.at[place.m])
    acts[0].start()
    gq = du.at[pl.ds(0, d), pl.ds(0, wide)]
    g1 = g.at[pl.ds(0, d)]
    DA, DB, UA, UB, PR, QA, QB = range(7)
    cut = (
        (3, 0, d // 2),
        (3, d // 2, d // 2),
        (2, 0, ff // 2),
        (2, ff // 2, ff // 2),
        (1, 0, d),
        (0, 0, wide // 2),
        (0, wide // 2, wide // 2),
    )
    fulls = (gq, gp, g1, g2)
    sc = [
        Scatter(
            place,
            fulls[w].at[:, pl.ds(at, size)],
            fulls[w].shape[0] // 16,
            got_sib[k],
            got[k],
            ss.at[k],
            rs.at[k],
        )
        for k, (w, at, size) in enumerate(cut)
    ]

    def back(k, go):
        w, at, size = cut[k]
        cols = pl.ds(at, size)
        into = [outs[far][w].at[:, :, cols] for far in range(2)]
        hand_back(place, stages[w].at[:, :, :, cols], into, hs.at[k], hr.at[k], go)

    def close(k, far):
        w, at, size = cut[k]
        total = sc[k].total(far)
        half = total.shape[0] // 2
        stages[w][far, 0, :, at : at + size] = total[:half]
        stages[w][far, 1, :, at : at + size] = total[half:]
        back(k, "far" if far else "near")

    def do_steps(steps):
        for what, k in steps:
            if what in "fc":
                close(k, int(what == "f"))
            else:
                getattr(sc[k], {"b": "begin", "s": "second", "t": "third"}[what])()

    sums[...] = jnp.zeros_like(sums)

    def add_sum(row, v):
        sums[row : row + 1] += jnp.sum(v, axis=0, keepdims=True)

    def span(start, count, step, body):
        chunks(count, step, lambda s: body(pl.ds(pl.multiple_of(start + s.start, step), step)))

    for copy in (*lay_l, *dz_l):
        copy.wait()
    for grp in range(2):
        live = lays[grp].T[:, 3:4]
        for part in range(4):
            rows = pl.ds(grp * n + part * (n // 4), n // 4)
            keep = live[part * (n // 4) : (part + 1) * (n // 4)]
            v = dz[rows, :].astype(F32) * keep
            dz[rows, :] = v.astype(BF)
            add_sum(5, v)
    g_l.wait()

    def down_grad(at, size):
        def body(rows):
            g2[rows, pl.ds(at, size)] = dot(g[:, rows], dz[:, pl.ds(at, size)], 0, 0).astype(BF)

        chunks(ff, 768, body)

    def hidden(cols):
        v = dot(dz[...], w2[cols, :], 1, 1) * du[:, cols].astype(F32)
        r = v.astype(BF)
        du[:, cols] = r
        line = jnp.sum(r.astype(F32), axis=0, keepdims=True)
        sums[pl.ds(6 + cols.start // d, 1), pl.ds(pl.multiple_of(lax.rem(cols.start, d), 128), 256)] = line

    pairs = HEADS // 2

    def turn(i):
        return 1 - i // pairs, lax.rem(i, pairs)

    def fetch(i):
        grp, j = turn(i)
        src = (grp * pairs + j) * 2
        slot = lax.rem(i, 3)
        for half in range(2):
            yield pltpu.make_async_copy(
                p_i.at[src + half],
                w2.at[pl.ds(pl.multiple_of((slot * 2 + half) * n, n), n), pl.ds(0, n)],
                ps.at[slot, half],
            )

    def up_grad(cols):
        g1[:, cols] = dot(c[...], du[:, cols], 0, 0).astype(BF)

    def second_norm(rows):
        dc = dot(du[rows, :], w1[...], 1, 1)
        nhat, r = norm(y1[rows, :])
        add_sum(3, dc * nhat)
        add_sum(4, dc)
        first = dz[rows, :].astype(F32) + unnorm(dc, nhat, r, vec[3:4])
        y1[rows, :] = first
        low = first.astype(BF)
        c[rows, :] = low
        add_sum(2, low.astype(F32))

    def first_norm(rows):
        nhat, _ = norm(c[rows, :].astype(F32))
        dz[rows, :] = (nhat * vec[0:1] + vec[1:2]).astype(BF)

    def attention(start, stop, work):
        @pl.loop(start, stop)
        def _(i):
            grp, j = turn(i)
            rows = pl.ds(pl.multiple_of(grp * n, n), n)
            for copy in fetch(i):
                copy.wait()
            slot = lax.rem(i, 3)
            probs = [
                w2.at[pl.ds(pl.multiple_of((slot * 2 + half) * n, n), n), pl.ds(0, n)]
                for half in range(2)
            ]
            attend_back(qkv, rows, [p[...] for p in probs], do, ob, j, d)

            @pl.when(i + 3 < 2 * pairs)
            def _():
                for copy in fetch(i + 3):
                    copy.start()

            for at, steps in work.items():

                @pl.when(i == at)
                def _(steps=steps):
                    do_steps(steps)

    def input_grad(rows):
        da = dot(qkv[rows, :], w1[:, pl.ds(0, wide)], 1, 1)
        nhat, r = norm(c[rows, :].astype(F32))
        add_sum(0, da * nhat)
        add_sum(1, da)
        c[rows, :] = (y1[rows, :] + unnorm(da, nhat, r, vec[0:1])).astype(BF)

    def qkv_grad(k):
        cols = pl.ds(cut[k][1], cut[k][2])
        gq[:, cols] = dot(dz[...], qkv[:, cols], 0, 0).astype(BF)

    around = (place.sib, place.xn, place.yn, place.at(x=1 - place.x, y=1 - place.y))
    beyond = (
        (place.zn, 1),
        (place.pair, 0),
        (place.at(z=1 - place.z, m=1 - place.m), 1),
    )

    def hop(i):
        return rcopy(sums, sgot.at[0], ts.at[0], tr.at[0], around[0]) if i == 0 else rcopy(
            sgot.at[4], sgot.at[i], ts.at[i], tr.at[i], around[i]
        )

    def leap(i):
        dev, far = beyond[i]
        return rcopy(os_.at[0, place.m], os_.at[far, place.m], ts.at[4 + i], tr.at[4 + i], dev)

    def small(step):
        if step == 0:
            hop(0).start()
        elif step == 1:
            hop(0).wait()
            sgot[4] = sums[...] + sgot[0]
            for i in range(1, 4):
                hop(i).start()
        elif step == 2:
            for i in range(1, 4):
                hop(i).wait()
            os_[0, place.m] = (sgot[4] + sgot[1]) + (sgot[2] + sgot[3])
            for i in range(3):
                leap(i).start()
        else:
            for i, (far, m) in enumerate(((1, place.m), (0, 1 - place.m), (1, 1 - place.m))):
                leap(i).wait_send()
                view = os_.at[far, m]
                rcopy(view, view, ts.at[4 + i], tr.at[4 + i], place.zn).wait_recv()

    down_grad(0, d // 2)
    do_steps([("b", DA)])
    down_grad(d // 2, d // 2)
    do_steps([("b", DB), ("s", DA)])
    w2_l.wait()
    du_l.wait()
    chunks(ff, 256, hidden)
    do_steps([("t", DA), ("s", DB)])
    for i in range(3):
        for copy in fetch(i):
            copy.start()
    c_l.wait()
    span(0, ff // 2, 768, up_grad)
    do_steps([("b", UA)])
    span(ff // 2, ff // 2, 768, up_grad)
    do_steps([("b", UB), ("f", DA), ("t", DB), ("s", UA)])
    w1_l.wait()
    y1_l.wait()
    chunks(2 * n, 256, second_norm)
    do_steps([("f", DB), ("t", UA), ("s", UB)])
    wq_l = load(wq_i, w1.at[:, pl.ds(0, wide)])
    o_l.wait()
    wp_l.wait()
    gp[...] = dot(ob[...], c[...], 0, 0).astype(BF)
    do_steps([("b", PR)])
    do[...] = dot(c[...], wp[...], 1, 1).astype(BF)
    x_l = (load(pat.at[place.m], c.at[pl.ds(0, n)]), load(x_i, c.at[pl.ds(n, n)]))
    for copy in x_l:
        copy.wait()
    chunks(2 * n, 256, first_norm)
    qkv_l.wait()
    attention(0, 6, {1: [("s", PR)], 3: [("c", DA), ("f", UA), ("t", UB)]})
    wq_l.wait()
    span(n, n, 256, input_grad)
    acts[1].start()
    do_steps([("t", PR)])
    do_steps([("c", DB)])
    do_steps([("f", UB)])
    attention(6, 9, {7: [("c", UA), ("f", PR)], 8: [("c", UB), ("c", PR)]})
    qkv_grad(QA)
    do_steps([("b", QA)])
    attention(9, 12, {9: [("s", QA)], 11: [("t", QA)]})
    qkv_grad(QB)
    do_steps([("b", QB)])
    span(0, n, 256, input_grad)
    pg_l = load(c.at[pl.ds(0, n)], pg_o.at[place.m])
    small(0)
    do_steps([("s", QB)])
    do_steps([("f", QA)])
    do_steps([("c", QA)])
    small(1)
    do_steps([("t", QB)])
    small(2)
    do_steps([("f", QB)])
    do_steps([("c", QB)])
    for k in range(7):
        back(k, "recv")
        back(k, "send")
    small(3)
    for act in acts:
        act.wait()
    enc_l.wait()
    pg_l.wait()


def backward(spread, pat, dog, *kept):
    any_, vm = pl.BlockSpec(memory_space=pl.ANY), pl.BlockSpec(memory_space=pltpu.VMEM)
    n, d = pat.shape[1:]
    wide, ff = kept[3].shape[1], kept[5].shape[1]
    lay = kept[2]
    shapes = ((48, wide), (48, d), (48, ff), (ff // 16, d))
    cuts = 2 * ((ff // 16, d // 2),) + 2 * ((48, ff // 2),) + ((48, d),) + 2 * ((48, wide // 2),)
    sd = jax.ShapeDtypeStruct
    out = 2 * [sd((2, r // 2, k), BF) for r, k in shapes]
    out += [sd((2, 2, 16, d), F32), sd((2, n, d), BF), sd((2, n, d), BF)]
    dma = pltpu.SemaphoreType.DMA
    vmem = pltpu.VMEM
    return pl.pallas_call(
        functools.partial(backward_kernel, spread),
        out_shape=out,
        in_specs=[any_] * 9 + [vm] + [any_] * 8,
        out_specs=[any_] * 8 + [vm] + [any_] * 2,
        scratch_shapes=[
            vmem((ff, d), BF),
            vmem((d, ff), BF),
            vmem((d, d), BF),
            vmem((2 * n, wide), BF),
            vmem((2 * n, ff), BF),
            vmem((2 * n, ff), BF),
            vmem((2 * n, d), BF),
            vmem((2 * n, d), BF),
            vmem((2 * n, d), BF),
            vmem((2 * n, d), F32),
            vmem((2 * n, d), BF),
            vmem((ff, d), BF),
            vmem((d, d), BF),
            vmem(lay.shape, F32),
            vmem((16, d), F32),
        ]
        + [vmem((2, 4 * r, k), BF) for r, k in cuts]
        + [vmem((6, r, k), BF) for r, k in cuts]
        + [vmem((2, 2, r // 2, k), BF) for r, k in shapes]
        + [
            vmem((5, 16, d), F32),
            dma((7, 9)),
            dma((7, 9)),
            dma((7, 4)),
            dma((7, 4)),
            dma((2,)),
            dma((2,)),
            dma((7,)),
            dma((7,)),
            dma((18,)),
            dma((3, 2)),
        ],
        compiler_params=pltpu.CompilerParams(
            collective_id=1, has_side_effects=True, vmem_limit_bytes=62 * 2**20
        ),
        name="backward",
    )(pat, dog, *kept)


def finish_kernel(spread, *refs):
    (pg, enc), near, far = refs[:2], refs[2:6], refs[6:10]
    small, (pg_o, enc_o), outs = refs[10], refs[11:13], refs[13:17]
    vecs, hid_o = refs[17:23], refs[23]
    pg_o[...] = pg[...].astype(F32)
    enc_o[...] = enc[...]

    @pl.when(pl.program_id(0) == 0)
    def _():
        for k, out in enumerate(outs):
            for m in range(2):
                total = near[k][m].astype(F32) + far[k][m].astype(F32)
                if k == 0:
                    width = total.shape[1] // 6
                    for at in range(6):
                        part, side = at // 2, at % 2
                        src = (side * 3 + part) * width
                        out[m, :, at * width : (at + 1) * width] = total[:, src : src + width]
                else:
                    out[m] = total
        p = lax.axis_index("fsdp") // spread
        d, seg, hid = small.shape[3], vecs[0].shape[1], hid_o.shape[1]
        per = d // hid
        for m in range(2):
            both = small[0, m] + small[1, m]
            both = pltpu.roll(both, d - p * seg, 1)
            for k, out in enumerate(vecs):
                out[m : m + 1] = both[k : k + 1, 0:seg]
            row = pl.ds(6 + p // per, 1)
            line = small[0, m, row, :] + small[1, m, row, :]
            hid_o[m : m + 1] = pltpu.roll(line, d - lax.rem(p, per) * hid, 1)[:, 0:hid]


def finish(spread, pg, enc, parts, small, hid):
    n, d = pg.shape[1:]
    steps = 4
    tile = pl.BlockSpec((2, n // steps, d), lambda i: (0, i, 0))
    whole = [pl.BlockSpec(v.shape, lambda i: (0, 0, 0)) for v in parts]
    sd = jax.ShapeDtypeStruct
    return pl.pallas_call(
        functools.partial(finish_kernel, spread),
        grid=(steps,),
        out_shape=[sd(pg.shape, F32), sd(enc.shape, BF)]
        + [sd(v.shape, F32) for v in parts[:4]]
        + [sd((2, d // RING), F32)] * 6
        + [sd((2, hid), F32)],
        in_specs=[tile, tile] + whole + [pl.BlockSpec(small.shape, lambda i: (0, 0, 0, 0))],
        out_specs=[tile, tile]
        + whole[:4]
        + [pl.BlockSpec((2, d // RING), lambda i: (0, 0))] * 6
        + [pl.BlockSpec((2, hid), lambda i: (0, 0))],
        compiler_params=pltpu.CompilerParams(vmem_limit_bytes=62 * 2**20),
        name="finish",
    )(pg, enc, *parts, small)


def local(
    count, patches, tile_kind, out_grad, n1g, n1b, wq, wp, bp, n2g, n2b, w1, b1, w2, b2
):
    spread = count // RING
    idx = lax.axis_index("fsdp")
    p = idx // spread
    rows, d = patches.shape[1:]
    parts = (n1g, n1b, bp, n2g, n2b, b2)
    if spread > 1:
        groups = [[q * spread + j for j in range(spread)] for q in range(RING)]
        ag = functools.partial(
            lax.all_gather, axis_name="fsdp", axis=1, tiled=True, axis_index_groups=groups
        )
        wq, wp, w1, w2, b1 = ag(wq), ag(wp), ag(w1), ag(w2), ag(b1)
        parts = tuple(ag(v) for v in parts)
    pat2, dog2, lay2, fq, fp, f1, f2, vecs, _, *saved = forward(
        spread, patches, out_grad, tile_kind, wq, wp, w1, w2, *parts, b1
    )
    *shares, os_, encoded, pgrad = backward(
        spread, patches, out_grad, pat2, dog2, lay2, fq, fp, f1, f2, vecs, *saved
    )
    pgrad, encoded, *grads, hid = finish(
        spread, pgrad, encoded, shares, os_, w2.shape[1]
    )
    grads, vec = grads[:4], grads[4:]
    if spread > 1:
        rs = functools.partial(
            lax.psum_scatter,
            axis_name="fsdp",
            scatter_dimension=1,
            tiled=True,
            axis_index_groups=groups,
        )
        grads, vec, hid = [rs(v) for v in grads], [rs(v) for v in vec], rs(hid)
    return (
        encoded,
        pgrad,
        vec[0],
        vec[1],
        grads[0],
        grads[1],
        vec[2],
        vec[3],
        vec[4],
        grads[2],
        hid,
        grads[3],
        vec[5],
    )


def solution(mesh):
    three, two = P(None, "fsdp", None), P(None, "fsdp")
    in_specs = (three, P("fsdp"), three, two, two, three, three, two, two, two, three, two, three, two)
    out_specs = (three, three, two, two, three, three, two, two, two, three, two, three, two)
    return jax.shard_map(
        functools.partial(local, mesh.shape["fsdp"]),
        mesh=mesh,
        in_specs=in_specs,
        out_specs=out_specs,
        check_vma=False,
    )
```

```python
import functools

import jax
import jax.numpy as jnp
from jax import lax
from jax.experimental import pallas as pl
from jax.experimental.pallas import tpu as pltpu
from jax.sharding import PartitionSpec as P

HEADS = 12
SIDE_S = 12
SIDE_M = 15
SIDE_L = 20
RING = 32
MESH = pl.DeviceIdType.MESH
BF = jnp.bfloat16
F32 = jnp.float32
FAR = 1e33


class Place:
    def __init__(self, spread):
        me = lax.axis_index("fsdp")
        self.rest = lax.rem(me, spread)
        self.spread = spread
        p = me // spread
        self.p = p
        self.c = lax.rem(p, 2)
        self.x = lax.rem(p // 2, 2)
        self.y = lax.rem(p // 4, 2)
        self.m = lax.rem(p // 8, 2)
        self.z = lax.rem(p // 16, 2)
        self.sib = self.at(c=1 - self.c)
        self.xn = self.at(x=1 - self.x)
        self.yn = self.at(y=1 - self.y)
        self.zn = self.at(z=1 - self.z)
        self.pair = self.at(m=1 - self.m)

    def at(self, **other):
        z, m, y, x, c = (other.get(k, getattr(self, k)) for k in "zmyxc")
        return ((((z * 2 + m) * 2 + y) * 2 + x) * 2 + c) * self.spread + self.rest,

    def chip(self, fz, fc, fy, fx):
        flip = lambda v, f: 1 - v if f else v
        return (
            (flip(self.z, fz) * 2 + flip(self.c, fc)) * 2 + flip(self.y, fy)
        ) * 2 + flip(self.x, fx)

    def greet(self):
        barrier = pltpu.get_barrier_semaphore()
        everyone = [self.sib, self.xn, self.yn, self.at(x=1 - self.x, y=1 - self.y)]
        for fz in range(2):
            for fm in range(2):
                for fc in range(2):
                    if fz or fm:
                        z, m, c = self.z, self.m, self.c
                        everyone.append(
                            self.at(
                                z=1 - z if fz else z, m=1 - m if fm else m, c=1 - c if fc else c
                            )
                        )
        for other in everyone:
            pl.semaphore_signal(barrier, inc=1, device_id=other, device_id_type=MESH)
        pl.semaphore_wait(barrier, len(everyone))


OWN, ZB, X0, X1, Y0, Y1, D0, D1 = range(8)
FLIPS = ((0, 0, 0), (1, 0, 0), (0, 0, 1), (1, 0, 1), (0, 1, 0), (1, 1, 0), (0, 1, 1), (1, 1, 1))


def rcopy(src, dst, ssem, rsem, dev):
    return pltpu.make_async_remote_copy(
        src_ref=src, dst_ref=dst, send_sem=ssem, recv_sem=rsem, device_id=dev, device_id_type=MESH
    )


class Gather:
    def __init__(self, place, full, rows, ssem, rsem):
        self.pl, self.full, self.rows, self.ssem, self.rsem = place, full, rows, ssem, rsem

    def block(self, kind, other=0):
        fz, fy, fx = FLIPS[kind]
        start = self.pl.chip(fz, other, fy, fx) * self.rows
        return self.full.at[pl.ds(pl.multiple_of(start, self.rows), self.rows)]

    def send(self, kind, way):
        place = self.pl
        if way == "s":
            dev, slot = place.sib, 8 + kind
        else:
            dev = {"x": place.xn, "y": place.yn}[way]
            fz, fy, fx = FLIPS[kind]
            flips = {"x": (fz, fy, 1 - fx), "y": (fz, 1 - fy, fx)}[way]
            slot = FLIPS.index(flips)
        view = self.block(kind)
        return rcopy(view, view, self.ssem.at[slot], self.rsem.at[slot], dev)

    AFTER = {
        OWN: "xys",
        ZB: "xys",
        X0: "ys",
        X1: "s",
        Y0: "s",
        Y1: "xs",
        D0: "s",
        D1: "s",
    }

    def start(self, kind):
        for way in self.AFTER[kind]:
            self.send(kind, way).start()

    def arrived(self, kind, other=0):
        view = self.block(kind, other)
        slot = kind + 8 * other
        rcopy(view, view, self.ssem.at[slot], self.rsem.at[slot], self.pl.sib).wait_recv()

    def finish(self):
        for kind in range(8):
            for way in self.AFTER[kind]:
                self.send(kind, way).wait_send()


def hand_in(place, shard, spot, ssem, rsem, go):
    def legs():
        for far in range(2):
            for fm in range(2):
                z = 1 - place.z if far else place.z
                m = 1 - place.m if fm else place.m
                yield far, fm, m, place.at(z=z, m=m, c=place.m)

    def copy(far, fm, m, dev):
        return rcopy(
            shard.at[m], spot(far, None), ssem.at[2 * far + fm], rsem.at[2 * far + place.c], dev
        )

    here = place.c == place.m
    if go == "start":
        for far, fm, m, dev in legs():
            if far or fm:
                copy(far, fm, m, dev).start()
            else:

                @pl.when(here)
                def _():
                    pltpu.make_async_copy(shard.at[m], spot(0, None), rsem.at[place.c]).start()

                @pl.when(jnp.logical_not(here))
                def _():
                    copy(far, fm, m, dev).start()

    elif go in ("near", "far"):
        far = int(go == "far")
        for piece in range(2):
            dst = spot(far, piece)
            rcopy(dst, dst, ssem.at[0], rsem.at[2 * far + piece], place.sib).wait_recv()
    else:
        for far, fm, m, dev in legs():
            if far or fm:
                copy(far, fm, m, dev).wait_send()
            else:

                @pl.when(jnp.logical_not(here))
                def _():
                    copy(far, fm, m, dev).wait_send()


def dot(a, b, ca, cb):
    return lax.dot_general(a, b, (((ca,), (cb,)), ((), ())), preferred_element_type=F32)


def chunks(count, step, body):
    @pl.loop(0, count // step)
    def _(i):
        body(pl.ds(pl.multiple_of(i * step, step), step))


def norm(v):
    center = v - jnp.mean(v, axis=-1, keepdims=True)
    r = lax.rsqrt(jnp.mean(center * center, axis=-1, keepdims=True) + 1e-06)
    return center * r, r


def fill_distance(dist, lay):
    across = lay[...]
    down = across.T
    gap_r = down[:, 1:2] - across[1:2]
    gap_c = down[:, 2:3] - across[2:3]
    far = jnp.sqrt(gap_r * gap_r + gap_c * gap_c)
    dist[...] = jnp.where(down[:, 0:1] == across[0:1], far, FAR)


STEP = 3


def lanes(half):
    return lax.broadcasted_iota(jnp.int32, (1, 128), 1) // 64 == half


def slope_of(head):
    return jnp.exp2(jnp.full((1, 1), -8.0 / HEADS, F32) * (head + 1).astype(F32))


def head_columns(j, d):
    pairs = HEADS // 4
    base = (j // pairs) * (3 * d // 2) + lax.rem(j, pairs) * 128
    return [pl.ds(pl.multiple_of(base + part * (d // 2), 128), 128) for part in range(3)]


def attend(qkv, rows, dist, pairs, prob, slot, o, d):
    zero = jnp.zeros((), BF)
    scores = []
    for j in pairs:
        cq, ck, _ = head_columns(j, d)
        q = qkv[rows, cq] * jnp.asarray(0.125, BF)
        k = qkv[rows, ck]
        scores.append([dot(k, jnp.where(lanes(half), q, zero), 1, 1) for half in range(2)])
    for at, j in enumerate(pairs):
        v = qkv[rows, head_columns(j, d)[2]]
        total = None
        for half in range(2):
            s = scores[at][half] - slope_of(2 * j + half) * dist
            e = jnp.exp(s - jnp.max(s, axis=0, keepdims=True))
            p = (e * (1.0 / jnp.sum(e, axis=0, keepdims=True))).astype(BF)
            prob[slot + 2 * at + half] = p
            part = dot(jnp.where(lanes(half), v, zero), p, 0, 0)
            total = part if total is None else total + part
        o[rows, pl.ds(pl.multiple_of(j * 128, 128), 128)] = total.T.astype(BF)


def fill_layout(lay, kinds, n):
    at = lax.broadcasted_iota(jnp.int32, (1, n), 1)
    slots = kinds.shape[0]
    segment, row, live = slots + at, at, jnp.zeros((1, n), jnp.int32)
    col = jnp.zeros((1, n), jnp.int32)
    start = jnp.int32(0)
    for slot in range(slots):
        kind = kinds[slot]
        side = jnp.where(kind == 0, SIDE_S, jnp.where(kind == 1, SIDE_M, SIDE_L))
        inverse = jnp.where(kind == 0, 1 / SIDE_S, jnp.where(kind == 1, 1 / SIDE_M, 1 / SIDE_L))
        end = start + side * side
        inside = (at >= start) & (at < end) & (end <= n)
        offset = at - start
        down = jnp.floor((offset.astype(F32) + 0.5) * inverse.astype(F32)).astype(jnp.int32)
        segment = jnp.where(inside, slot, segment)
        row = jnp.where(inside, down, row)
        col = jnp.where(inside, offset - down * side, col)
        live = jnp.where(inside, 1, live)
        start = end
    zero = jnp.zeros((4, n), F32)
    lay[...] = jnp.concatenate([v.astype(F32) for v in (segment, row, col, live)] + [zero], axis=0)


def forward_kernel(spread, *refs):
    (pat, dog, kinds, wq, wp, w1, w2) = refs[:7]
    vectors = refs[7:14]
    (x_o, dog_o, lay_o, wq_o, wp_o, w1_o, w2_o, vec_o, b1_o) = refs[14:23]
    (qkv_o, p_o, o_o, y1_o, c_o, g_o, gs_o, enc_o) = refs[23:31]
    (fq, fp, f1, f2, fs, gq, gp, g1) = refs[31:39]
    (lays, dist, xb, ac, qkv, prob, ob, y1, g, gs, smf, sm) = refs[39:51]
    (hs, hr, ss, rs, as_, ar, ls, ps) = refs[51:]
    place = Place(spread)
    d = xb.shape[2]
    n = xb.shape[1]
    ff = g.shape[1]
    smf[...] = jnp.zeros_like(smf)
    for at, ref in enumerate(vectors):
        both = ref[...].astype(F32)
        for m in range(2):
            smf[m, at : at + 1, 0 : both.shape[1]] = both[m : m + 1]
    for m in range(2):
        sm[m] = smf[m].astype(BF)
    place.greet()
    hand = ((sm, fs, None, 16), (wq, fq, gq, 24), (wp, fp, gp, 24), (w1, f1, g1, 24))
    hand += ((w2, f2, None, w2.shape[1]),)
    SM, QA, QB, PR, UA, UB, DA, DB = range(8)
    half = 3 * d // 2
    cut = (
        (0, fs),
        (1, fq.at[:, pl.ds(0, half)]),
        (1, fq.at[:, pl.ds(half, half)]),
        (2, fp),
        (3, f1.at[:, pl.ds(0, ff // 2)]),
        (3, f1.at[:, pl.ds(ff // 2, ff // 2)]),
        (4, f2.at[:, pl.ds(0, d // 2)]),
        (4, f2.at[:, pl.ds(d // 2, d // 2)]),
    )
    pieces = [
        Gather(place, view, 2 * hand[k][3], ss.at[i], rs.at[i]) for i, (k, view) in enumerate(cut)
    ]

    def spot_of(k):
        _, full, stage, rows = hand[k]

        def spot(far, piece):
            if stage is not None:
                return stage.at[far, place.c if piece is None else piece]
            at = place.p if piece is None else place.chip(far, 0, 0, 0) * 2 + piece
            return full.at[pl.ds(pl.multiple_of(at * rows, 16), rows)]

        return spot

    def hand_over(k, go):
        hand_in(place, hand[k][0], spot_of(k), hs.at[k], hr.at[k], go)

    def ready(k, far):
        hand_over(k, "far" if far else "near")
        _, full, stage, rows = hand[k]
        if stage is not None:
            start = pl.multiple_of(place.chip(far, 0, 0, 0) * (2 * rows), 2 * rows)

            def pack(src, dst):
                both = [stage[far, piece, :, src].astype(F32) for piece in range(2)]
                full[pl.ds(start, 2 * rows), dst] = jnp.concatenate(both, axis=0).astype(BF)

            if k == 1:
                for part in range(3):
                    for side in range(2):
                        pack(
                            pl.ds(part * d + side * (d // 2), d // 2),
                            pl.ds((side * 3 + part) * (d // 2), d // 2),
                        )
            else:
                pack(pl.ds(0, full.shape[1]), pl.ds(0, full.shape[1]))
        for i, (at, _) in enumerate(cut):
            if at == k:
                pieces[i].start(ZB if far else OWN)

    def pump(i, *kinds):
        for kind in kinds:
            pieces[i].arrived(kind)
            pieces[i].start(kind)

    def whole(i):
        for kind in range(8):
            pieces[i].arrived(kind, 1)

    saves = []

    def save(src, dst):
        copy = pltpu.make_async_copy(src, dst, ls.at[len(saves)])
        copy.start()
        saves.append(copy)
        return copy

    send_x = rcopy(pat.at[1 - place.m], xb.at[1], as_.at[0], ar.at[0], place.pair)
    send_dog = rcopy(dog.at[1 - place.m], dog_o, as_.at[1], ar.at[1], place.pair)
    send_lay = rcopy(lays.at[0], lays.at[1], as_.at[2], ar.at[2], place.pair)
    own_x = pltpu.make_async_copy(pat.at[place.m], xb.at[0], ps.at[0])
    own_x.start()
    FIRST = (X0, Y0)
    THEN = (X1, Y1)
    LAST = (D0, D1)

    def assemble():
        whole(SM)
        seg = d // RING
        hid = w2.shape[1]
        for q in range(RING):
            tile = fs[16 * q : 16 * q + 16].astype(F32)
            vec_o[0:8, seg * q : seg * q + seg] = tile[0:8, 0:seg]
            b1_o[0:1, hid * q : hid * q + hid] = tile[6:7, 0:hid]

    def first_norm(grp):
        def body(rows):
            nhat, _ = norm(xb[grp, rows, :].astype(F32))
            here = pl.ds(pl.multiple_of(grp * n + rows.start, 128), 128)
            ac[here, :] = (nhat * vec_o[0:1] + vec_o[1:2]).astype(BF)

        chunks(n, 128, body)

    def project(grp, side):
        cols = pl.ds(side * half, half)
        qkv[grp * n : grp * n + n, cols] = dot(ac[grp * n : grp * n + n], fq[:, cols], 1, 0).astype(BF)

    pairs = HEADS // 2

    def keep_prob(i):
        slots = pl.ds(i * STEP * 2, STEP * 2)
        return pltpu.make_async_copy(prob.at[slots], p_o.at[slots], ps.at[2 + i])

    def attention(start, stop, early):
        @pl.loop(start, stop)
        def _(i):
            grp, j = i // (pairs // STEP), lax.rem(i, pairs // STEP) * STEP
            rows = pl.ds(pl.multiple_of(grp * n, n), n)
            attend(qkv, rows, dist[grp], [j + k for k in range(STEP)], prob, 2 * STEP * i, ob, d)
            keep_prob(i).start()
            for at, steps in early.items():

                @pl.when(i == at)
                def _(steps=steps):
                    for step in steps:
                        if step[0] == "far":
                            ready(step[1], 1)
                        else:
                            pump(*step)

    def second_norm(rows):
        first = (
            xb[rows.start // n, pl.ds(pl.multiple_of(lax.rem(rows.start, n), 256), 256), :].astype(F32)
            + dot(ob[rows, :], fp[...], 1, 0)
            + vec_o[2:3]
        )
        y1[rows, :] = first
        nhat, _ = norm(first)
        ac[rows, :] = (nhat * vec_o[3:4] + vec_o[4:5]).astype(BF)

    def hidden(cols):
        u = dot(ac[...], f1[:, cols], 1, 0) + b1_o[0:1, cols]
        phi = 0.5 + 0.5 * lax.erf(u * 0.7071067811865476)
        g[:, cols] = (u * phi).astype(BF)
        gs[:, cols] = (phi + u * (0.3989422804014327 * jnp.exp(-0.5 * u * u))).astype(BF)

    def span(start, count, step, body):
        chunks(count, step, lambda s: body(pl.ds(pl.multiple_of(start + s.start, step), step)))

    def result(side):
        cols = pl.ds(side * (d // 2), d // 2)

        def body(rows):
            total = y1[rows, cols] + dot(g[rows, :], f2[:, cols], 1, 0) + vec_o[5:6, cols]
            qkv[rows, cols] = total.astype(BF)

        chunks(2 * n, 512, body)

    for k in range(5):
        hand_over(k, "start")
    fill_layout(lays.at[0], kinds, n)
    send_lay.start()
    send_x.start()
    fill_distance(dist.at[0], lays.at[0])
    for k in range(3):
        ready(k, 0)
    ready(0, 1)
    ready(1, 1)
    ready(3, 0)
    pump(SM, *FIRST)
    pump(QA, *FIRST)
    pump(QB, *FIRST)
    ready(4, 0)
    pump(SM, *THEN)
    pump(QA, *THEN)
    pump(QB, *THEN)
    ready(2, 1)
    pump(PR, *FIRST)
    pump(SM, *LAST)
    assemble()
    own_x.wait()
    first_norm(0)
    pump(QA, *LAST)
    pump(QB, *LAST)
    send_dog.start()
    whole(QA)
    project(0, 0)
    ready(3, 1)
    pump(UA, *FIRST)
    whole(QB)
    project(0, 1)
    pump(UB, *FIRST)
    pump(PR, *THEN)
    attention(0, 2, {0: [("far", 4), (UA, *THEN)], 1: [(UB, *THEN), (DA, *FIRST), (DB, *FIRST), (PR, *LAST)]})
    save(fq, wq_o)
    send_lay.wait_recv()
    fill_distance(dist.at[1], lays.at[1])
    send_x.wait_recv()
    first_norm(1)
    project(1, 0)
    project(1, 1)
    qkv_saved = save(qkv, qkv_o)
    save(xb.at[1], x_o)
    save(lays, lay_o)
    attention(2, 4, {2: [(DA, *THEN), (UA, *LAST)], 3: [(DB, *THEN), (UB, *LAST)]})
    save(ob, o_o)
    whole(PR)
    save(fp, wp_o)
    chunks(2 * n, 256, second_norm)
    save(y1, y1_o)
    save(ac, c_o)
    pump(DA, *LAST)
    whole(UA)
    span(0, ff // 2, 256, hidden)
    pump(DB, *LAST)
    whole(UB)
    save(f1, w1_o)
    span(ff // 2, ff // 2, 256, hidden)
    save(g, g_o)
    save(gs, gs_o)
    qkv_saved.wait()
    whole(DA)
    result(0)
    whole(DB)
    save(f2, w2_o)
    result(1)
    save(qkv.at[:, pl.ds(0, d)], enc_o)
    for k in range(5):
        hand_over(k, "send")
    for piece in pieces:
        piece.finish()
    send_x.wait_send()
    send_lay.wait_send()
    send_dog.wait()
    for i in range(2 * pairs // STEP):
        keep_prob(i).wait()
    for copy in saves:
        if copy is not qkv_saved:
            copy.wait()


def forward(spread, pat, dog, kinds, wq, wp, w1, w2, *vectors):
    any_, vm = pl.BlockSpec(memory_space=pl.ANY), pl.BlockSpec(memory_space=pltpu.VMEM)
    n, d = pat.shape[1:]
    ff = w2.shape[1] * RING
    sd = jax.ShapeDtypeStruct
    out = [
        sd((n, d), BF),
        sd((n, d), BF),
        sd((2, 8, n), F32),
        sd((d, wq.shape[2]), BF),
        sd((d, d), BF),
        sd((d, ff), BF),
        sd((ff, d), BF),
        sd((8, d), F32),
        sd((8, ff), F32),
        sd((2 * n, wq.shape[2]), BF),
        sd((2 * HEADS, n, n), BF),
        sd((2 * n, d), BF),
        sd((2 * n, d), F32),
        sd((2 * n, d), BF),
        sd((2 * n, ff), BF),
        sd((2 * n, ff), BF),
        sd((2 * n, d), BF),
    ]
    dma = pltpu.SemaphoreType.DMA
    vmem = pltpu.VMEM
    return pl.pallas_call(
        functools.partial(forward_kernel, spread),
        out_shape=out,
        in_specs=[any_] * 2 + [pl.BlockSpec(memory_space=pltpu.SMEM)] + [any_] * 4 + [vm] * 7,
        out_specs=[any_] * 7 + [vm] * 2 + [any_] * 8,
        scratch_shapes=[
            vmem((d, wq.shape[2]), BF),
            vmem((d, d), BF),
            vmem((d, ff), BF),
            vmem((ff, d), BF),
            vmem((RING * 16, 128), BF),
            vmem((2, 2, 24, wq.shape[2]), BF),
            vmem((2, 2, 24, d), BF),
            vmem((2, 2, 24, ff), BF),
            vmem((2, 8, n), F32),
            vmem((2, n, n), F32),
            vmem((2, n, d), BF),
            vmem((2 * n, d), BF),
            vmem((2 * n, wq.shape[2]), BF),
            vmem((2 * HEADS, n, n), BF),
            vmem((2 * n, d), BF),
            vmem((2 * n, d), F32),
            vmem((2 * n, ff), BF),
            vmem((2 * n, ff), BF),
            vmem((2, 16, 128), F32),
            vmem((2, 16, 128), BF),
            dma((5, 4)),
            dma((5, 4)),
            dma((8, 16)),
            dma((8, 16)),
            dma((3,)),
            dma((3,)),
            dma((16,)),
            dma((2 + HEADS,)),
        ],
        compiler_params=pltpu.CompilerParams(
            collective_id=0, has_side_effects=True, vmem_limit_bytes=62 * 2**20
        ),
        name="forward",
    )(pat, dog, kinds, wq, wp, w1, w2, *vectors)


class Scatter:
    def __init__(self, place, full, rows, got_sib, got, ssem, rsem):
        self.pl, self.full, self.rows = place, full, rows
        self.got_sib, self.got, self.ssem, self.rsem = got_sib, got, ssem, rsem

    def start_of(self, kind):
        fz, fy, fx = FLIPS[kind]
        return pl.multiple_of(self.pl.chip(fz, 0, fy, fx) * self.rows, self.rows)

    def plane(self, z, other):
        c = 1 - self.pl.c if other else self.pl.c
        return pl.ds(pl.multiple_of((z * 2 + c) * (4 * self.rows), self.rows), 4 * self.rows)

    def sib(self, z):
        return rcopy(
            self.full.at[self.plane(z, 1)],
            self.got_sib.at[z],
            self.ssem.at[z],
            self.rsem.at[z],
            self.pl.sib,
        )

    MOVES = {D0: ("y", 0), D1: ("x", 1), X0: ("x", 2), X1: ("x", 3), Y0: ("y", 4), Y1: ("y", 5)}

    def move(self, kind):
        way, slot = self.MOVES[kind]
        dev = {"x": self.pl.xn, "y": self.pl.yn}[way]
        return rcopy(
            self.full.at[pl.ds(self.start_of(kind), self.rows)],
            self.got.at[slot],
            self.ssem.at[2 + slot],
            self.rsem.at[2 + slot],
            dev,
        )

    def add(self, kind, slot):
        rows = pl.ds(self.start_of(kind), self.rows)
        self.full[rows, :] = self.full[rows, :] + self.got[slot]

    def begin(self):
        self.sib(0).start()
        self.sib(1).start()

    def second(self):
        for z in range(2):
            self.sib(z).wait()
        step = 16

        for z in range(2):
            base = (z * 2 + self.pl.c) * (4 * self.rows)

            @pl.loop(0, 4 * self.rows // step)
            def _(i, z=z, base=base):
                rows = pl.ds(pl.multiple_of(base + i * step, step), step)
                theirs = self.got_sib[z, pl.ds(pl.multiple_of(i * step, step), step), :]
                self.full[rows, :] = self.full[rows, :] + theirs

        for kind in (D0, D1, X1, Y0):
            self.move(kind).start()

    def third(self):
        self.move(D0).wait()
        self.add(X0, 0)
        self.move(X0).start()
        self.move(D1).wait()
        self.add(Y1, 1)
        self.move(Y1).start()

    def total(self, far):
        kind, slots = (ZB, (X1, Y1)) if far else (OWN, (X0, Y0))
        rows = pl.ds(self.start_of(kind), self.rows)
        total = self.full[rows, :].astype(F32)
        for move in slots:
            self.move(move).wait()
            total = total + self.got[self.MOVES[move][1]].astype(F32)
        return total.astype(BF)


def hand_back(place, stage, outs, ssem, rsem, go):
    def leg(far, k):
        z = 1 - place.z if far else place.z
        return rcopy(
            stage.at[far, k],
            outs[far].at[place.m],
            ssem.at[2 * far + k],
            rsem.at[2 * far + place.m],
            place.at(z=z, m=place.c, c=k),
        )

    def each(far, k, local, remote):
        if far:
            remote()
        else:
            here = jnp.logical_and(place.c == place.m, place.c == k)
            pl.when(here)(local)
            pl.when(jnp.logical_not(here))(remote)

    if go in ("near", "far"):
        far = int(go == "far")
        for k in range(2):

            def local(k=k):
                pltpu.make_async_copy(
                    stage.at[0, k], outs[0].at[place.m], rsem.at[place.m]
                ).start()

            each(far, k, local, lambda k=k: leg(far, k).start())
    elif go == "recv":
        for far in range(2):
            for m in range(2):
                dst = outs[far].at[m]
                rcopy(dst, dst, ssem.at[0], rsem.at[2 * far + m], place.sib).wait_recv()
    else:
        for far in range(2):
            for k in range(2):
                each(far, k, lambda: None, lambda far=far, k=k: leg(far, k).wait_send())


def unnorm(dn, nhat, r, gain):
    dh = dn * gain
    return r * (
        dh - jnp.mean(dh, axis=-1, keepdims=True) - nhat * jnp.mean(dh * nhat, axis=-1, keepdims=True)
    )


def attend_back(qkv, rows, probs, do, o, j, d):
    col = pl.multiple_of(j * 128, 128)
    eighth = jnp.asarray(0.125, BF)
    zero = jnp.zeros((), BF)
    cq, ck, cv = head_columns(j, d)
    q, k, v = qkv[rows, cq], qkv[rows, ck], qkv[rows, cv]
    g = do[rows, pl.ds(col, 128)]
    both = g.astype(F32) * o[rows, pl.ds(col, 128)].astype(F32)
    dq = dk = dv = 0.0
    for half in range(2):
        keep = lanes(half)
        p = probs[half]
        gm = jnp.where(keep, g, zero)
        centre = jnp.sum(jnp.where(keep, both, 0.0), axis=1, keepdims=True)
        centre = jnp.broadcast_to(centre, (both.shape[0], 128)).T[0:1]
        ds = (p.astype(F32) * (dot(v, gm, 1, 1) - centre)).astype(BF)
        dk = dk + dot(ds, jnp.where(keep, q * eighth, zero), 1, 0)
        dv = dv + dot(p, gm, 1, 0)
        dq = dq + dot(jnp.where(keep, k * eighth, zero), ds, 0, 0)
    qkv[rows, cq] = dq.T.astype(BF)
    qkv[rows, ck] = dk.astype(BF)
    qkv[rows, cv] = dv.astype(BF)


def backward_kernel(spread, *refs):
    (pat, dog, x_i, dog_i, lay_i, wq_i, wp_i, w1_i, w2_i, vec) = refs[:10]
    (qkv_i, p_i, o_i, y1_i, c_i, g_i, gs_i, y_i) = refs[10:18]
    outs = (refs[18:22], refs[22:26])
    (os_, enc_o, pg_o) = refs[26:29]
    (w2, w1, wp, qkv, g, du, c, ob, dz, y1, do, g2, gp, lays, sums) = refs[29:44]
    got_sib, got, stages = refs[44:51], refs[51:58], refs[58:62]
    (sgot, ss, rs, hs, hr, es, er, ts, tr, ls, ps) = refs[62:]
    place = Place(spread)
    n, d = c.shape[0] // 2, c.shape[1]
    ff = w1.shape[1]
    wide = qkv.shape[1]
    loads = []

    def load(src, dst):
        copy = pltpu.make_async_copy(src, dst, ls.at[len(loads)])
        copy.start()
        loads.append(copy)
        return copy

    lay_l = (load(lay_i, lays),)
    dz_l = (
        load(dog.at[place.m], dz.at[pl.ds(0, n)]),
        load(dog_i, dz.at[pl.ds(n, n)]),
    )
    g_l = load(g_i, g)
    w2_l = load(w2_i, w2)
    du_l = load(gs_i, du)
    c_l = load(c_i, c)
    w1_l = load(w1_i, w1)
    y1_l = load(y1_i, y1)
    o_l = load(o_i, ob)
    wp_l = load(wp_i, wp)
    qkv_l = load(qkv_i, qkv)
    place.greet()
    acts = [
        rcopy(y_i.at[pl.ds(n, n)], enc_o.at[place.m], es.at[0], er.at[0], place.pair),
        rcopy(c.at[pl.ds(n, n)], pg_o.at[place.m], es.at[1], er.at[1], place.pair),
    ]
    enc_l = load(y_i.at[pl.ds(0, n)], enc_o.at[place.m])
    acts[0].start()
    gq = du.at[pl.ds(0, d), pl.ds(0, wide)]
    g1 = g.at[pl.ds(0, d)]
    DA, DB, UA, UB, PR, QA, QB = range(7)
    cut = (
        (3, 0, d // 2),
        (3, d // 2, d // 2),
        (2, 0, ff // 2),
        (2, ff // 2, ff // 2),
        (1, 0, d),
        (0, 0, wide // 2),
        (0, wide // 2, wide // 2),
    )
    fulls = (gq, gp, g1, g2)
    sc = [
        Scatter(
            place,
            fulls[w].at[:, pl.ds(at, size)],
            fulls[w].shape[0] // 16,
            got_sib[k],
            got[k],
            ss.at[k],
            rs.at[k],
        )
        for k, (w, at, size) in enumerate(cut)
    ]

    def back(k, go):
        w, at, size = cut[k]
        cols = pl.ds(at, size)
        into = [outs[far][w].at[:, :, cols] for far in range(2)]
        hand_back(place, stages[w].at[:, :, :, cols], into, hs.at[k], hr.at[k], go)

    def close(k, far):
        w, at, size = cut[k]
        total = sc[k].total(far)
        half = total.shape[0] // 2
        stages[w][far, 0, :, at : at + size] = total[:half]
        stages[w][far, 1, :, at : at + size] = total[half:]
        back(k, "far" if far else "near")

    def do_steps(steps):
        for what, k in steps:
            if what in "fc":
                close(k, int(what == "f"))
            else:
                getattr(sc[k], {"b": "begin", "s": "second", "t": "third"}[what])()

    sums[...] = jnp.zeros_like(sums)

    def add_sum(row, v):
        sums[row : row + 1] += jnp.sum(v, axis=0, keepdims=True)

    def span(start, count, step, body):
        chunks(count, step, lambda s: body(pl.ds(pl.multiple_of(start + s.start, step), step)))

    for copy in (*lay_l, *dz_l):
        copy.wait()
    for grp in range(2):
        live = lays[grp].T[:, 3:4]
        for part in range(4):
            rows = pl.ds(grp * n + part * (n // 4), n // 4)
            keep = live[part * (n // 4) : (part + 1) * (n // 4)]
            v = dz[rows, :].astype(F32) * keep
            dz[rows, :] = v.astype(BF)
            add_sum(5, v)
    g_l.wait()

    def down_grad(at, size):
        def body(rows):
            g2[rows, pl.ds(at, size)] = dot(g[:, rows], dz[:, pl.ds(at, size)], 0, 0).astype(BF)

        chunks(ff, 768, body)

    def hidden(cols):
        v = dot(dz[...], w2[cols, :], 1, 1) * du[:, cols].astype(F32)
        r = v.astype(BF)
        du[:, cols] = r
        line = jnp.sum(r.astype(F32), axis=0, keepdims=True)
        sums[pl.ds(6 + cols.start // d, 1), pl.ds(pl.multiple_of(lax.rem(cols.start, d), 128), 256)] = line

    pairs = HEADS // 2

    def turn(i):
        return 1 - i // pairs, lax.rem(i, pairs)

    def fetch(i):
        grp, j = turn(i)
        src = (grp * pairs + j) * 2
        slot = lax.rem(i, 3)
        for half in range(2):
            yield pltpu.make_async_copy(
                p_i.at[src + half],
                w2.at[pl.ds(pl.multiple_of((slot * 2 + half) * n, n), n), pl.ds(0, n)],
                ps.at[slot, half],
            )

    def up_grad(cols):
        g1[:, cols] = dot(c[...], du[:, cols], 0, 0).astype(BF)

    def second_norm(rows):
        dc = dot(du[rows, :], w1[...], 1, 1)
        nhat, r = norm(y1[rows, :])
        add_sum(3, dc * nhat)
        add_sum(4, dc)
        first = dz[rows, :].astype(F32) + unnorm(dc, nhat, r, vec[3:4])
        y1[rows, :] = first
        low = first.astype(BF)
        c[rows, :] = low
        add_sum(2, low.astype(F32))

    def first_norm(rows):
        nhat, _ = norm(c[rows, :].astype(F32))
        dz[rows, :] = (nhat * vec[0:1] + vec[1:2]).astype(BF)

    def attention(start, stop, work):
        @pl.loop(start, stop)
        def _(i):
            grp, j = turn(i)
            rows = pl.ds(pl.multiple_of(grp * n, n), n)
            for copy in fetch(i):
                copy.wait()
            slot = lax.rem(i, 3)
            probs = [
                w2.at[pl.ds(pl.multiple_of((slot * 2 + half) * n, n), n), pl.ds(0, n)]
                for half in range(2)
            ]
            attend_back(qkv, rows, [p[...] for p in probs], do, ob, j, d)

            @pl.when(i + 3 < 2 * pairs)
            def _():
                for copy in fetch(i + 3):
                    copy.start()

            for at, steps in work.items():

                @pl.when(i == at)
                def _(steps=steps):
                    do_steps(steps)

    def input_grad(rows):
        da = dot(qkv[rows, :], w1[:, pl.ds(0, wide)], 1, 1)
        nhat, r = norm(c[rows, :].astype(F32))
        add_sum(0, da * nhat)
        add_sum(1, da)
        c[rows, :] = (y1[rows, :] + unnorm(da, nhat, r, vec[0:1])).astype(BF)

    def qkv_grad(k):
        cols = pl.ds(cut[k][1], cut[k][2])
        gq[:, cols] = dot(dz[...], qkv[:, cols], 0, 0).astype(BF)

    around = (place.sib, place.xn, place.yn, place.at(x=1 - place.x, y=1 - place.y))
    beyond = (
        (place.zn, 1),
        (place.pair, 0),
        (place.at(z=1 - place.z, m=1 - place.m), 1),
    )

    def hop(i):
        return rcopy(sums, sgot.at[0], ts.at[0], tr.at[0], around[0]) if i == 0 else rcopy(
            sgot.at[4], sgot.at[i], ts.at[i], tr.at[i], around[i]
        )

    def leap(i):
        dev, far = beyond[i]
        return rcopy(os_.at[0, place.m], os_.at[far, place.m], ts.at[4 + i], tr.at[4 + i], dev)

    def small(step):
        if step == 0:
            hop(0).start()
        elif step == 1:
            hop(0).wait()
            sgot[4] = sums[...] + sgot[0]
            for i in range(1, 4):
                hop(i).start()
        elif step == 2:
            for i in range(1, 4):
                hop(i).wait()
            os_[0, place.m] = (sgot[4] + sgot[1]) + (sgot[2] + sgot[3])
            for i in range(3):
                leap(i).start()
        else:
            for i, (far, m) in enumerate(((1, place.m), (0, 1 - place.m), (1, 1 - place.m))):
                leap(i).wait_send()
                view = os_.at[far, m]
                rcopy(view, view, ts.at[4 + i], tr.at[4 + i], place.zn).wait_recv()

    down_grad(0, d // 2)
    do_steps([("b", DA)])
    down_grad(d // 2, d // 2)
    do_steps([("b", DB), ("s", DA)])
    w2_l.wait()
    du_l.wait()
    chunks(ff, 256, hidden)
    do_steps([("t", DA), ("s", DB)])
    for i in range(3):
        for copy in fetch(i):
            copy.start()
    c_l.wait()
    span(0, ff // 2, 768, up_grad)
    do_steps([("b", UA)])
    span(ff // 2, ff // 2, 768, up_grad)
    do_steps([("b", UB), ("f", DA), ("t", DB), ("s", UA)])
    w1_l.wait()
    y1_l.wait()
    chunks(2 * n, 256, second_norm)
    do_steps([("f", DB), ("t", UA), ("s", UB)])
    wq_l = load(wq_i, w1.at[:, pl.ds(0, wide)])
    o_l.wait()
    wp_l.wait()
    gp[...] = dot(ob[...], c[...], 0, 0).astype(BF)
    do_steps([("b", PR)])
    do[...] = dot(c[...], wp[...], 1, 1).astype(BF)
    x_l = (load(pat.at[place.m], c.at[pl.ds(0, n)]), load(x_i, c.at[pl.ds(n, n)]))
    for copy in x_l:
        copy.wait()
    chunks(2 * n, 256, first_norm)
    qkv_l.wait()
    attention(0, 6, {1: [("s", PR)], 3: [("c", DA), ("f", UA), ("t", UB)]})
    wq_l.wait()
    span(n, n, 256, input_grad)
    acts[1].start()
    do_steps([("t", PR)])
    do_steps([("c", DB)])
    do_steps([("f", UB)])
    attention(6, 9, {7: [("c", UA), ("f", PR)], 8: [("c", UB), ("c", PR)]})
    qkv_grad(QA)
    do_steps([("b", QA)])
    attention(9, 12, {9: [("s", QA)], 11: [("t", QA)]})
    qkv_grad(QB)
    do_steps([("b", QB)])
    span(0, n, 256, input_grad)
    pg_l = load(c.at[pl.ds(0, n)], pg_o.at[place.m])
    small(0)
    do_steps([("s", QB)])
    do_steps([("f", QA)])
    do_steps([("c", QA)])
    small(1)
    do_steps([("t", QB)])
    small(2)
    do_steps([("f", QB)])
    do_steps([("c", QB)])
    for k in range(7):
        back(k, "recv")
        back(k, "send")
    small(3)
    for act in acts:
        act.wait()
    enc_l.wait()
    pg_l.wait()


def backward(spread, pat, dog, *kept):
    any_, vm = pl.BlockSpec(memory_space=pl.ANY), pl.BlockSpec(memory_space=pltpu.VMEM)
    n, d = pat.shape[1:]
    wide, ff = kept[3].shape[1], kept[5].shape[1]
    lay = kept[2]
    shapes = ((48, wide), (48, d), (48, ff), (ff // 16, d))
    cuts = 2 * ((ff // 16, d // 2),) + 2 * ((48, ff // 2),) + ((48, d),) + 2 * ((48, wide // 2),)
    sd = jax.ShapeDtypeStruct
    out = 2 * [sd((2, r // 2, k), BF) for r, k in shapes]
    out += [sd((2, 2, 16, d), F32), sd((2, n, d), BF), sd((2, n, d), BF)]
    dma = pltpu.SemaphoreType.DMA
    vmem = pltpu.VMEM
    return pl.pallas_call(
        functools.partial(backward_kernel, spread),
        out_shape=out,
        in_specs=[any_] * 9 + [vm] + [any_] * 8,
        out_specs=[any_] * 8 + [vm] + [any_] * 2,
        scratch_shapes=[
            vmem((ff, d), BF),
            vmem((d, ff), BF),
            vmem((d, d), BF),
            vmem((2 * n, wide), BF),
            vmem((2 * n, ff), BF),
            vmem((2 * n, ff), BF),
            vmem((2 * n, d), BF),
            vmem((2 * n, d), BF),
            vmem((2 * n, d), BF),
            vmem((2 * n, d), F32),
            vmem((2 * n, d), BF),
            vmem((ff, d), BF),
            vmem((d, d), BF),
            vmem(lay.shape, F32),
            vmem((16, d), F32),
        ]
        + [vmem((2, 4 * r, k), BF) for r, k in cuts]
        + [vmem((6, r, k), BF) for r, k in cuts]
        + [vmem((2, 2, r // 2, k), BF) for r, k in shapes]
        + [
            vmem((5, 16, d), F32),
            dma((7, 9)),
            dma((7, 9)),
            dma((7, 4)),
            dma((7, 4)),
            dma((2,)),
            dma((2,)),
            dma((7,)),
            dma((7,)),
            dma((18,)),
            dma((3, 2)),
        ],
        compiler_params=pltpu.CompilerParams(
            collective_id=1, has_side_effects=True, vmem_limit_bytes=62 * 2**20
        ),
        name="backward",
    )(pat, dog, *kept)


def finish_kernel(*refs):
    (pg, enc), near, far = refs[:2], refs[2:6], refs[6:10]
    (pg_o, enc_o), outs = refs[10:12], refs[12:16]
    pg_o[...] = pg[...].astype(F32)
    enc_o[...] = enc[...]

    @pl.when(pl.program_id(0) == 0)
    def _():
        for k, out in enumerate(outs):
            for m in range(2):
                total = near[k][m].astype(F32) + far[k][m].astype(F32)
                if k == 0:
                    width = total.shape[1] // 6
                    for at in range(6):
                        part, side = at // 2, at % 2
                        src = (side * 3 + part) * width
                        out[m, :, at * width : (at + 1) * width] = total[:, src : src + width]
                else:
                    out[m] = total


def finish(pg, enc, parts):
    n, d = pg.shape[1:]
    steps = 4
    tile = pl.BlockSpec((2, n // steps, d), lambda i: (0, i, 0))
    whole = [pl.BlockSpec(v.shape, lambda i: (0, 0, 0)) for v in parts]
    sd = jax.ShapeDtypeStruct
    return pl.pallas_call(
        finish_kernel,
        grid=(steps,),
        out_shape=[sd(pg.shape, F32), sd(enc.shape, BF)] + [sd(v.shape, F32) for v in parts[:4]],
        in_specs=[tile, tile] + whole,
        out_specs=[tile, tile] + whole[:4],
        compiler_params=pltpu.CompilerParams(vmem_limit_bytes=62 * 2**20),
        name="finish",
    )(pg, enc, *parts)


def local(
    count, patches, tile_kind, out_grad, n1g, n1b, wq, wp, bp, n2g, n2b, w1, b1, w2, b2
):
    spread = count // RING
    idx = lax.axis_index("fsdp")
    p = idx // spread
    rows, d = patches.shape[1:]
    parts = (n1g, n1b, bp, n2g, n2b, b2)
    if spread > 1:
        groups = [[q * spread + j for j in range(spread)] for q in range(RING)]
        ag = functools.partial(
            lax.all_gather, axis_name="fsdp", axis=1, tiled=True, axis_index_groups=groups
        )
        wq, wp, w1, w2, b1 = ag(wq), ag(wp), ag(w1), ag(w2), ag(b1)
        parts = tuple(ag(v) for v in parts)
    pat2, dog2, lay2, fq, fp, f1, f2, vecs, _, *saved = forward(
        spread, patches, out_grad, tile_kind, wq, wp, w1, w2, *parts, b1
    )
    *shares, os_, encoded, pgrad = backward(
        spread, patches, out_grad, pat2, dog2, lay2, fq, fp, f1, f2, vecs, *saved
    )
    pgrad, encoded, *grads = finish(pgrad, encoded, shares)
    os_ = os_[0] + os_[1]
    seg = d // RING
    vec = lax.dynamic_slice_in_dim(os_[:, :6], p * seg, seg, axis=2)
    hid = os_[:, 6 : 6 + w2.shape[1] * RING // d].reshape(2, -1)
    hid = lax.dynamic_slice_in_dim(hid, p * w2.shape[1], w2.shape[1], axis=1)
    if spread > 1:
        rs = functools.partial(
            lax.psum_scatter, axis_name="fsdp", tiled=True, axis_index_groups=groups
        )
        grads = [rs(v, scatter_dimension=1) for v in grads]
        vec, hid = rs(vec, scatter_dimension=2), rs(hid, scatter_dimension=1)
    return (
        encoded,
        pgrad,
        vec[:, 0],
        vec[:, 1],
        grads[0],
        grads[1],
        vec[:, 2],
        vec[:, 3],
        vec[:, 4],
        grads[2],
        hid,
        grads[3],
        vec[:, 5],
    )


def solution(mesh):
    three, two = P(None, "fsdp", None), P(None, "fsdp")
    in_specs = (three, P("fsdp"), three, two, two, three, three, two, two, two, three, two, three, two)
    out_specs = (three, three, two, two, three, three, two, two, two, three, two, three, two)
    return jax.shard_map(
        functools.partial(local, mesh.shape["fsdp"]),
        mesh=mesh,
        in_specs=in_specs,
        out_specs=out_specs,
        check_vma=False,
    )
```
